32 devices in a mesh: job: 2 (over x), gddi: 4 (over y, core), intra: 4 (over z).
Axes of the slice: x: 2, y: 2, z: 4, core: 2. Of those that a mesh axis runs over, the one named last changes fastest.
Arguments:
- density: bfloat16 [64, 256, 256], P(('job', 'gddi', 'intra')), parts along dimension 0, as said below
- h_core: bfloat16 [64, 256, 256], P(('job', 'gddi', 'intra')), parts along dimension 0, may hold values from -6 to 6
- esp_block: bfloat16 [64, 8, 256, 256], P(('job', 'gddi'), 'intra'), parts along dimension 0, may hold values from -0.1875 to 0.1875
- nbr: int32 [64, 8], P('job'), parts along dimension 0, may hold values from 0 to 31, as said below
Outputs:
- fock: float32 [64, 256, 256], P(('job', 'gddi', 'intra')), parts along dimension 0
The draws below stay inside these ranges and needn't reach their ends.
There are 2 independent parts, one for each index of `job`. The reference program is written for one: setup_inputs(seed, part) draws one part's arguments, and reference() takes and returns one part's arrays. A program takes and returns all parts, laid end to end along the dimension named above; each array names one. Nothing has to cross between parts.
Inputs may be any that keep to these rules, and one draw needn't show every extreme that they name: nbr[I, c] is never I. Group g holds fragments g * 8 to (g + 1) * 8 - 1. For a group h and d of 0 to 3, take the 16 pairs of fragments of group h with slots d * 2 to (d + 1) * 2 - 1: at most 8 of them name fragments of any one group, and they name at most 4 distinct fragments of any one group; both bounds are reached for every such set of pairs. `density`: symmetric.
All inputs are finite; a program needn't handle non-finite values.
Results may differ from the reference program's by a relative error of at most 0.0003.
Values may be sent and summed in bfloat16 or wider, within the bound.
No kernel may reach another device: no remote copies, remote signals or barrier semaphores. Data moves between devices by JAX's collectives and lax.ppermute only.
A program may use at most 128 MiB of HBM per device.

```python
import jax
import jax.numpy as jnp
from jax import lax

NB = 256
SLOT_DEV = 2
GROUPS = 4
LANES = 4
MONO_GRP = 8
MONO = 32
NBR = 8
PAIRS = 16
CAP = 4


def draw_density(key, part):
    key = jax.random.fold_in(key, 5)
    key_one = jax.random.fold_in(key, 0)
    raw_values = jax.random.normal(key_one, (MONO, NB, NB), jnp.float32)
    symmetric = (raw_values + jnp.swapaxes(raw_values, 1, 2)) * 0.7071
    return symmetric.astype(jnp.bfloat16)


def draw_nbr(key, part):
    key = jax.random.fold_in(key, 11)
    key_rot, key_perm, key_cand = jax.random.split(key, 3)
    base_count = PAIRS // GROUPS
    rotation = jax.random.randint(key_rot, (GROUPS, LANES), 0, GROUPS)
    perm_keys = jax.random.split(key_perm, GROUPS * LANES)
    perms = jax.vmap(lambda one_key: jax.random.permutation(one_key, PAIRS))(perm_keys).reshape(GROUPS, LANES, PAIRS)
    cand_keys = jax.random.split(key_cand, GROUPS * LANES * GROUPS)
    cands = jax.vmap(lambda one_key: jax.random.permutation(one_key, MONO_GRP)[:CAP])(cand_keys).reshape(GROUPS, LANES, GROUPS, CAP)
    offset = jnp.maximum(perms // base_count - 1, 0)
    home = jnp.arange(GROUPS, dtype=jnp.int32)[:, None, None]
    source = (home + offset + rotation[:, :, None]) % GROUPS
    pair_rank = jnp.where(perms < 2 * base_count, perms, perms % base_count)
    pick = pair_rank % CAP
    source_index = jnp.broadcast_to(source[:, :, :, None], (GROUPS, LANES, PAIRS, CAP))
    cand_rows = jnp.take_along_axis(cands, source_index, axis=2)
    member = jnp.take_along_axis(cand_rows, pick[:, :, :, None], axis=3)[:, :, :, 0]
    backup = jnp.take_along_axis(cand_rows, ((pick + 1) % CAP)[:, :, :, None], axis=3)[:, :, :, 0]
    position = jnp.arange(PAIRS, dtype=jnp.int32)[None, None, :]
    self_id = home * MONO_GRP + position // SLOT_DEV
    ident = source * MONO_GRP + member
    ident = jnp.where(ident == self_id, source * MONO_GRP + backup, ident)
    ident = ident.reshape(GROUPS, LANES, MONO_GRP, SLOT_DEV).transpose(0, 2, 1, 3)
    return ident.reshape(MONO, NBR).astype(jnp.int32)


def levels(own_key, shape, shards, least, top_value):
    factor_of = 1.0
    for dim, shards_of in shards:
        steps = jax.random.uniform(jax.random.fold_in(jax.random.fold_in(own_key, 6), dim), (shards_of,), jnp.float32, least / len(shards), top_value / len(shards))
        factor_of = factor_of * jnp.repeat(jnp.exp(steps), shape[dim] // shards_of).reshape((-1,) + (1,) * (len(shape) - 1 - dim))
    return factor_of


def scatter_about(own_key, shape, scale, most, cuts=(), held_as=jnp.bfloat16):
    array = jax.random.normal(own_key, shape, jnp.float32) * scale
    if len(cuts) > 0:
        array = levels(own_key, shape, cuts, -0.22, 0.18) * array
    return jnp.clip(array, min=-most, max=most).astype(held_as)


def setup_inputs(seed: int = 0, part: int = 0) -> dict:
    key_of = jax.random.split(jax.random.key(seed), 5)
    part_keys = jax.random.split(jax.random.fold_in(key_of[4], part), 5)
    density = draw_density(jax.random.fold_in(jax.random.fold_in(key_of[4], part), 71), part)
    h_core = scatter_about(part_keys[1], (MONO, NB, NB), 1.0, 6.0, ((0, 16),))
    esp_block = scatter_about(part_keys[2], (MONO, NBR, NB, NB), (4 * NB) ** -0.5, 0.1875, ((0, 4), (1, 4)))
    nbr = draw_nbr(jax.random.fold_in(jax.random.fold_in(key_of[4], part), 71), part)
    return dict(density=density, h_core=h_core, esp_block=esp_block, nbr=nbr)


def reference(density, h_core, esp_block, nbr):
    def monomer_fock(inputs_one):
        blocks, near_ids, core_block = inputs_one
        nearby = density[near_ids.astype(jnp.int32)]
        half_term = jnp.einsum("cab,cbd->cad", blocks, nearby, preferred_element_type=jnp.float32)
        blocks_wide = blocks.astype(jnp.float32)
        field_term = jnp.einsum("cab,cdb->cad", half_term, blocks_wide, precision=lax.Precision.HIGHEST)
        return core_block.astype(jnp.float32) + jnp.sum(field_term, axis=0)

    return lax.map(monomer_fock, (esp_block, nbr, h_core))
```

```python
import functools

import jax
import jax.numpy as jnp
from jax import lax
from jax.experimental import pallas as pl
from jax.experimental.pallas import tpu as pltpu
from jax.sharding import PartitionSpec as P


def xor_pairs(size, k):
    return [(i, i ^ k) for i in range(size)]


def transposed_dot(a, b):
    return lax.dot_general(a, b, (((1,), (1,)), ((), ())), preferred_element_type=jnp.float32)


def fold(f):
    half = f.shape[0] // 2
    first, off, second = f[:half, :half], f[:half, half:], f[half:, half:]
    row = lax.broadcasted_iota(jnp.int32, (half, half), 0)
    col = lax.broadcasted_iota(jnp.int32, (half, half), 1)
    mixed = jnp.where(row <= col, first, second)
    diag = jnp.sum(jnp.where(row == col, second, 0.0), axis=0, keepdims=True)
    return off, mixed, jnp.broadcast_to(diag, (8, half))


def unfold(off, mixed, diag):
    half = off.shape[0]
    row = lax.broadcasted_iota(jnp.int32, (half, half), 0)
    col = lax.broadcasted_iota(jnp.int32, (half, half), 1)
    turned = mixed.T
    first = jnp.where(row <= col, mixed, turned)
    second = jnp.where(row > col, mixed, jnp.where(row < col, turned, diag))
    return first, off, off.T, second


def couple_kernel(groups, lanes, mono_dev, slot_dev, nbr_ref, esp_ref, *refs):
    n_pieces = groups * lanes
    pieces = refs[:n_pieces]
    outs = refs[n_pieces : n_pieces + lanes]
    esp, dens, esp_sem, dens_sem = refs[n_pieces + lanes :]
    my_group = lax.axis_index("gddi")
    my_lane = lax.axis_index("intra")
    mono_grp = mono_dev * lanes
    half = outs[0].shape[2]
    esp_copy = pltpu.make_async_copy(esp_ref, esp, esp_sem)
    esp_copy.start()
    copies = []
    for i, piece in enumerate(pieces):
        copy = pltpu.make_async_copy(piece, dens.at[pl.ds(i * mono_dev, mono_dev)], dens_sem.at[i])
        copy.start()
        copies.append(copy)
    esp_copy.wait()
    for copy in copies:
        copy.wait()

    def slot_of(fragment):
        apart = (fragment // mono_grp) ^ my_group
        lane = ((fragment % mono_grp) // mono_dev) ^ my_lane
        place = (apart & 1) * (groups // 2) + (apart >> 1)
        return (place * lanes + lane) * mono_dev + fragment % mono_dev

    for k in range(lanes):
        for m in range(mono_dev):
            mine = (my_lane ^ k) * mono_dev + m
            total = None
            for s in range(slot_dev):
                name = nbr_ref[my_group * mono_grp + mine, my_lane * slot_dev + s]
                block = esp[mine, s]
                half_term = jnp.dot(block, dens[slot_of(name)], preferred_element_type=jnp.float32)
                high = half_term.astype(jnp.bfloat16)
                low = (half_term - high.astype(jnp.float32)).astype(jnp.bfloat16)
                term = transposed_dot(high, block) + transposed_dot(low, block)
                total = term if total is None else total + term
            off, mixed, diag = fold(total)
            outs[k][m, :half] = off
            outs[k][m, half : 2 * half] = mixed
            outs[k][m, 2 * half :] = diag


def finish_kernel(core_ref, *refs):
    parts, out_ref = refs[:-1], refs[-1]
    half = out_ref.shape[1] // 2
    for m in range(out_ref.shape[0]):
        total = parts[0][m]
        for part in parts[1:]:
            total = total + part[m]
        first, off, off_t, second = unfold(total[:half], total[half : 2 * half], total[2 * half : 2 * half + 1])
        core = core_ref[m].astype(jnp.float32)
        out_ref[m, :half, :half] = core[:half, :half] + first
        out_ref[m, :half, half:] = core[:half, half:] + off
        out_ref[m, half:, :half] = core[half:, :half] + off_t
        out_ref[m, half:, half:] = core[half:, half:] + second


def local(density, h_core, esp_block, nbr):
    groups = lax.axis_size("gddi")
    lanes = lax.axis_size("intra")
    mono_dev, basis = density.shape[0], density.shape[1]
    mono_grp, slot_dev = esp_block.shape[0], esp_block.shape[1]
    half = basis // 2

    row = [density if k == 0 else lax.ppermute(density, "intra", xor_pairs(lanes, k)) for k in range(lanes)]
    near = []
    for k in range(groups // 2):
        for piece in row:
            near.append(piece if k == 0 else lax.ppermute(piece, "gddi", xor_pairs(groups, 2 * k)))
    pieces = near + [lax.ppermute(piece, "gddi", xor_pairs(groups, 1)) for piece in near]

    folded = jax.ShapeDtypeStruct((mono_dev, basis + 8, half), jnp.float32)
    any_space = pl.BlockSpec(memory_space=pl.ANY)
    in_vmem = pl.BlockSpec(memory_space=pltpu.VMEM)
    partials = pl.pallas_call(
        functools.partial(couple_kernel, groups, lanes, mono_dev, slot_dev),
        out_shape=[folded] * lanes,
        in_specs=[pl.BlockSpec(memory_space=pltpu.SMEM)] + [any_space] * (1 + len(pieces)),
        out_specs=[in_vmem] * lanes,
        scratch_shapes=[
            pltpu.VMEM(esp_block.shape, esp_block.dtype),
            pltpu.VMEM((mono_dev * len(pieces), basis, basis), density.dtype),
            pltpu.SemaphoreType.DMA,
            pltpu.SemaphoreType.DMA((len(pieces),)),
        ],
        compiler_params=pltpu.CompilerParams(vmem_limit_bytes=56 * 2**20),
        name="couple",
    )(nbr, esp_block, *pieces)

    terms = [partials[0]] + [lax.ppermute(partials[k], "intra", xor_pairs(lanes, k)) for k in range(1, lanes)]
    return pl.pallas_call(
        finish_kernel,
        out_shape=jax.ShapeDtypeStruct((mono_dev, basis, basis), jnp.float32),
        in_specs=[in_vmem] * (1 + lanes),
        out_specs=in_vmem,
        name="finish",
    )(h_core, *terms)


def solution(mesh):
    return jax.shard_map(
        local,
        mesh=mesh,
        in_specs=(
            P(("job", "gddi", "intra"), None, None),
            P(("job", "gddi", "intra"), None, None),
            P(("job", "gddi"), "intra", None, None),
            P("job", None),
        ),
        out_specs=P(("job", "gddi", "intra"), None, None),
        check_vma=False,
    )
```

```python
import functools

import jax
import jax.numpy as jnp
from jax import lax
from jax.experimental import pallas as pl
from jax.experimental.pallas import tpu as pltpu
from jax.sharding import PartitionSpec as P

STEPS = 32.0
TOP = 32000.0
SHRINK = 1.0 / 16.0
IN_VMEM = pl.BlockSpec(memory_space=pltpu.VMEM)
IN_SMEM = pl.BlockSpec(memory_space=pltpu.SMEM)


def xor_pairs(size, k):
    return [(i, i ^ k) for i in range(size)]


def round_up(n, to):
    return -(-n // to) * to


def transposed_dot(a, b):
    return lax.dot_general(a, b, (((1,), (1,)), ((), ())), preferred_element_type=jnp.float32)


def square_iotas(half):
    row = lax.broadcasted_iota(jnp.int32, (half, half), 0)
    col = lax.broadcasted_iota(jnp.int32, (half, half), 1)
    return row, col


def fold(first, second):
    row, col = square_iotas(first.shape[0])
    mixed = jnp.where(row <= col, first, second)
    diag = jnp.sum(jnp.where(row == col, second, 0.0), axis=0, keepdims=True)
    return mixed, diag


def unfold(mixed, diag):
    row, col = square_iotas(mixed.shape[0])
    turned = mixed.T
    first = jnp.where(row <= col, mixed, turned)
    second = jnp.where(row > col, mixed, jnp.where(row < col, turned, diag))
    return first, second


def scale_code(peak):
    wanted = jnp.log(jnp.maximum(peak * SHRINK, 2.0**-120)) * STEPS
    return jnp.floor(wanted + 1.5).astype(jnp.int32)


def encode(x, code):
    units = jnp.exp(code.astype(jnp.float32) * (-1.0 / STEPS)) * TOP
    return jnp.floor(x * SHRINK * units + 0.5).astype(jnp.int32)


def decode(q, code):
    units = jnp.exp(code.astype(jnp.float32) * (1.0 / STEPS)) * (1.0 / TOP)
    return q.astype(jnp.float32) * units * (1.0 / SHRINK)


def pack(high, low):
    return lax.shift_left(high, 16) | (low & 0xFFFF)


def unpack(word):
    return lax.shift_right_arithmetic(word, 16), lax.shift_right_arithmetic(lax.shift_left(word, 16), 16)


def peak_of(x):
    return jnp.max(jnp.abs(x), axis=0, keepdims=True)


def fold_kernel(dens_ref, out_ref):
    mono_dev, basis, _ = dens_ref.shape
    half = basis // 2
    diags = []
    for m in range(mono_dev):
        out_ref[pl.ds(m * basis, half)] = dens_ref[m, :half, half:]
        mixed, diag = fold(
            dens_ref[m, :half, :half].astype(jnp.float32), dens_ref[m, half:, half:].astype(jnp.float32)
        )
        out_ref[pl.ds(m * basis + half, half)] = mixed.astype(out_ref.dtype)
        diags.append(diag)
    rows = out_ref.shape[0] - mono_dev * basis
    row = lax.broadcasted_iota(jnp.int32, (rows, half), 0)
    tail = jnp.zeros((rows, half), jnp.float32)
    for m in range(mono_dev):
        tail = jnp.where(row == m, diags[m], tail)
    out_ref[pl.ds(mono_dev * basis, rows)] = tail.astype(out_ref.dtype)


def couple_kernel(groups, lanes, mono_dev, nbr_ref, esp_ref, *refs):
    n_pieces = groups * lanes
    pieces = refs[:n_pieces]
    own_ref = refs[n_pieces]
    outs = refs[n_pieces + 1 : n_pieces + lanes]
    store = refs[n_pieces + lanes]
    my_group = lax.axis_index("gddi")
    my_lane = lax.axis_index("intra")
    mono_grp, slot_dev, basis, _ = esp_ref.shape
    half = basis // 2
    tail_rows = store.shape[1] - mono_dev * basis
    for i, piece in enumerate(pieces):
        store[i] = piece[...]

    def near_density(fragment):
        apart = (fragment // mono_grp) ^ my_group
        lane = ((fragment % mono_grp) // mono_dev) ^ my_lane
        place = ((apart & 1) * (groups // 2) + (apart >> 1)) * lanes + lane
        member = fragment % mono_dev
        start = pl.multiple_of(member * basis, basis)
        off = store[place, pl.ds(start, half)]
        mixed = store[place, pl.ds(start + half, half)].astype(jnp.float32)
        tail = store[place, pl.ds(mono_dev * basis, tail_rows)].astype(jnp.float32)
        row = lax.broadcasted_iota(jnp.int32, (tail_rows, half), 0)
        diag = jnp.sum(jnp.where(row == member, tail, 0.0), axis=0, keepdims=True)
        first, second = unfold(mixed, diag)
        top = jnp.concatenate([first.astype(off.dtype), off], axis=1)
        bottom = jnp.concatenate([off.T, second.astype(off.dtype)], axis=1)
        return jnp.concatenate([top, bottom], axis=0)

    def partial_of(mine):
        total = None
        for s in range(slot_dev):
            name = nbr_ref[my_group * mono_grp + mine, my_lane * slot_dev + s]
            block = esp_ref[mine, s]
            half_term = jnp.dot(block, near_density(name), preferred_element_type=jnp.float32)
            high = half_term.astype(jnp.bfloat16)
            low = (half_term - high.astype(jnp.float32)).astype(jnp.bfloat16)
            term = transposed_dot(high, block) + transposed_dot(low, block)
            total = term if total is None else total + term
        mixed, diag = fold(total[:half, :half], total[half:, half:])
        return total[:half, half:], mixed, diag

    for k in range(1, lanes):
        out = outs[k - 1]
        tail = []
        for m in range(mono_dev):
            off, mixed, diag = partial_of((my_lane ^ k) * mono_dev + m)
            off_code = scale_code(peak_of(off))
            mixed_code = scale_code(jnp.maximum(peak_of(mixed), jnp.abs(diag)))
            out[pl.ds(m * half, half)] = pack(encode(off, off_code), encode(mixed, mixed_code))
            tail += [pack(off_code, mixed_code), encode(diag, mixed_code)]
        row = lax.broadcasted_iota(jnp.int32, (out.shape[0] - mono_dev * half, half), 0)
        last = jnp.zeros(row.shape, jnp.int32)
        for i, values in enumerate(tail):
            last = jnp.where(row == i, values, last)
        out[pl.ds(mono_dev * half, row.shape[0])] = last
    for m in range(mono_dev):
        off, mixed, diag = partial_of(my_lane * mono_dev + m)
        own_ref[m, :half] = off
        own_ref[m, half : 2 * half] = mixed
        own_ref[m, 2 * half :] = jnp.broadcast_to(diag, (8, half))


def finish_kernel(core_ref, own_ref, *refs):
    parts, out_ref = refs[:-1], refs[-1]
    mono_dev, basis, _ = out_ref.shape
    half = basis // 2
    for m in range(mono_dev):
        off = own_ref[m, :half]
        mixed = own_ref[m, half : 2 * half]
        diag = own_ref[m, 2 * half : 2 * half + 1]
        for part in parts:
            tail = mono_dev * half + 2 * m
            off_code, mixed_code = unpack(part[tail : tail + 1])
            off_q, mixed_q = unpack(part[m * half : (m + 1) * half])
            off = off + decode(off_q, off_code)
            mixed = mixed + decode(mixed_q, mixed_code)
            diag = diag + decode(part[tail + 1 : tail + 2], mixed_code)
        first, second = unfold(mixed, diag)
        core = core_ref[m].astype(jnp.float32)
        out_ref[m, :half, :half] = core[:half, :half] + first
        out_ref[m, :half, half:] = core[:half, half:] + off
        out_ref[m, half:, :half] = core[half:, :half] + off.T
        out_ref[m, half:, half:] = core[half:, half:] + second


def local(density, h_core, esp_block, nbr):
    groups = lax.axis_size("gddi")
    lanes = lax.axis_size("intra")
    mono_dev, basis = density.shape[0], density.shape[1]
    half = basis // 2

    rows = mono_dev * basis + round_up(mono_dev, 16)
    shard = pl.pallas_call(
        fold_kernel,
        out_shape=jax.ShapeDtypeStruct((rows, half), density.dtype),
        in_specs=[IN_VMEM],
        out_specs=IN_VMEM,
        name="fold",
    )(density)
    row = [shard if k == 0 else lax.ppermute(shard, "intra", xor_pairs(lanes, k)) for k in range(lanes)]
    near = []
    for k in range(groups // 2):
        for piece in row:
            near.append(piece if k == 0 else lax.ppermute(piece, "gddi", xor_pairs(groups, 2 * k)))
    pieces = near + [lax.ppermute(piece, "gddi", xor_pairs(groups, 1)) for piece in near]

    own = jax.ShapeDtypeStruct((mono_dev, basis + 8, half), jnp.float32)
    coded = jax.ShapeDtypeStruct((mono_dev * half + round_up(2 * mono_dev, 8), half), jnp.int32)
    piece_bytes = len(pieces) * rows * half * 2
    partials = pl.pallas_call(
        functools.partial(couple_kernel, groups, lanes, mono_dev),
        out_shape=[own] + [coded] * (lanes - 1),
        in_specs=[IN_SMEM] + [IN_VMEM] * (1 + len(pieces)),
        out_specs=[IN_VMEM] * lanes,
        scratch_shapes=[pltpu.VMEM((len(pieces), rows, half), density.dtype)],
        compiler_params=pltpu.CompilerParams(
            vmem_limit_bytes=2 * (piece_bytes + esp_block.size * 2) + 8 * 2**20
        ),
        name="couple",
    )(nbr, esp_block, *pieces)

    terms = [lax.ppermute(partials[k], "intra", xor_pairs(lanes, k)) for k in range(1, lanes)]
    return pl.pallas_call(
        finish_kernel,
        out_shape=jax.ShapeDtypeStruct((mono_dev, basis, basis), jnp.float32),
        in_specs=[IN_VMEM] * (1 + lanes),
        out_specs=IN_VMEM,
        name="finish",
    )(h_core, partials[0], *terms)


def solution(mesh):
    return jax.shard_map(
        local,
        mesh=mesh,
        in_specs=(
            P(("job", "gddi", "intra"), None, None),
            P(("job", "gddi", "intra"), None, None),
            P(("job", "gddi"), "intra", None, None),
            P("job", None),
        ),
        out_specs=P(("job", "gddi", "intra"), None, None),
        check_vma=False,
    )
```

```python
import functools

import jax
import jax.numpy as jnp
from jax import lax
from jax.experimental import pallas as pl
from jax.experimental.pallas import tpu as pltpu
from jax.sharding import PartitionSpec as P

STEPS = 32.0
TOP = 32000.0
SHRINK = 1.0 / 16.0
IN_VMEM = pl.BlockSpec(memory_space=pltpu.VMEM)
IN_SMEM = pl.BlockSpec(memory_space=pltpu.SMEM)


def xor_pairs(size, k):
    return [(i, i ^ k) for i in range(size)]


def round_up(n, to):
    return -(-n // to) * to


def transposed_dot(a, b):
    return lax.dot_general(a, b, (((1,), (1,)), ((), ())), preferred_element_type=jnp.float32)


def square_iotas(half):
    row = lax.broadcasted_iota(jnp.int32, (half, half), 0)
    col = lax.broadcasted_iota(jnp.int32, (half, half), 1)
    return row, col


def fold(first, second):
    row, col = square_iotas(first.shape[0])
    mixed = jnp.where(row <= col, first, second)
    diag = jnp.sum(jnp.where(row == col, second, 0.0), axis=0, keepdims=True)
    return mixed, diag


def unfold(mixed, diag):
    row, col = square_iotas(mixed.shape[0])
    turned = mixed.T
    first = jnp.where(row <= col, mixed, turned)
    second = jnp.where(row > col, mixed, jnp.where(row < col, turned, diag))
    return first, second


def scale_code(peak):
    wanted = jnp.log(jnp.maximum(peak * SHRINK, 2.0**-120)) * STEPS
    return jnp.floor(wanted + 1.5).astype(jnp.int32)


def encode(x, code):
    units = jnp.exp(code.astype(jnp.float32) * (-1.0 / STEPS)) * TOP
    return jnp.floor(x * SHRINK * units + 0.5).astype(jnp.int32)


def decode(q, code):
    units = jnp.exp(code.astype(jnp.float32) * (1.0 / STEPS)) * (1.0 / TOP)
    return q.astype(jnp.float32) * units * (1.0 / SHRINK)


def pack(high, low):
    return lax.shift_left(high, 16) | (low & 0xFFFF)


def unpack(word):
    return lax.shift_right_arithmetic(word, 16), lax.shift_right_arithmetic(lax.shift_left(word, 16), 16)


def peak_of(x):
    return jnp.max(jnp.abs(x), axis=0, keepdims=True)


def fold_kernel(dens_ref, out_ref):
    mono_dev, basis, _ = dens_ref.shape
    half = basis // 2
    diags = []
    for m in range(mono_dev):
        out_ref[pl.ds(m * basis, half)] = dens_ref[m, :half, half:]
        mixed, diag = fold(
            dens_ref[m, :half, :half].astype(jnp.float32), dens_ref[m, half:, half:].astype(jnp.float32)
        )
        out_ref[pl.ds(m * basis + half, half)] = mixed.astype(out_ref.dtype)
        diags.append(diag)
    rows = out_ref.shape[0] - mono_dev * basis
    row = lax.broadcasted_iota(jnp.int32, (rows, half), 0)
    tail = jnp.zeros((rows, half), jnp.float32)
    for m in range(mono_dev):
        tail = jnp.where(row == m, diags[m], tail)
    out_ref[pl.ds(mono_dev * basis, rows)] = tail.astype(out_ref.dtype)


def couple_kernel(groups, lanes, mono_dev, units, nbr_ref, esp_ref, *refs):
    outs = refs[-3 - len(units) : -3]
    pieces = refs[: -3 - len(units)]
    store, blocks, sems = refs[-3:]
    my_group = lax.axis_index("gddi")
    my_lane = lax.axis_index("intra")
    _, slot_dev, basis, _ = esp_ref.shape
    mono_grp = mono_dev * lanes
    half = basis // 2
    tail_rows = store.shape[1] - mono_dev * basis
    fragments = [(my_lane ^ k) * mono_dev + m for k in units for m in range(mono_dev)]
    copies = [pltpu.make_async_copy(esp_ref.at[f], blocks.at[i], sems.at[i]) for i, f in enumerate(fragments)]
    for copy in copies:
        copy.start()
    for i, piece in enumerate(pieces):
        store[i] = piece[...]

    def near_density(fragment):
        apart = (fragment // mono_grp) ^ my_group
        lane = ((fragment % mono_grp) // mono_dev) ^ my_lane
        place = ((apart & 1) * (groups // 2) + (apart >> 1)) * lanes + lane
        member = fragment % mono_dev
        start = pl.multiple_of(member * basis, basis)
        off = store[place, pl.ds(start, half)]
        mixed = store[place, pl.ds(start + half, half)].astype(jnp.float32)
        tail = store[place, pl.ds(mono_dev * basis, tail_rows)].astype(jnp.float32)
        row = lax.broadcasted_iota(jnp.int32, (tail_rows, half), 0)
        diag = jnp.sum(jnp.where(row == member, tail, 0.0), axis=0, keepdims=True)
        first, second = unfold(mixed, diag)
        top = jnp.concatenate([first.astype(off.dtype), off], axis=1)
        bottom = jnp.concatenate([off.T, second.astype(off.dtype)], axis=1)
        return jnp.concatenate([top, bottom], axis=0)

    def partial_of(i):
        copies[i].wait()
        total = None
        for s in range(slot_dev):
            name = nbr_ref[my_lane * slot_dev + s, my_group * mono_grp + fragments[i]]
            block = blocks[i, s]
            half_term = jnp.dot(block, near_density(name), preferred_element_type=jnp.float32)
            high = half_term.astype(jnp.bfloat16)
            low = (half_term - high.astype(jnp.float32)).astype(jnp.bfloat16)
            term = transposed_dot(high, block) + transposed_dot(low, block)
            total = term if total is None else total + term
        mixed, diag = fold(total[:half, :half], total[half:, half:])
        return total[:half, half:], mixed, diag

    for i, (k, out) in enumerate(zip(units, outs)):
        if k == 0:
            for m in range(mono_dev):
                off, mixed, diag = partial_of(i * mono_dev + m)
                out[m, :half] = off
                out[m, half : 2 * half] = mixed
                out[m, 2 * half :] = jnp.broadcast_to(diag, (8, half))
            continue
        tail = []
        for m in range(mono_dev):
            off, mixed, diag = partial_of(i * mono_dev + m)
            off_code = scale_code(peak_of(off))
            mixed_code = scale_code(jnp.maximum(peak_of(mixed), jnp.abs(diag)))
            out[pl.ds(m * half, half)] = pack(encode(off, off_code), encode(mixed, mixed_code))
            tail += [pack(off_code, mixed_code), encode(diag, mixed_code)]
        row = lax.broadcasted_iota(jnp.int32, (out.shape[0] - mono_dev * half, half), 0)
        last = jnp.zeros(row.shape, jnp.int32)
        for i, values in enumerate(tail):
            last = jnp.where(row == i, values, last)
        out[pl.ds(mono_dev * half, row.shape[0])] = last


def finish_kernel(core_ref, own_ref, *refs):
    parts, out_ref = refs[:-1], refs[-1]
    mono_dev, basis, _ = out_ref.shape
    half = basis // 2
    for m in range(mono_dev):
        off = own_ref[m, :half]
        mixed = own_ref[m, half : 2 * half]
        diag = own_ref[m, 2 * half : 2 * half + 1]
        for part in parts:
            tail = mono_dev * half + 2 * m
            off_code, mixed_code = unpack(part[tail : tail + 1])
            off_q, mixed_q = unpack(part[m * half : (m + 1) * half])
            off = off + decode(off_q, off_code)
            mixed = mixed + decode(mixed_q, mixed_code)
            diag = diag + decode(part[tail + 1 : tail + 2], mixed_code)
        first, second = unfold(mixed, diag)
        core = core_ref[m].astype(jnp.float32)
        out_ref[m, :half, :half] = core[:half, :half] + first
        out_ref[m, :half, half:] = core[:half, half:] + off
        out_ref[m, half:, :half] = core[half:, :half] + off.T
        out_ref[m, half:, half:] = core[half:, half:] + second


def local(density, h_core, esp_block, nbr):
    groups = lax.axis_size("gddi")
    lanes = lax.axis_size("intra")
    mono_dev, basis = density.shape[0], density.shape[1]
    half = basis // 2
    small = pltpu.CompilerParams(vmem_limit_bytes=8 * 2**20)

    rows = mono_dev * basis + round_up(mono_dev, 16)
    shard = pl.pallas_call(
        fold_kernel,
        out_shape=jax.ShapeDtypeStruct((rows, half), density.dtype),
        in_specs=[IN_VMEM],
        out_specs=IN_VMEM,
        compiler_params=small,
        name="fold",
    )(density)
    row = {0: shard}
    bit = lanes // 2
    while bit:
        for k in list(row):
            row[k ^ bit] = lax.ppermute(row[k], "intra", xor_pairs(lanes, bit))
        bit //= 2
    near = []
    for y in range(groups // 2):
        for k in range(lanes):
            near.append(row[k] if y == 0 else lax.ppermute(row[k], "gddi", xor_pairs(groups, 2 * y)))
    pieces = near + [lax.ppermute(piece, "gddi", xor_pairs(groups, 1)) for piece in near]

    own = jax.ShapeDtypeStruct((mono_dev, basis + 8, half), jnp.float32)
    coded = jax.ShapeDtypeStruct((mono_dev * half + round_up(2 * mono_dev, 8), half), jnp.int32)
    piece_bytes = len(pieces) * rows * half * 2

    blocks = pltpu.with_memory_space_constraint(esp_block, pltpu.HBM)

    names = pltpu.with_memory_space_constraint(nbr.T, pltpu.HBM)

    def couple(units, name):
        return pl.pallas_call(
            functools.partial(couple_kernel, groups, lanes, mono_dev, units),
            out_shape=[own if k == 0 else coded for k in units],
            in_specs=[IN_SMEM, pl.BlockSpec(memory_space=pl.ANY)] + [IN_VMEM] * len(pieces),
            out_specs=[IN_VMEM] * len(units),
            scratch_shapes=[
                pltpu.VMEM((len(pieces), rows, half), density.dtype),
                pltpu.VMEM((len(units) * mono_dev,) + esp_block.shape[1:], esp_block.dtype),
                pltpu.SemaphoreType.DMA((len(units) * mono_dev,)),
            ],
            compiler_params=pltpu.CompilerParams(
                vmem_limit_bytes=2 * (piece_bytes + esp_block.size * 2) + 8 * 2**20
            ),
            name=name,
        )(names, blocks, *pieces)

    far_units = range(lanes // 2, lanes)
    near_units = range(lanes // 2)
    far = couple(far_units, "couple_far")
    far_terms = [lax.ppermute(far[k - lanes // 2], "intra", xor_pairs(lanes, k)) for k in far_units]
    close = couple(near_units, "couple_near")
    close_terms = [lax.ppermute(close[k], "intra", xor_pairs(lanes, k)) for k in near_units[1:]]
    return pl.pallas_call(
        finish_kernel,
        out_shape=jax.ShapeDtypeStruct((mono_dev, basis, basis), jnp.float32),
        in_specs=[IN_VMEM] * (1 + lanes),
        out_specs=IN_VMEM,
        compiler_params=small,
        name="finish",
    )(h_core, close[0], *close_terms, *far_terms)


def solution(mesh):
    return jax.shard_map(
        local,
        mesh=mesh,
        in_specs=(
            P(("job", "gddi", "intra"), None, None),
            P(("job", "gddi", "intra"), None, None),
            P(("job", "gddi"), "intra", None, None),
            P("job", None),
        ),
        out_specs=P(("job", "gddi", "intra"), None, None),
        check_vma=False,
    )
```

```python
import functools

import jax
import jax.numpy as jnp
from jax import lax
from jax.experimental import pallas as pl
from jax.experimental.pallas import tpu as pltpu
from jax.sharding import PartitionSpec as P

STEPS = 32.0
TOP = 32000.0
SHRINK = 1.0 / 16.0
IN_VMEM = pl.BlockSpec(memory_space=pltpu.VMEM)
IN_SMEM = pl.BlockSpec(memory_space=pltpu.SMEM)


def xor_pairs(size, k):
    return [(i, i ^ k) for i in range(size)]


def round_up(n, to):
    return -(-n // to) * to


def transposed_dot(a, b):
    return lax.dot_general(a, b, (((1,), (1,)), ((), ())), preferred_element_type=jnp.float32)


def square_iotas(half):
    row = lax.broadcasted_iota(jnp.int32, (half, half), 0)
    col = lax.broadcasted_iota(jnp.int32, (half, half), 1)
    return row, col


def fold(first, second):
    row, col = square_iotas(first.shape[0])
    mixed = jnp.where(row <= col, first, second)
    diag = jnp.sum(jnp.where(row == col, second, 0.0), axis=0, keepdims=True)
    return mixed, diag


def unfold(mixed, diag):
    row, col = square_iotas(mixed.shape[0])
    turned = mixed.T
    first = jnp.where(row <= col, mixed, turned)
    second = jnp.where(row > col, mixed, jnp.where(row < col, turned, diag))
    return first, second


def scale_code(peak):
    wanted = jnp.log(jnp.maximum(peak * SHRINK, 2.0**-120)) * STEPS
    return jnp.floor(wanted + 1.5).astype(jnp.int32)


def encode(x, code):
    units = jnp.exp(code.astype(jnp.float32) * (-1.0 / STEPS)) * TOP
    return jnp.floor(x * SHRINK * units + 0.5).astype(jnp.int32)


def decode(q, code):
    units = jnp.exp(code.astype(jnp.float32) * (1.0 / STEPS)) * (1.0 / TOP)
    return q.astype(jnp.float32) * units * (1.0 / SHRINK)


def pack(high, low):
    return lax.shift_left(high, 16) | (low & 0xFFFF)


def unpack(word):
    return lax.shift_right_arithmetic(word, 16), lax.shift_right_arithmetic(lax.shift_left(word, 16), 16)


def peak_of(x):
    return jnp.max(jnp.abs(x), axis=0, keepdims=True)


def fold_kernel(dens_ref, out_ref):
    mono_dev, basis, _ = dens_ref.shape
    half = basis // 2
    diags = []
    for m in range(mono_dev):
        out_ref[pl.ds(m * basis, half)] = dens_ref[m, :half, half:]
        mixed, diag = fold(
            dens_ref[m, :half, :half].astype(jnp.float32), dens_ref[m, half:, half:].astype(jnp.float32)
        )
        out_ref[pl.ds(m * basis + half, half)] = mixed.astype(out_ref.dtype)
        diags.append(diag)
    rows = out_ref.shape[0] - mono_dev * basis
    row = lax.broadcasted_iota(jnp.int32, (rows, half), 0)
    tail = jnp.zeros((rows, half), jnp.float32)
    for m in range(mono_dev):
        tail = jnp.where(row == m, diags[m], tail)
    out_ref[pl.ds(mono_dev * basis, rows)] = tail.astype(out_ref.dtype)


def gate_kernel(piece_ref, *refs):
    refs[-1][...] = piece_ref[...]


def gather_kernel(*refs):
    for i, piece in enumerate(refs[:-1]):
        refs[-1][i] = piece[...]


def stage_kernel(nbr_ref, esp_ref, *refs):
    nbr_out, esp_out, row_out, sems = refs[-4:]
    copies = [
        pltpu.make_async_copy(esp_ref, esp_out, sems.at[0]),
        pltpu.make_async_copy(nbr_ref, nbr_out, sems.at[1]),
    ]
    for copy in copies:
        copy.start()
    for i, piece in enumerate(refs[:-4]):
        row_out[i] = piece[...]
    for copy in copies:
        copy.wait()


def couple_kernel(groups, lanes, mono_dev, units, places, nbr_ref, esp_ref, *refs):
    pieces, outs, store = refs[: len(places)], refs[len(places) : -1], refs[-1]
    my_group = lax.axis_index("gddi")
    my_lane = lax.axis_index("intra")
    _, slot_dev, basis, _ = esp_ref.shape
    mono_grp = mono_dev * lanes
    half = basis // 2
    tail_rows = store.shape[1] - mono_dev * basis
    for piece, where in zip(pieces, places):
        for i, place in enumerate(where):
            store[place] = piece[i]

    def near_density(fragment):
        apart = (fragment // mono_grp) ^ my_group
        lane = ((fragment % mono_grp) // mono_dev) ^ my_lane
        place = ((apart & 1) * (groups // 2) + (apart >> 1)) * lanes + lane
        member = fragment % mono_dev
        start = pl.multiple_of(member * basis, basis)
        off = store[place, pl.ds(start, half)]
        mixed = store[place, pl.ds(start + half, half)].astype(jnp.float32)
        tail = store[place, pl.ds(mono_dev * basis, tail_rows)].astype(jnp.float32)
        row = lax.broadcasted_iota(jnp.int32, (tail_rows, half), 0)
        diag = jnp.sum(jnp.where(row == member, tail, 0.0), axis=0, keepdims=True)
        first, second = unfold(mixed, diag)
        top = jnp.concatenate([first.astype(off.dtype), off], axis=1)
        bottom = jnp.concatenate([off.T, second.astype(off.dtype)], axis=1)
        return jnp.concatenate([top, bottom], axis=0)

    def partial_of(fragment):
        total = None
        for s in range(slot_dev):
            name = nbr_ref[my_lane * slot_dev + s, my_group * mono_grp + fragment]
            block = esp_ref[fragment, s]
            half_term = jnp.dot(block, near_density(name), preferred_element_type=jnp.float32)
            high = half_term.astype(jnp.bfloat16)
            low = (half_term - high.astype(jnp.float32)).astype(jnp.bfloat16)
            term = transposed_dot(high, block) + transposed_dot(low, block)
            total = term if total is None else total + term
        mixed, diag = fold(total[:half, :half], total[half:, half:])
        return total[:half, half:], mixed, diag

    for k, out in zip(units, outs):
        if k == 0:
            for m in range(mono_dev):
                off, mixed, diag = partial_of((my_lane ^ k) * mono_dev + m)
                out[m, :half] = off
                out[m, half : 2 * half] = mixed
                out[m, 2 * half :] = jnp.broadcast_to(diag, (8, half))
            continue
        tail = []
        for m in range(mono_dev):
            off, mixed, diag = partial_of((my_lane ^ k) * mono_dev + m)
            off_code = scale_code(peak_of(off))
            mixed_code = scale_code(jnp.maximum(peak_of(mixed), jnp.abs(diag)))
            out[pl.ds(m * half, half)] = pack(encode(off, off_code), encode(mixed, mixed_code))
            tail += [pack(off_code, mixed_code), encode(diag, mixed_code)]
        row = lax.broadcasted_iota(jnp.int32, (out.shape[0] - mono_dev * half, half), 0)
        last = jnp.zeros(row.shape, jnp.int32)
        for i, values in enumerate(tail):
            last = jnp.where(row == i, values, last)
        out[pl.ds(mono_dev * half, row.shape[0])] = last


def finish_kernel(core_ref, own_ref, *refs):
    parts, out_ref = refs[:-1], refs[-1]
    mono_dev, basis, _ = out_ref.shape
    half = basis // 2
    for m in range(mono_dev):
        off = own_ref[m, :half]
        mixed = own_ref[m, half : 2 * half]
        diag = own_ref[m, 2 * half : 2 * half + 1]
        for part in parts:
            tail = mono_dev * half + 2 * m
            off_code, mixed_code = unpack(part[tail : tail + 1])
            off_q, mixed_q = unpack(part[m * half : (m + 1) * half])
            off = off + decode(off_q, off_code)
            mixed = mixed + decode(mixed_q, mixed_code)
            diag = diag + decode(part[tail + 1 : tail + 2], mixed_code)
        first, second = unfold(mixed, diag)
        core = core_ref[m].astype(jnp.float32)
        out_ref[m, :half, :half] = core[:half, :half] + first
        out_ref[m, :half, half:] = core[:half, half:] + off
        out_ref[m, half:, :half] = core[half:, :half] + off.T
        out_ref[m, half:, half:] = core[half:, half:] + second


def local(density, h_core, esp_block, nbr):
    groups = lax.axis_size("gddi")
    lanes = lax.axis_size("intra")
    mono_dev, basis = density.shape[0], density.shape[1]
    half = basis // 2
    hbm = pl.BlockSpec(memory_space=pl.ANY)
    small = pltpu.CompilerParams(vmem_limit_bytes=8 * 2**20)

    rows = mono_dev * basis + round_up(mono_dev, 16)
    shard = pl.pallas_call(
        fold_kernel,
        out_shape=jax.ShapeDtypeStruct((rows, half), density.dtype),
        in_specs=[IN_VMEM],
        out_specs=IN_VMEM,
        compiler_params=small,
        name="fold",
    )(density)
    def along_z(piece, bit):
        return lax.ppermute(piece, "intra", xor_pairs(lanes, bit))

    def along_y(piece, y):
        return lax.ppermute(piece, "gddi", xor_pairs(groups, 2 * y))

    rows_y = groups // 2
    top = lanes // 2
    near = {(0, 0): shard, (0, top): along_z(shard, top)}
    bit = top // 2
    while bit:
        near[0, bit] = along_z(shard, bit)
        bit //= 2
    for y in range(1, rows_y):
        near[y, 0] = along_y(shard, y)
    others = [piece for key, piece in near.items() if key != (0, top)]
    for after in ([], others):
        near[0, top] = pl.pallas_call(
            gate_kernel,
            out_shape=pltpu.VMEM(shard.shape, shard.dtype),
            in_specs=[IN_VMEM] + [hbm] * len(after),
            out_specs=IN_VMEM,
            compiler_params=small,
            name="gate",
        )(near[0, top], *after)
    bit = top // 2
    while bit:
        for k in [k for y, k in near if y == 0 and k and (0, k ^ bit) not in near]:
            near[0, k ^ bit] = along_z(near[0, k], bit)
        bit //= 2
    for y in range(1, rows_y):
        for k in range(1, lanes):
            near[y, k] = along_y(near[0, k], y)

    early = [(y, k) for y, k in near if (y > 0) + bin(k).count("1") <= 1]
    later = [key for key in near if key not in early]

    def shape(count):
        return pltpu.VMEM((count, rows, half), density.dtype)

    names, blocks, first = pl.pallas_call(
        stage_kernel,
        out_shape=[
            pltpu.SMEM((nbr.shape[1], nbr.shape[0]), nbr.dtype),
            pltpu.VMEM(esp_block.shape, esp_block.dtype),
            shape(len(early)),
        ],
        in_specs=[hbm, hbm] + [IN_VMEM] * len(early),
        out_specs=[IN_SMEM, IN_VMEM, IN_VMEM],
        scratch_shapes=[pltpu.SemaphoreType.DMA((2,))],
        compiler_params=small,
        name="stage",
    )(
        pltpu.with_memory_space_constraint(nbr.T, pltpu.HBM),
        pltpu.with_memory_space_constraint(esp_block, pltpu.HBM),
        *[near[key] for key in early],
    )
    second = pl.pallas_call(
        gather_kernel,
        out_shape=shape(len(later)),
        in_specs=[IN_VMEM] * len(later),
        out_specs=IN_VMEM,
        compiler_params=pltpu.CompilerParams(vmem_limit_bytes=2 * len(later) * rows * half * 2 + 4 * 2**20),
        name="gather",
    )(*[near[key] for key in later])
    mine = [first, second]
    pieces = mine + [lax.ppermute(piece, "gddi", xor_pairs(groups, 1)) for piece in mine]
    places = [[y * lanes + k for y, k in keys] for keys in (early, later)]
    places += [[rows_y * lanes + place for place in keys] for keys in places]

    own = jax.ShapeDtypeStruct((mono_dev, basis + 8, half), jnp.float32)
    coded = jax.ShapeDtypeStruct((mono_dev * half + round_up(2 * mono_dev, 8), half), jnp.int32)
    piece_bytes = groups * lanes * rows * half * 2

    def couple(units, name):
        return pl.pallas_call(
            functools.partial(couple_kernel, groups, lanes, mono_dev, units, places),
            out_shape=[own if k == 0 else coded for k in units],
            in_specs=[IN_SMEM] + [IN_VMEM] * (1 + len(pieces)),
            out_specs=[IN_VMEM] * len(units),
            scratch_shapes=[pltpu.VMEM((groups * lanes, rows, half), density.dtype)],
            compiler_params=pltpu.CompilerParams(
                vmem_limit_bytes=2 * (piece_bytes + esp_block.size * 2) + 8 * 2**20
            ),
            name=name,
        )(names, blocks, *pieces)

    far_units = range(lanes // 2, lanes)
    near_units = range(lanes // 2)
    far = couple(far_units, "couple_far")
    far_terms = [lax.ppermute(far[k - lanes // 2], "intra", xor_pairs(lanes, k)) for k in far_units]
    close = couple(near_units, "couple_near")
    close_terms = [lax.ppermute(close[k], "intra", xor_pairs(lanes, k)) for k in near_units[1:]]
    return pl.pallas_call(
        finish_kernel,
        out_shape=jax.ShapeDtypeStruct((mono_dev, basis, basis), jnp.float32),
        in_specs=[IN_VMEM] * (1 + lanes),
        out_specs=IN_VMEM,
        compiler_params=small,
        name="finish",
    )(h_core, close[0], *close_terms, *far_terms)


def solution(mesh):
    return jax.shard_map(
        local,
        mesh=mesh,
        in_specs=(
            P(("job", "gddi", "intra"), None, None),
            P(("job", "gddi", "intra"), None, None),
            P(("job", "gddi"), "intra", None, None),
            P("job", None),
        ),
        out_specs=P(("job", "gddi", "intra"), None, None),
        check_vma=False,
    )
```

```python
import functools

import jax
import jax.numpy as jnp
from jax import lax
from jax.experimental import pallas as pl
from jax.experimental.pallas import tpu as pltpu
from jax.sharding import PartitionSpec as P

STEPS = 32.0
TOP = 32000.0
SHRINK = 1.0 / 16.0
IN_VMEM = pl.BlockSpec(memory_space=pltpu.VMEM)
IN_SMEM = pl.BlockSpec(memory_space=pltpu.SMEM)


def xor_pairs(size, k):
    return [(i, i ^ k) for i in range(size)]


def round_up(n, to):
    return -(-n // to) * to


def transposed_dot(a, b):
    return lax.dot_general(a, b, (((1,), (1,)), ((), ())), preferred_element_type=jnp.float32)


def square_iotas(half):
    row = lax.broadcasted_iota(jnp.int32, (half, half), 0)
    col = lax.broadcasted_iota(jnp.int32, (half, half), 1)
    return row, col


def fold(first, second):
    row, col = square_iotas(first.shape[0])
    mixed = jnp.where(row <= col, first, second)
    diag = jnp.sum(jnp.where(row == col, second, 0.0), axis=0, keepdims=True)
    return mixed, diag


def unfold(mixed, diag):
    row, col = square_iotas(mixed.shape[0])
    turned = mixed.T
    first = jnp.where(row <= col, mixed, turned)
    second = jnp.where(row > col, mixed, jnp.where(row < col, turned, diag))
    return first, second


def scale_code(peak):
    wanted = jnp.log(jnp.maximum(peak * SHRINK, 2.0**-120)) * STEPS
    return jnp.floor(wanted + 1.5).astype(jnp.int32)


def encode(x, code):
    units = jnp.exp(code.astype(jnp.float32) * (-1.0 / STEPS)) * TOP
    return jnp.floor(x * SHRINK * units + 0.5).astype(jnp.int32)


def decode(q, code):
    units = jnp.exp(code.astype(jnp.float32) * (1.0 / STEPS)) * (1.0 / TOP)
    return q.astype(jnp.float32) * units * (1.0 / SHRINK)


def pack(high, low):
    return lax.shift_left(high, 16) | (low & 0xFFFF)


def unpack(word):
    return lax.shift_right_arithmetic(word, 16), lax.shift_right_arithmetic(lax.shift_left(word, 16), 16)


def peak_of(x):
    return jnp.max(jnp.abs(x), axis=0, keepdims=True)


def fold_kernel(dens_ref, out_ref):
    mono_dev, basis, _ = dens_ref.shape
    half = basis // 2
    diags = []
    for m in range(mono_dev):
        out_ref[pl.ds(m * basis, half)] = dens_ref[m, :half, half:]
        mixed, diag = fold(
            dens_ref[m, :half, :half].astype(jnp.float32), dens_ref[m, half:, half:].astype(jnp.float32)
        )
        out_ref[pl.ds(m * basis + half, half)] = mixed.astype(out_ref.dtype)
        diags.append(diag)
    rows = out_ref.shape[0] - mono_dev * basis
    row = lax.broadcasted_iota(jnp.int32, (rows, half), 0)
    tail = jnp.zeros((rows, half), jnp.float32)
    for m in range(mono_dev):
        tail = jnp.where(row == m, diags[m], tail)
    out_ref[pl.ds(mono_dev * basis, rows)] = tail.astype(out_ref.dtype)


def gate_kernel(piece_ref, *refs):
    refs[-1][...] = piece_ref[...]


def gather_kernel(*refs):
    for i, piece in enumerate(refs[:-1]):
        refs[-1][i] = piece[...]


def stage_kernel(nbr_ref, esp_ref, *refs):
    nbr_out, esp_out, row_out, sems = refs[-4:]
    copies = [
        pltpu.make_async_copy(esp_ref, esp_out, sems.at[0]),
        pltpu.make_async_copy(nbr_ref, nbr_out, sems.at[1]),
    ]
    for copy in copies:
        copy.start()
    for i, piece in enumerate(refs[:-4]):
        row_out[i] = piece[...]
    for copy in copies:
        copy.wait()


def couple_kernel(groups, lanes, mono_dev, units, places, nbr_ref, esp_ref, *refs):
    pieces, outs, store = refs[: len(places)], refs[len(places) : -1], refs[-1]
    my_group = lax.axis_index("gddi")
    my_lane = lax.axis_index("intra")
    _, slot_dev, basis, _ = esp_ref.shape
    mono_grp = mono_dev * lanes
    half = basis // 2
    tail_rows = store.shape[1] - mono_dev * basis
    for piece, where in zip(pieces, places):
        for i, place in enumerate(where):
            store[place] = piece[i]

    def near_density(fragment):
        apart = (fragment // mono_grp) ^ my_group
        lane = ((fragment % mono_grp) // mono_dev) ^ my_lane
        place = ((apart & 1) * (groups // 2) + (apart >> 1)) * lanes + lane
        member = fragment % mono_dev
        start = pl.multiple_of(member * basis, basis)
        off = store[place, pl.ds(start, half)]
        mixed = store[place, pl.ds(start + half, half)].astype(jnp.float32)
        tail = store[place, pl.ds(mono_dev * basis, tail_rows)].astype(jnp.float32)
        row = lax.broadcasted_iota(jnp.int32, (tail_rows, half), 0)
        diag = jnp.sum(jnp.where(row == member, tail, 0.0), axis=0, keepdims=True)
        first, second = unfold(mixed, diag)
        top = jnp.concatenate([first.astype(off.dtype), off], axis=1)
        bottom = jnp.concatenate([off.T, second.astype(off.dtype)], axis=1)
        return jnp.concatenate([top, bottom], axis=0)

    def partial_of(fragment):
        total = None
        for s in range(slot_dev):
            name = nbr_ref[my_lane * slot_dev + s, my_group * mono_grp + fragment]
            block = esp_ref[fragment, s]
            half_term = jnp.dot(block, near_density(name), preferred_element_type=jnp.float32)
            high = half_term.astype(jnp.bfloat16)
            low = (half_term - high.astype(jnp.float32)).astype(jnp.bfloat16)
            term = transposed_dot(high, block) + transposed_dot(low, block)
            total = term if total is None else total + term
        mixed, diag = fold(total[:half, :half], total[half:, half:])
        return total[:half, half:], mixed, diag

    for k, out in zip(units, outs):
        if k == 0:
            for m in range(mono_dev):
                off, mixed, diag = partial_of((my_lane ^ k) * mono_dev + m)
                out[m, :half] = off
                out[m, half : 2 * half] = mixed
                out[m, 2 * half :] = jnp.broadcast_to(diag, (8, half))
            continue
        tail = []
        for m in range(mono_dev):
            off, mixed, diag = partial_of((my_lane ^ k) * mono_dev + m)
            off_code = scale_code(peak_of(off))
            mixed_code = scale_code(jnp.maximum(peak_of(mixed), jnp.abs(diag)))
            out[pl.ds(m * half, half)] = pack(encode(off, off_code), encode(mixed, mixed_code))
            tail += [pack(off_code, mixed_code), encode(diag, mixed_code)]
        row = lax.broadcasted_iota(jnp.int32, (out.shape[0] - mono_dev * half, half), 0)
        last = jnp.zeros(row.shape, jnp.int32)
        for i, values in enumerate(tail):
            last = jnp.where(row == i, values, last)
        out[pl.ds(mono_dev * half, row.shape[0])] = last


def finish_kernel(core_ref, own_ref, *refs):
    parts, out_ref = refs[:-1], refs[-1]
    mono_dev, basis, _ = out_ref.shape
    half = basis // 2
    for m in range(mono_dev):
        off = own_ref[m, :half]
        mixed = own_ref[m, half : 2 * half]
        diag = own_ref[m, 2 * half : 2 * half + 1]
        for part in parts:
            tail = mono_dev * half + 2 * m
            off_code, mixed_code = unpack(part[tail : tail + 1])
            off_q, mixed_q = unpack(part[m * half : (m + 1) * half])
            off = off + decode(off_q, off_code)
            mixed = mixed + decode(mixed_q, mixed_code)
            diag = diag + decode(part[tail + 1 : tail + 2], mixed_code)
        first, second = unfold(mixed, diag)
        core = core_ref[m].astype(jnp.float32)
        out_ref[m, :half, :half] = core[:half, :half] + first
        out_ref[m, :half, half:] = core[:half, half:] + off
        out_ref[m, half:, :half] = core[half:, :half] + off.T
        out_ref[m, half:, half:] = core[half:, half:] + second


def local(density, h_core, esp_block, nbr):
    groups = lax.axis_size("gddi")
    lanes = lax.axis_size("intra")
    mono_dev, basis = density.shape[0], density.shape[1]
    half = basis // 2
    hbm = pl.BlockSpec(memory_space=pl.ANY)
    small = pltpu.CompilerParams(vmem_limit_bytes=8 * 2**20)

    rows = mono_dev * basis + round_up(mono_dev, 16)
    shard = pl.pallas_call(
        fold_kernel,
        out_shape=jax.ShapeDtypeStruct((rows, half), density.dtype),
        in_specs=[IN_VMEM],
        out_specs=IN_VMEM,
        compiler_params=small,
        name="fold",
    )(density)
    def along_z(piece, bit):
        return lax.ppermute(piece, "intra", xor_pairs(lanes, bit))

    def along_y(piece, y):
        return lax.ppermute(piece, "gddi", xor_pairs(groups, 2 * y))

    rows_y = groups // 2
    top = lanes // 2
    near = {(0, 0): shard, (0, top): along_z(shard, top)}

    def double(start):
        bit = top // 2
        while bit:
            for k in range(start, start + top):
                if (0, k) in near and (0, k ^ bit) not in near:
                    near[0, k ^ bit] = along_z(near[0, k], bit)
            bit //= 2

    double(0)
    for y in range(1, rows_y):
        near[y, 0] = along_y(shard, y)

    def gate(piece, *after):
        return pl.pallas_call(
            gate_kernel,
            out_shape=pltpu.VMEM(shard.shape, shard.dtype),
            in_specs=[IN_VMEM] + [hbm] * len(after),
            out_specs=IN_VMEM,
            compiler_params=small,
            name="gate",
        )(piece, *after)

    others = [piece for key, piece in near.items() if key != (0, top)]
    near[0, top] = gate(gate(near[0, top]), *others)
    for y in range(1, rows_y):
        for k in range(1, top):
            near[y, k] = along_y(near[0, k], y)
    double(top)
    ahead = [near[y, k] for y in range(1, rows_y) for k in range(1, top)]
    for _ in range(3):
        ahead = [gate(ahead[0], *ahead[1:])]
    for y in range(1, rows_y):
        near[y, top] = along_y(near[0, top], y)
        for k in range(top + 1, lanes):
            near[y, k] = along_y(gate(near[0, k], *ahead), y)

    early = [(y, k) for y, k in near if (y > 0) + bin(k).count("1") <= 1]
    later = [key for key in near if key not in early]

    def shape(count):
        return pltpu.VMEM((count, rows, half), density.dtype)

    names, blocks, first = pl.pallas_call(
        stage_kernel,
        out_shape=[
            pltpu.SMEM((nbr.shape[1], nbr.shape[0]), nbr.dtype),
            pltpu.VMEM(esp_block.shape, esp_block.dtype),
            shape(len(early)),
        ],
        in_specs=[hbm, hbm] + [IN_VMEM] * len(early),
        out_specs=[IN_SMEM, IN_VMEM, IN_VMEM],
        scratch_shapes=[pltpu.SemaphoreType.DMA((2,))],
        compiler_params=small,
        name="stage",
    )(
        pltpu.with_memory_space_constraint(nbr.T, pltpu.HBM),
        pltpu.with_memory_space_constraint(esp_block, pltpu.HBM),
        *[near[key] for key in early],
    )
    second = pl.pallas_call(
        gather_kernel,
        out_shape=shape(len(later)),
        in_specs=[IN_VMEM] * len(later),
        out_specs=IN_VMEM,
        compiler_params=pltpu.CompilerParams(vmem_limit_bytes=2 * len(later) * rows * half * 2 + 4 * 2**20),
        name="gather",
    )(*[near[key] for key in later])
    mine = [first, second]
    pieces = mine + [lax.ppermute(piece, "gddi", xor_pairs(groups, 1)) for piece in mine]
    places = [[y * lanes + k for y, k in keys] for keys in (early, later)]
    places += [[rows_y * lanes + place for place in keys] for keys in places]

    own = jax.ShapeDtypeStruct((mono_dev, basis + 8, half), jnp.float32)
    coded = jax.ShapeDtypeStruct((mono_dev * half + round_up(2 * mono_dev, 8), half), jnp.int32)
    piece_bytes = groups * lanes * rows * half * 2

    def couple(units, name):
        return pl.pallas_call(
            functools.partial(couple_kernel, groups, lanes, mono_dev, units, places),
            out_shape=[own if k == 0 else coded for k in units],
            in_specs=[IN_SMEM] + [IN_VMEM] * (1 + len(pieces)),
            out_specs=[IN_VMEM] * len(units),
            scratch_shapes=[pltpu.VMEM((groups * lanes, rows, half), density.dtype)],
            compiler_params=pltpu.CompilerParams(
                vmem_limit_bytes=2 * (piece_bytes + esp_block.size * 2) + 8 * 2**20
            ),
            name=name,
        )(names, blocks, *pieces)

    far_units = range(lanes // 2, lanes)
    near_units = range(lanes // 2)
    far = couple(far_units, "couple_far")
    far_terms = [lax.ppermute(far[k - lanes // 2], "intra", xor_pairs(lanes, k)) for k in far_units]
    close = couple(near_units, "couple_near")
    close_terms = [lax.ppermute(close[k], "intra", xor_pairs(lanes, k)) for k in near_units[1:]]
    return pl.pallas_call(
        finish_kernel,
        out_shape=jax.ShapeDtypeStruct((mono_dev, basis, basis), jnp.float32),
        in_specs=[IN_VMEM] * (1 + lanes),
        out_specs=IN_VMEM,
        compiler_params=small,
        name="finish",
    )(h_core, close[0], *close_terms, *far_terms)


def solution(mesh):
    return jax.shard_map(
        local,
        mesh=mesh,
        in_specs=(
            P(("job", "gddi", "intra"), None, None),
            P(("job", "gddi", "intra"), None, None),
            P(("job", "gddi"), "intra", None, None),
            P("job", None),
        ),
        out_specs=P(("job", "gddi", "intra"), None, None),
        check_vma=False,
    )
```

```python
import functools

import jax
import jax.numpy as jnp
from jax import lax
from jax.experimental import pallas as pl
from jax.experimental.pallas import tpu as pltpu
from jax.sharding import PartitionSpec as P

STEPS = 32.0
TOP = 32000.0
SHRINK = 1.0 / 16.0
IN_VMEM = pl.BlockSpec(memory_space=pltpu.VMEM)
IN_SMEM = pl.BlockSpec(memory_space=pltpu.SMEM)


def xor_pairs(size, k):
    return [(i, i ^ k) for i in range(size)]


def round_up(n, to):
    return -(-n // to) * to


def transposed_dot(a, b):
    return lax.dot_general(a, b, (((1,), (1,)), ((), ())), preferred_element_type=jnp.float32)


def square_iotas(half):
    row = lax.broadcasted_iota(jnp.int32, (half, half), 0)
    col = lax.broadcasted_iota(jnp.int32, (half, half), 1)
    return row, col


def fold(first, second):
    row, col = square_iotas(first.shape[0])
    mixed = jnp.where(row <= col, first, second)
    diag = jnp.sum(jnp.where(row == col, second, 0.0), axis=0, keepdims=True)
    return mixed, diag


def unfold(mixed, diag):
    row, col = square_iotas(mixed.shape[0])
    turned = mixed.T
    first = jnp.where(row <= col, mixed, turned)
    second = jnp.where(row > col, mixed, jnp.where(row < col, turned, diag))
    return first, second


def scale_code(peak):
    wanted = jnp.log(jnp.maximum(peak * SHRINK, 2.0**-120)) * STEPS
    return jnp.floor(wanted + 1.5).astype(jnp.int32)


def encode(x, code):
    units = jnp.exp(code.astype(jnp.float32) * (-1.0 / STEPS)) * TOP
    return jnp.floor(x * SHRINK * units + 0.5).astype(jnp.int32)


def decode(q, code):
    units = jnp.exp(code.astype(jnp.float32) * (1.0 / STEPS)) * (1.0 / TOP)
    return q.astype(jnp.float32) * units * (1.0 / SHRINK)


def pack(high, low):
    return lax.shift_left(high, 16) | (low & 0xFFFF)


def unpack(word):
    return lax.shift_right_arithmetic(word, 16), lax.shift_right_arithmetic(lax.shift_left(word, 16), 16)


def peak_of(x):
    return jnp.max(jnp.abs(x), axis=0, keepdims=True)


def fold_kernel(dens_ref, out_ref, far_ref):
    mono_dev, basis, _ = dens_ref.shape
    half = basis // 2
    diags = []
    for m in range(mono_dev):
        out_ref[pl.ds(m * basis, half)] = dens_ref[m, :half, half:]
        mixed, diag = fold(
            dens_ref[m, :half, :half].astype(jnp.float32), dens_ref[m, half:, half:].astype(jnp.float32)
        )
        out_ref[pl.ds(m * basis + half, half)] = mixed.astype(out_ref.dtype)
        diags.append(diag)
    rows = out_ref.shape[0] - mono_dev * basis
    row = lax.broadcasted_iota(jnp.int32, (rows, half), 0)
    tail = jnp.zeros((rows, half), jnp.float32)
    for m in range(mono_dev):
        tail = jnp.where(row == m, diags[m], tail)
    out_ref[pl.ds(mono_dev * basis, rows)] = tail.astype(out_ref.dtype)
    far_ref[...] = jnp.zeros_like(far_ref)
    far_ref[pl.ds(0, out_ref.shape[0])] = out_ref[...]


def gate_kernel(piece_ref, *refs):
    refs[-1][...] = piece_ref[: refs[-1].shape[0]]


def gather_kernel(*refs):
    for i, piece in enumerate(refs[:-1]):
        refs[-1][i] = piece[...]


def stage_kernel(nbr_ref, esp_ref, *refs):
    nbr_out, esp_out, row_out, sems = refs[-4:]
    copies = [
        pltpu.make_async_copy(esp_ref, esp_out, sems.at[0]),
        pltpu.make_async_copy(nbr_ref, nbr_out, sems.at[1]),
    ]
    for copy in copies:
        copy.start()
    for i, piece in enumerate(refs[:-4]):
        row_out[i] = piece[...]
    for copy in copies:
        copy.wait()


def couple_kernel(groups, lanes, mono_dev, units, places, nbr_ref, esp_ref, *refs):
    pieces, outs, store = refs[: len(places)], refs[len(places) : -1], refs[-1]
    my_group = lax.axis_index("gddi")
    my_lane = lax.axis_index("intra")
    _, slot_dev, basis, _ = esp_ref.shape
    mono_grp = mono_dev * lanes
    half = basis // 2
    tail_rows = store.shape[1] - mono_dev * basis
    for piece, where in zip(pieces, places):
        for i, place in enumerate(where):
            store[place] = piece[i]

    def near_density(fragment):
        apart = (fragment // mono_grp) ^ my_group
        lane = ((fragment % mono_grp) // mono_dev) ^ my_lane
        place = ((apart & 1) * (groups // 2) + (apart >> 1)) * lanes + lane
        member = fragment % mono_dev
        start = pl.multiple_of(member * basis, basis)
        off = store[place, pl.ds(start, half)]
        mixed = store[place, pl.ds(start + half, half)].astype(jnp.float32)
        tail = store[place, pl.ds(mono_dev * basis, tail_rows)].astype(jnp.float32)
        row = lax.broadcasted_iota(jnp.int32, (tail_rows, half), 0)
        diag = jnp.sum(jnp.where(row == member, tail, 0.0), axis=0, keepdims=True)
        first, second = unfold(mixed, diag)
        top = jnp.concatenate([first.astype(off.dtype), off], axis=1)
        bottom = jnp.concatenate([off.T, second.astype(off.dtype)], axis=1)
        return jnp.concatenate([top, bottom], axis=0)

    def partial_of(fragment):
        total = None
        for s in range(slot_dev):
            name = nbr_ref[my_lane * slot_dev + s, my_group * mono_grp + fragment]
            block = esp_ref[fragment, s]
            half_term = jnp.dot(block, near_density(name), preferred_element_type=jnp.float32)
            high = half_term.astype(jnp.bfloat16)
            low = (half_term - high.astype(jnp.float32)).astype(jnp.bfloat16)
            term = transposed_dot(high, block) + transposed_dot(low, block)
            total = term if total is None else total + term
        mixed, diag = fold(total[:half, :half], total[half:, half:])
        return total[:half, half:], mixed, diag

    for (k, coded), out in zip(units, outs):
        write = write_coded if coded else write_plain
        write(out, [partial_of((my_lane ^ k) * mono_dev + m) for m in range(mono_dev)])


def write_plain(out, parts):
    half = out.shape[2]
    for m, (off, mixed, diag) in enumerate(parts):
        out[m, :half] = off
        out[m, half : 2 * half] = mixed
        out[m, 2 * half :] = jnp.broadcast_to(diag, (8, half))


def read_plain(ref, m):
    half = ref.shape[2]
    return ref[m, :half], ref[m, half : 2 * half], ref[m, 2 * half : 2 * half + 1]


def write_coded(out, parts):
    half = out.shape[1]
    tail = []
    for m, (off, mixed, diag) in enumerate(parts):
        off_code = scale_code(peak_of(off))
        mixed_code = scale_code(jnp.maximum(peak_of(mixed), jnp.abs(diag)))
        out[pl.ds(m * half, half)] = pack(encode(off, off_code), encode(mixed, mixed_code))
        tail += [pack(off_code, mixed_code), encode(diag, mixed_code)]
    row = lax.broadcasted_iota(jnp.int32, (out.shape[0] - len(parts) * half, half), 0)
    last = jnp.zeros(row.shape, jnp.int32)
    for i, values in enumerate(tail):
        last = jnp.where(row == i, values, last)
    out[pl.ds(len(parts) * half, row.shape[0])] = last


def read_coded(ref, m, mono_dev):
    half = ref.shape[1]
    tail = mono_dev * half + 2 * m
    off_code, mixed_code = unpack(ref[tail : tail + 1])
    off_q, mixed_q = unpack(ref[m * half : (m + 1) * half])
    return decode(off_q, off_code), decode(mixed_q, mixed_code), decode(ref[tail + 1 : tail + 2], mixed_code)


def summed(plain_ref, coded_refs, m):
    total = read_plain(plain_ref, m)
    for ref in coded_refs:
        total = [a + b for a, b in zip(total, read_coded(ref, m, plain_ref.shape[0]))]
    return total


def merge_kernel(plain_ref, *refs):
    write_coded(refs[-1], [summed(plain_ref, refs[:-1], m) for m in range(plain_ref.shape[0])])


def finish_kernel(core_ref, own_ref, *refs):
    parts, out_ref = refs[:-1], refs[-1]
    mono_dev, basis, _ = out_ref.shape
    half = basis // 2
    for m in range(mono_dev):
        off, mixed, diag = summed(own_ref, parts, m)
        first, second = unfold(mixed, diag)
        core = core_ref[m].astype(jnp.float32)
        out_ref[m, :half, :half] = core[:half, :half] + first
        out_ref[m, :half, half:] = core[:half, half:] + off
        out_ref[m, half:, :half] = core[half:, :half] + off.T
        out_ref[m, half:, half:] = core[half:, half:] + second


def local(density, h_core, esp_block, nbr):
    groups = lax.axis_size("gddi")
    lanes = lax.axis_size("intra")
    mono_dev, basis = density.shape[0], density.shape[1]
    half = basis // 2
    hbm = pl.BlockSpec(memory_space=pl.ANY)
    small = pltpu.CompilerParams(vmem_limit_bytes=8 * 2**20)

    rows = mono_dev * basis + round_up(mono_dev, 16)
    shard, shard_far = pl.pallas_call(
        fold_kernel,
        out_shape=[pltpu.VMEM((rows, half), density.dtype), pltpu.VMEM((rows + 16, half), density.dtype)],
        in_specs=[IN_VMEM],
        out_specs=[IN_VMEM] * 2,
        compiler_params=small,
        name="fold",
    )(density)
    def along_z(piece, bit):
        return lax.ppermute(piece, "intra", xor_pairs(lanes, bit))

    def along_y(piece, y):
        return lax.ppermute(piece, "gddi", xor_pairs(groups, 2 * y))

    rows_y = groups // 2
    top = lanes // 2
    near = {(0, 0): shard, (0, top): along_z(shard_far, top)}

    def double(start):
        bit = top // 2
        while bit:
            for k in range(start, start + top):
                if (0, k) in near and (0, k ^ bit) not in near:
                    near[0, k ^ bit] = along_z(near[0, k], bit)
            bit //= 2

    double(0)
    for y in range(1, rows_y):
        near[y, 0] = along_y(shard, y)

    def gate(piece, *after):
        return pl.pallas_call(
            gate_kernel,
            out_shape=pltpu.VMEM(shard.shape, shard.dtype),
            in_specs=[IN_VMEM] + [hbm] * len(after),
            out_specs=IN_VMEM,
            compiler_params=small,
            name="gate",
        )(piece, *after)

    others = [piece for key, piece in near.items() if key != (0, top)]
    near[0, top] = gate(gate(near[0, top]), *others)
    for y in range(1, rows_y):
        for k in range(1, top):
            near[y, k] = along_y(near[0, k], y)
    double(top)
    ahead = [near[y, k] for y in range(1, rows_y) for k in range(1, top)]
    for _ in range(3):
        ahead = [gate(ahead[0], *ahead[1:])]
    for y in range(1, rows_y):
        near[y, top] = along_y(near[0, top], y)
        for k in range(top + 1, lanes):
            near[y, k] = along_y(gate(near[0, k], *ahead), y)

    early = [(y, k) for y, k in near if (y > 0) + bin(k).count("1") <= 1]
    later = [key for key in near if key not in early]

    def shape(count):
        return pltpu.VMEM((count, rows, half), density.dtype)

    names, blocks, first = pl.pallas_call(
        stage_kernel,
        out_shape=[
            pltpu.SMEM((nbr.shape[1], nbr.shape[0]), nbr.dtype),
            pltpu.VMEM(esp_block.shape, esp_block.dtype),
            shape(len(early)),
        ],
        in_specs=[hbm, hbm] + [IN_VMEM] * len(early),
        out_specs=[IN_SMEM, IN_VMEM, IN_VMEM],
        scratch_shapes=[pltpu.SemaphoreType.DMA((2,))],
        compiler_params=small,
        name="stage",
    )(
        pltpu.with_memory_space_constraint(nbr.T, pltpu.HBM),
        pltpu.with_memory_space_constraint(esp_block, pltpu.HBM),
        *[near[key] for key in early],
    )
    second = pl.pallas_call(
        gather_kernel,
        out_shape=shape(len(later)),
        in_specs=[IN_VMEM] * len(later),
        out_specs=IN_VMEM,
        compiler_params=pltpu.CompilerParams(vmem_limit_bytes=2 * len(later) * rows * half * 2 + 4 * 2**20),
        name="gather",
    )(*[near[key] for key in later])
    mine = [first, second]
    pieces = mine + [lax.ppermute(piece, "gddi", xor_pairs(groups, 1)) for piece in mine]
    places = [[y * lanes + k for y, k in keys] for keys in (early, later)]
    places += [[rows_y * lanes + place for place in keys] for keys in places]

    plain = pltpu.VMEM((mono_dev, basis + 8, half), jnp.float32)
    coded = pltpu.VMEM((mono_dev * half + round_up(2 * mono_dev, 8), half), jnp.int32)
    piece_bytes = groups * lanes * rows * half * 2

    def couple(units, name):
        return pl.pallas_call(
            functools.partial(couple_kernel, groups, lanes, mono_dev, units, places),
            out_shape=[coded if is_coded else plain for _, is_coded in units],
            in_specs=[IN_SMEM] + [IN_VMEM] * (1 + len(pieces)),
            out_specs=[IN_VMEM] * len(units),
            scratch_shapes=[pltpu.VMEM((groups * lanes, rows, half), density.dtype)],
            compiler_params=pltpu.CompilerParams(
                vmem_limit_bytes=2 * (piece_bytes + esp_block.size * 2) + 8 * 2**20
            ),
            name=name,
        )(names, blocks, *pieces)

    steps = range(1, top)
    relayed = couple([(top ^ k, True) for k in steps], "couple_relay") if top > 1 else []
    relayed = [along_z(unit, k) for k, unit in zip(steps, relayed)]
    own, across, *close = couple([(0, False), (top, False)] + [(k, True) for k in steps], "couple")
    close = [along_z(unit, k) for k, unit in zip(steps, close)]
    across = pl.pallas_call(
        merge_kernel,
        out_shape=coded,
        in_specs=[IN_VMEM] * (1 + len(relayed)),
        out_specs=IN_VMEM,
        compiler_params=small,
        name="merge",
    )(across, *relayed)
    return pl.pallas_call(
        finish_kernel,
        out_shape=jax.ShapeDtypeStruct((mono_dev, basis, basis), jnp.float32),
        in_specs=[IN_VMEM] * (3 + len(close)),
        out_specs=IN_VMEM,
        compiler_params=small,
        name="finish",
    )(h_core, own, *close, along_z(across, top))


def solution(mesh):
    return jax.shard_map(
        local,
        mesh=mesh,
        in_specs=(
            P(("job", "gddi", "intra"), None, None),
            P(("job", "gddi", "intra"), None, None),
            P(("job", "gddi"), "intra", None, None),
            P("job", None),
        ),
        out_specs=P(("job", "gddi", "intra"), None, None),
        check_vma=False,
    )
```

```python
import functools

import jax
import jax.numpy as jnp
from jax import lax
from jax.experimental import pallas as pl
from jax.experimental.pallas import tpu as pltpu
from jax.sharding import PartitionSpec as P

STEPS = 32.0
TOP = 32000.0
SHRINK = 1.0 / 16.0
IN_VMEM = pl.BlockSpec(memory_space=pltpu.VMEM)
IN_SMEM = pl.BlockSpec(memory_space=pltpu.SMEM)


def xor_pairs(size, k):
    return [(i, i ^ k) for i in range(size)]


def round_up(n, to):
    return -(-n // to) * to


def transposed_dot(a, b):
    return lax.dot_general(a, b, (((1,), (1,)), ((), ())), preferred_element_type=jnp.float32)


def square_iotas(half):
    row = lax.broadcasted_iota(jnp.int32, (half, half), 0)
    col = lax.broadcasted_iota(jnp.int32, (half, half), 1)
    return row, col


def fold(first, second):
    row, col = square_iotas(first.shape[0])
    mixed = jnp.where(row <= col, first, second)
    diag = jnp.sum(jnp.where(row == col, second, 0.0), axis=0, keepdims=True)
    return mixed, diag


def unfold(mixed, diag):
    row, col = square_iotas(mixed.shape[0])
    turned = mixed.T
    first = jnp.where(row <= col, mixed, turned)
    second = jnp.where(row > col, mixed, jnp.where(row < col, turned, diag))
    return first, second


def scale_code(peak):
    wanted = jnp.log(jnp.maximum(peak * SHRINK, 2.0**-120)) * STEPS
    return jnp.floor(wanted + 1.5).astype(jnp.int32)


def encode(x, code):
    units = jnp.exp(code.astype(jnp.float32) * (-1.0 / STEPS)) * TOP
    return jnp.floor(x * SHRINK * units + 0.5).astype(jnp.int32)


def decode(q, code):
    units = jnp.exp(code.astype(jnp.float32) * (1.0 / STEPS)) * (1.0 / TOP)
    return q.astype(jnp.float32) * units * (1.0 / SHRINK)


def pack(high, low):
    return lax.shift_left(high, 16) | (low & 0xFFFF)


def unpack(word):
    return lax.shift_right_arithmetic(word, 16), lax.shift_right_arithmetic(lax.shift_left(word, 16), 16)


def peak_of(x):
    return jnp.max(jnp.abs(x), axis=0, keepdims=True)


def fold_kernel(dens_ref, out_ref):
    mono_dev, basis, _ = dens_ref.shape
    half = basis // 2
    diags = []
    for m in range(mono_dev):
        out_ref[pl.ds(m * basis, half)] = dens_ref[m, :half, half:]
        mixed, diag = fold(
            dens_ref[m, :half, :half].astype(jnp.float32), dens_ref[m, half:, half:].astype(jnp.float32)
        )
        out_ref[pl.ds(m * basis + half, half)] = mixed.astype(out_ref.dtype)
        diags.append(diag)
    rows = out_ref.shape[0] - mono_dev * basis
    row = lax.broadcasted_iota(jnp.int32, (rows, half), 0)
    tail = jnp.zeros((rows, half), jnp.float32)
    for m in range(mono_dev):
        tail = jnp.where(row == m, diags[m], tail)
    out_ref[pl.ds(mono_dev * basis, rows)] = tail.astype(out_ref.dtype)


def gate_kernel(piece_ref, *refs):
    out_ref = refs[-1]
    out_ref[pl.ds(0, piece_ref.shape[0])] = piece_ref[...]
    extra = out_ref.shape[0] - piece_ref.shape[0]
    if extra:
        out_ref[pl.ds(piece_ref.shape[0], extra)] = jnp.zeros((extra, out_ref.shape[1]), out_ref.dtype)


def stage_kernel(nbr_ref, esp_ref, piece_ref, *refs):
    nbr_out, esp_out, piece_out, sems = refs[-4:]
    copies = [
        pltpu.make_async_copy(esp_ref, esp_out, sems.at[0]),
        pltpu.make_async_copy(nbr_ref, nbr_out, sems.at[1]),
    ]
    for copy in copies:
        copy.start()
    piece_out[...] = piece_ref[...]
    for copy in copies:
        copy.wait()


def couple_kernel(groups, lanes, mono_dev, units, nbr_ref, esp_ref, *refs):
    n_pieces = groups * lanes
    pieces, outs, store = refs[:n_pieces], refs[n_pieces:-1], refs[-1]
    my_group = lax.axis_index("gddi")
    my_lane = lax.axis_index("intra")
    _, slot_dev, basis, _ = esp_ref.shape
    mono_grp = mono_dev * lanes
    half = basis // 2
    tail_rows = store.shape[1] - mono_dev * basis
    for i, piece in enumerate(pieces):
        store[i] = piece[pl.ds(0, store.shape[1])]

    def near_density(fragment):
        apart = (fragment // mono_grp) ^ my_group
        lane = ((fragment % mono_grp) // mono_dev) ^ my_lane
        place = ((apart & 1) * (groups // 2) + (apart >> 1)) * lanes + lane
        member = fragment % mono_dev
        start = pl.multiple_of(member * basis, basis)
        off = store[place, pl.ds(start, half)]
        mixed = store[place, pl.ds(start + half, half)].astype(jnp.float32)
        tail = store[place, pl.ds(mono_dev * basis, tail_rows)].astype(jnp.float32)
        row = lax.broadcasted_iota(jnp.int32, (tail_rows, half), 0)
        diag = jnp.sum(jnp.where(row == member, tail, 0.0), axis=0, keepdims=True)
        first, second = unfold(mixed, diag)
        top = jnp.concatenate([first.astype(off.dtype), off], axis=1)
        bottom = jnp.concatenate([off.T, second.astype(off.dtype)], axis=1)
        return jnp.concatenate([top, bottom], axis=0)

    def partial_of(fragment):
        total = None
        for s in range(slot_dev):
            name = nbr_ref[my_lane * slot_dev + s, my_group * mono_grp + fragment]
            block = esp_ref[fragment, s]
            half_term = jnp.dot(block, near_density(name), preferred_element_type=jnp.float32)
            high = half_term.astype(jnp.bfloat16)
            low = (half_term - high.astype(jnp.float32)).astype(jnp.bfloat16)
            term = transposed_dot(high, block) + transposed_dot(low, block)
            total = term if total is None else total + term
        mixed, diag = fold(total[:half, :half], total[half:, half:])
        return total[:half, half:], mixed, diag

    for (k, coded), out in zip(units, outs):
        write = write_coded if coded else write_plain
        write(out, [partial_of((my_lane ^ k) * mono_dev + m) for m in range(mono_dev)])


def write_plain(out, parts):
    half = out.shape[2]
    for m, (off, mixed, diag) in enumerate(parts):
        out[m, :half] = off
        out[m, half : 2 * half] = mixed
        out[m, 2 * half :] = jnp.broadcast_to(diag, (8, half))


def read_plain(ref, m):
    half = ref.shape[2]
    return ref[m, :half], ref[m, half : 2 * half], ref[m, 2 * half : 2 * half + 1]


def write_coded(out, parts):
    half = out.shape[1]
    tail = []
    for m, (off, mixed, diag) in enumerate(parts):
        off_code = scale_code(peak_of(off))
        mixed_code = scale_code(jnp.maximum(peak_of(mixed), jnp.abs(diag)))
        out[pl.ds(m * half, half)] = pack(encode(off, off_code), encode(mixed, mixed_code))
        tail += [pack(off_code, mixed_code), encode(diag, mixed_code)]
    row = lax.broadcasted_iota(jnp.int32, (out.shape[0] - len(parts) * half, half), 0)
    last = jnp.zeros(row.shape, jnp.int32)
    for i, values in enumerate(tail):
        last = jnp.where(row == i, values, last)
    out[pl.ds(len(parts) * half, row.shape[0])] = last


def read_coded(ref, m, mono_dev):
    half = ref.shape[1]
    tail = mono_dev * half + 2 * m
    off_code, mixed_code = unpack(ref[tail : tail + 1])
    off_q, mixed_q = unpack(ref[m * half : (m + 1) * half])
    return decode(off_q, off_code), decode(mixed_q, mixed_code), decode(ref[tail + 1 : tail + 2], mixed_code)


def summed(plain_ref, coded_refs, m):
    total = read_plain(plain_ref, m)
    for ref in coded_refs:
        total = [a + b for a, b in zip(total, read_coded(ref, m, plain_ref.shape[0]))]
    return total


def merge_kernel(plain_ref, *refs):
    write_coded(refs[-1], [summed(plain_ref, refs[:-1], m) for m in range(plain_ref.shape[0])])


def finish_kernel(core_ref, own_ref, *refs):
    parts, out_ref = refs[:-1], refs[-1]
    mono_dev, basis, _ = out_ref.shape
    half = basis // 2
    for m in range(mono_dev):
        off, mixed, diag = summed(own_ref, parts, m)
        first, second = unfold(mixed, diag)
        core = core_ref[m].astype(jnp.float32)
        out_ref[m, :half, :half] = core[:half, :half] + first
        out_ref[m, :half, half:] = core[:half, half:] + off
        out_ref[m, half:, :half] = core[half:, :half] + off.T
        out_ref[m, half:, half:] = core[half:, half:] + second


def local(density, h_core, esp_block, nbr):
    groups = lax.axis_size("gddi")
    lanes = lax.axis_size("intra")
    mono_dev, basis = density.shape[0], density.shape[1]
    half = basis // 2
    hbm = pl.BlockSpec(memory_space=pl.ANY)
    small = pltpu.CompilerParams(vmem_limit_bytes=8 * 2**20)

    rows = mono_dev * basis + round_up(mono_dev, 16)
    shard = pl.pallas_call(
        fold_kernel,
        out_shape=pltpu.VMEM((rows, half), density.dtype),
        in_specs=[IN_VMEM],
        out_specs=IN_VMEM,
        compiler_params=small,
        name="fold",
    )(density)
    def along_z(piece, bit):
        return lax.ppermute(piece, "intra", xor_pairs(lanes, bit))

    def along_y(piece, y):
        return lax.ppermute(piece, "gddi", xor_pairs(groups, 2 * y))

    rows_y = groups // 2
    top = lanes // 2
    near = {(0, 0): shard, (0, top): along_z(shard, top)}

    def double(start):
        bit = top // 2
        while bit:
            for k in range(start, start + top):
                if (0, k) in near and (0, k ^ bit) not in near:
                    near[0, k ^ bit] = along_z(near[0, k], bit)
            bit //= 2

    double(0)
    for y in range(1, rows_y):
        near[y, 0] = along_y(shard, y)

    def gate(piece, *after, extra=0):
        return pl.pallas_call(
            gate_kernel,
            out_shape=pltpu.VMEM((piece.shape[0] + extra,) + piece.shape[1:], piece.dtype),
            in_specs=[IN_VMEM] + [hbm] * len(after),
            out_specs=IN_VMEM,
            compiler_params=small,
            name="gate",
        )(piece, *after)

    others = [piece for key, piece in near.items() if key != (0, top)]
    near[0, top] = gate(gate(near[0, top]), *others)
    for y in range(1, rows_y):
        for k in range(1, top):
            near[y, k] = along_y(near[0, k], y)
    double(top)
    ahead = [near[y, k] for y in range(1, rows_y) for k in range(1, top)]
    for _ in range(3):
        ahead = [gate(ahead[0], *ahead[1:])]
    for y in range(1, rows_y):
        near[y, top] = along_y(near[0, top], y)
        near[y, top] = gate(near[y, top])
        for k in range(top + 1, lanes):
            near[y, k] = along_y(gate(near[0, k], *ahead), y)

    names, blocks, near[rows_y - 1, 0] = pl.pallas_call(
        stage_kernel,
        out_shape=[
            pltpu.SMEM((nbr.shape[1], nbr.shape[0]), nbr.dtype),
            pltpu.VMEM(esp_block.shape, esp_block.dtype),
            pltpu.VMEM(shard.shape, shard.dtype),
        ],
        in_specs=[hbm, hbm, IN_VMEM, hbm],
        out_specs=[IN_SMEM, IN_VMEM, IN_VMEM],
        scratch_shapes=[pltpu.SemaphoreType.DMA((2,))],
        compiler_params=small,
        name="stage",
    )(
        pltpu.with_memory_space_constraint(nbr.T, pltpu.HBM),
        pltpu.with_memory_space_constraint(esp_block, pltpu.HBM),
        near[rows_y - 1, 0],
        near[0, lanes - 1],
    )
    mine = [near[y, k] for y in range(rows_y) for k in range(lanes)]
    pieces = mine + [lax.ppermute(piece, "gddi", xor_pairs(groups, 1)) for piece in mine]

    plain = pltpu.VMEM((mono_dev, basis + 8, half), jnp.float32)
    coded = pltpu.VMEM((mono_dev * half + round_up(2 * mono_dev, 8), half), jnp.int32)
    piece_bytes = groups * lanes * rows * half * 2

    def couple(units, name):
        return pl.pallas_call(
            functools.partial(couple_kernel, groups, lanes, mono_dev, units),
            out_shape=[coded if is_coded else plain for _, is_coded in units],
            in_specs=[IN_SMEM] + [IN_VMEM] * (1 + len(pieces)),
            out_specs=[IN_VMEM] * len(units),
            scratch_shapes=[pltpu.VMEM((groups * lanes, rows, half), density.dtype)],
            compiler_params=pltpu.CompilerParams(
                vmem_limit_bytes=2 * (piece_bytes + esp_block.size * 2) + 8 * 2**20
            ),
            name=name,
        )(names, blocks, *pieces)

    steps = range(1, top)
    relayed = couple([(top ^ k, True) for k in steps], "couple_relay") if top > 1 else []
    relayed = [along_z(unit, k) for k, unit in zip(steps, relayed)]
    own, across, *close = couple([(0, False), (top, False)] + [(k, True) for k in steps], "couple")
    across = pl.pallas_call(
        merge_kernel,
        out_shape=pltpu.VMEM((coded.shape[0] + 8, half), jnp.int32),
        in_specs=[IN_VMEM] * (1 + len(relayed)),
        out_specs=IN_VMEM,
        compiler_params=small,
        name="merge",
    )(across, *relayed)
    close = [along_z(gate(unit, across), k) for k, unit in zip(steps, close)]
    return pl.pallas_call(
        finish_kernel,
        out_shape=jax.ShapeDtypeStruct((mono_dev, basis, basis), jnp.float32),
        in_specs=[IN_VMEM] * (3 + len(close)),
        out_specs=IN_VMEM,
        compiler_params=small,
        name="finish",
    )(h_core, own, *close, along_z(across, top))


def solution(mesh):
    return jax.shard_map(
        local,
        mesh=mesh,
        in_specs=(
            P(("job", "gddi", "intra"), None, None),
            P(("job", "gddi", "intra"), None, None),
            P(("job", "gddi"), "intra", None, None),
            P("job", None),
        ),
        out_specs=P(("job", "gddi", "intra"), None, None),
        check_vma=False,
    )
```

```python
import functools

import jax
import jax.numpy as jnp
from jax import lax
from jax.experimental import pallas as pl
from jax.experimental.pallas import tpu as pltpu
from jax.sharding import PartitionSpec as P

STEPS = 32.0
TOP = 32000.0
SHRINK = 1.0 / 16.0
IN_VMEM = pl.BlockSpec(memory_space=pltpu.VMEM)
IN_SMEM = pl.BlockSpec(memory_space=pltpu.SMEM)


def xor_pairs(size, k):
    return [(i, i ^ k) for i in range(size)]


def round_up(n, to):
    return -(-n // to) * to


def transposed_dot(a, b):
    return lax.dot_general(a, b, (((1,), (1,)), ((), ())), preferred_element_type=jnp.float32)


def square_iotas(half):
    row = lax.broadcasted_iota(jnp.int32, (half, half), 0)
    col = lax.broadcasted_iota(jnp.int32, (half, half), 1)
    return row, col


def fold(first, second):
    row, col = square_iotas(first.shape[0])
    mixed = jnp.where(row <= col, first, second)
    diag = jnp.sum(jnp.where(row == col, second, 0.0), axis=0, keepdims=True)
    return mixed, diag


def unfold(mixed, diag):
    row, col = square_iotas(mixed.shape[0])
    turned = mixed.T
    first = jnp.where(row <= col, mixed, turned)
    second = jnp.where(row > col, mixed, jnp.where(row < col, turned, diag))
    return first, second


def scale_code(peak):
    wanted = jnp.log(jnp.maximum(peak * SHRINK, 2.0**-120)) * STEPS
    return jnp.floor(wanted + 1.5).astype(jnp.int32)


def encode(x, code):
    units = jnp.exp(code.astype(jnp.float32) * (-1.0 / STEPS)) * TOP
    return jnp.floor(x * SHRINK * units + 0.5).astype(jnp.int32)


def decode(q, code):
    units = jnp.exp(code.astype(jnp.float32) * (1.0 / STEPS)) * (1.0 / TOP)
    return q.astype(jnp.float32) * units * (1.0 / SHRINK)


def pack(high, low):
    return lax.shift_left(high, 16) | (low & 0xFFFF)


def unpack(word):
    return lax.shift_right_arithmetic(word, 16), lax.shift_right_arithmetic(lax.shift_left(word, 16), 16)


def peak_of(x):
    return jnp.max(jnp.abs(x), axis=0, keepdims=True)


def fold_kernel(dens_ref, out_ref):
    mono_dev, basis, _ = dens_ref.shape
    half = basis // 2
    diags = []
    for m in range(mono_dev):
        out_ref[pl.ds(m * basis, half)] = dens_ref[m, :half, half:]
        mixed, diag = fold(
            dens_ref[m, :half, :half].astype(jnp.float32), dens_ref[m, half:, half:].astype(jnp.float32)
        )
        out_ref[pl.ds(m * basis + half, half)] = mixed.astype(out_ref.dtype)
        diags.append(diag)
    rows = out_ref.shape[0] - mono_dev * basis
    row = lax.broadcasted_iota(jnp.int32, (rows, half), 0)
    tail = jnp.zeros((rows, half), jnp.float32)
    for m in range(mono_dev):
        tail = jnp.where(row == m, diags[m], tail)
    out_ref[pl.ds(mono_dev * basis, rows)] = tail.astype(out_ref.dtype)


def gate_kernel(piece_ref, *refs):
    refs[-1][...] = piece_ref[...]


def stage_kernel(nbr_ref, esp_ref, piece_ref, *refs):
    nbr_out, esp_out, piece_out, sems = refs[-4:]
    copies = [
        pltpu.make_async_copy(esp_ref, esp_out, sems.at[0]),
        pltpu.make_async_copy(nbr_ref, nbr_out, sems.at[1]),
    ]
    for copy in copies:
        copy.start()
    piece_out[...] = piece_ref[...]
    for copy in copies:
        copy.wait()


def couple_kernel(groups, lanes, mono_dev, units, nbr_ref, esp_ref, *refs):
    outs = refs[len(refs) - len(units) :]
    if len(refs) > len(units) + 1:
        pieces, store = refs[: -1 - len(units)], refs[-1 - len(units)]
        for i, piece in enumerate(pieces):
            store[i] = piece[...]
    else:
        store = refs[0]
    my_group = lax.axis_index("gddi")
    my_lane = lax.axis_index("intra")
    _, slot_dev, basis, _ = esp_ref.shape
    mono_grp = mono_dev * lanes
    half = basis // 2
    tail_rows = store.shape[1] - mono_dev * basis

    def near_density(fragment):
        apart = (fragment // mono_grp) ^ my_group
        lane = ((fragment % mono_grp) // mono_dev) ^ my_lane
        place = ((apart & 1) * (groups // 2) + (apart >> 1)) * lanes + lane
        member = fragment % mono_dev
        start = pl.multiple_of(member * basis, basis)
        off = store[place, pl.ds(start, half)]
        mixed = store[place, pl.ds(start + half, half)].astype(jnp.float32)
        tail = store[place, pl.ds(mono_dev * basis, tail_rows)].astype(jnp.float32)
        row = lax.broadcasted_iota(jnp.int32, (tail_rows, half), 0)
        diag = jnp.sum(jnp.where(row == member, tail, 0.0), axis=0, keepdims=True)
        first, second = unfold(mixed, diag)
        top = jnp.concatenate([first.astype(off.dtype), off], axis=1)
        bottom = jnp.concatenate([off.T, second.astype(off.dtype)], axis=1)
        return jnp.concatenate([top, bottom], axis=0)

    def partial_of(fragment):
        total = None
        for s in range(slot_dev):
            name = nbr_ref[my_lane * slot_dev + s, my_group * mono_grp + fragment]
            block = esp_ref[fragment, s]
            half_term = jnp.dot(block, near_density(name), preferred_element_type=jnp.float32)
            high = half_term.astype(jnp.bfloat16)
            low = (half_term - high.astype(jnp.float32)).astype(jnp.bfloat16)
            term = transposed_dot(high, block) + transposed_dot(low, block)
            total = term if total is None else total + term
        mixed, diag = fold(total[:half, :half], total[half:, half:])
        return total[:half, half:], mixed, diag

    for (k, coded), out in zip(units, outs):
        write = write_coded if coded else write_plain
        write(out, [partial_of((my_lane ^ k) * mono_dev + m) for m in range(mono_dev)])


def write_plain(out, parts):
    half = out.shape[2]
    for m, (off, mixed, diag) in enumerate(parts):
        out[m, :half] = off
        out[m, half : 2 * half] = mixed
        out[m, 2 * half :] = jnp.broadcast_to(diag, (8, half))


def read_plain(ref, m):
    half = ref.shape[2]
    return ref[m, :half], ref[m, half : 2 * half], ref[m, 2 * half : 2 * half + 1]


def write_coded(out, parts):
    half = out.shape[1]
    tail = []
    for m, (off, mixed, diag) in enumerate(parts):
        off_code = scale_code(peak_of(off))
        mixed_code = scale_code(jnp.maximum(peak_of(mixed), jnp.abs(diag)))
        out[pl.ds(m * half, half)] = pack(encode(off, off_code), encode(mixed, mixed_code))
        tail += [pack(off_code, mixed_code), encode(diag, mixed_code)]
    row = lax.broadcasted_iota(jnp.int32, (out.shape[0] - len(parts) * half, half), 0)
    last = jnp.zeros(row.shape, jnp.int32)
    for i, values in enumerate(tail):
        last = jnp.where(row == i, values, last)
    out[pl.ds(len(parts) * half, row.shape[0])] = last


def read_coded(ref, m, mono_dev):
    half = ref.shape[1]
    tail = mono_dev * half + 2 * m
    off_code, mixed_code = unpack(ref[tail : tail + 1])
    off_q, mixed_q = unpack(ref[m * half : (m + 1) * half])
    return decode(off_q, off_code), decode(mixed_q, mixed_code), decode(ref[tail + 1 : tail + 2], mixed_code)


def summed(plain_ref, coded_refs, m):
    total = read_plain(plain_ref, m)
    for ref in coded_refs:
        total = [a + b for a, b in zip(total, read_coded(ref, m, plain_ref.shape[0]))]
    return total


def merge_kernel(plain_ref, *refs):
    write_coded(refs[-1], [summed(plain_ref, refs[:-1], m) for m in range(plain_ref.shape[0])])


def finish_kernel(core_ref, own_ref, *refs):
    parts, out_ref = refs[:-1], refs[-1]
    mono_dev, basis, _ = out_ref.shape
    half = basis // 2
    for m in range(mono_dev):
        off, mixed, diag = summed(own_ref, parts, m)
        first, second = unfold(mixed, diag)
        core = core_ref[m].astype(jnp.float32)
        out_ref[m, :half, :half] = core[:half, :half] + first
        out_ref[m, :half, half:] = core[:half, half:] + off
        out_ref[m, half:, :half] = core[half:, :half] + off.T
        out_ref[m, half:, half:] = core[half:, half:] + second


def local(density, h_core, esp_block, nbr):
    groups = lax.axis_size("gddi")
    lanes = lax.axis_size("intra")
    mono_dev, basis = density.shape[0], density.shape[1]
    half = basis // 2
    hbm = pl.BlockSpec(memory_space=pl.ANY)
    small = pltpu.CompilerParams(vmem_limit_bytes=8 * 2**20)

    rows = mono_dev * basis + round_up(mono_dev, 16)
    shard = pl.pallas_call(
        fold_kernel,
        out_shape=pltpu.VMEM((rows, half), density.dtype),
        in_specs=[IN_VMEM],
        out_specs=IN_VMEM,
        compiler_params=small,
        name="fold",
    )(density)
    def along_z(piece, bit):
        return lax.ppermute(piece, "intra", xor_pairs(lanes, bit))

    def along_y(piece, y):
        return lax.ppermute(piece, "gddi", xor_pairs(groups, 2 * y))

    rows_y = groups // 2
    top = lanes // 2
    near = {(0, 0): shard, (0, top): along_z(shard, top)}

    def double(start):
        bit = top // 2
        while bit:
            for k in range(start, start + top):
                if (0, k) in near and (0, k ^ bit) not in near:
                    near[0, k ^ bit] = along_z(near[0, k], bit)
            bit //= 2

    double(0)
    for y in range(1, rows_y):
        near[y, 0] = along_y(shard, y)

    def gate(piece, *after):
        return pl.pallas_call(
            gate_kernel,
            out_shape=pltpu.VMEM(piece.shape, piece.dtype),
            in_specs=[IN_VMEM] + [hbm] * len(after),
            out_specs=IN_VMEM,
            compiler_params=small,
            name="gate",
        )(piece, *after)

    others = [piece for key, piece in near.items() if key != (0, top)]
    near[0, top] = gate(gate(near[0, top]), *others)
    for y in range(1, rows_y):
        for k in range(1, top):
            near[y, k] = along_y(near[0, k], y)
    double(top)
    ahead = [near[y, k] for y in range(1, rows_y) for k in range(1, top)]
    for _ in range(3):
        ahead = [gate(ahead[0], *ahead[1:])]
    for y in range(1, rows_y):
        near[y, top] = along_y(near[0, top], y)
        near[y, top] = gate(near[y, top])
        for k in range(top + 1, lanes):
            near[y, k] = along_y(gate(near[0, k], *ahead), y)

    names, blocks, near[rows_y - 1, 0] = pl.pallas_call(
        stage_kernel,
        out_shape=[
            pltpu.SMEM((nbr.shape[1], nbr.shape[0]), nbr.dtype),
            pltpu.VMEM(esp_block.shape, esp_block.dtype),
            pltpu.VMEM(shard.shape, shard.dtype),
        ],
        in_specs=[hbm, hbm, IN_VMEM, hbm],
        out_specs=[IN_SMEM, IN_VMEM, IN_VMEM],
        scratch_shapes=[pltpu.SemaphoreType.DMA((2,))],
        compiler_params=small,
        name="stage",
    )(
        pltpu.with_memory_space_constraint(nbr.T, pltpu.HBM),
        pltpu.with_memory_space_constraint(esp_block, pltpu.HBM),
        near[rows_y - 1, 0],
        near[0, lanes - 1],
    )
    mine = [near[y, k] for y in range(rows_y) for k in range(lanes)]
    pieces = mine + [lax.ppermute(piece, "gddi", xor_pairs(groups, 1)) for piece in mine]

    plain = pltpu.VMEM((mono_dev, basis + 8, half), jnp.float32)
    coded = pltpu.VMEM((mono_dev * half + round_up(2 * mono_dev, 8), half), jnp.int32)
    piece_bytes = groups * lanes * rows * half * 2

    keep = pltpu.VMEM if piece_bytes <= 4 * 2**20 else jax.ShapeDtypeStruct
    store = keep((groups * lanes, rows, half), density.dtype)

    def couple(units, name, pieces, fill=False):
        return pl.pallas_call(
            functools.partial(couple_kernel, groups, lanes, mono_dev, units),
            out_shape=[store] * fill + [coded if is_coded else plain for _, is_coded in units],
            in_specs=[IN_SMEM] + [IN_VMEM] * (1 + len(pieces)),
            out_specs=[IN_VMEM] * (fill + len(units)),
            compiler_params=pltpu.CompilerParams(
                vmem_limit_bytes=2 * (piece_bytes + esp_block.size * 2) + 8 * 2**20
            ),
            name=name,
        )(names, blocks, *pieces)

    steps = range(1, top)
    filled, *relayed = couple([(top ^ k, True) for k in steps], "couple_relay", pieces, fill=True)
    relayed = [along_z(unit, k) for k, unit in zip(steps, relayed)]
    close = couple([(k, True) for k in steps], "couple_near", [filled])
    close = [along_z(unit, k) for k, unit in zip(steps, close)]
    for _ in range(5):
        close = [gate(unit) for unit in close]
    across, own = couple([(top, False), (0, False)], "couple_far", [filled])
    across = pl.pallas_call(
        merge_kernel,
        out_shape=coded,
        in_specs=[IN_VMEM] * (1 + len(relayed)),
        out_specs=IN_VMEM,
        compiler_params=small,
        name="merge",
    )(across, *relayed)
    return pl.pallas_call(
        finish_kernel,
        out_shape=jax.ShapeDtypeStruct((mono_dev, basis, basis), jnp.float32),
        in_specs=[IN_VMEM] * (3 + len(close)),
        out_specs=IN_VMEM,
        compiler_params=small,
        name="finish",
    )(h_core, own, *close, along_z(across, top))


def solution(mesh):
    return jax.shard_map(
        local,
        mesh=mesh,
        in_specs=(
            P(("job", "gddi", "intra"), None, None),
            P(("job", "gddi", "intra"), None, None),
            P(("job", "gddi"), "intra", None, None),
            P("job", None),
        ),
        out_specs=P(("job", "gddi", "intra"), None, None),
        check_vma=False,
    )
```

```python
import functools

import jax
import jax.numpy as jnp
from jax import lax
from jax.experimental import pallas as pl
from jax.experimental.pallas import tpu as pltpu
from jax.sharding import PartitionSpec as P

STEPS = 32.0
TOP = 32000.0
SHRINK = 1.0 / 16.0
IN_VMEM = pl.BlockSpec(memory_space=pltpu.VMEM)
IN_SMEM = pl.BlockSpec(memory_space=pltpu.SMEM)


def xor_pairs(size, k):
    return [(i, i ^ k) for i in range(size)]


def round_up(n, to):
    return -(-n // to) * to


def transposed_dot(a, b):
    return lax.dot_general(a, b, (((1,), (1,)), ((), ())), preferred_element_type=jnp.float32)


def square_iotas(half):
    row = lax.broadcasted_iota(jnp.int32, (half, half), 0)
    col = lax.broadcasted_iota(jnp.int32, (half, half), 1)
    return row, col


def fold(first, second):
    row, col = square_iotas(first.shape[0])
    mixed = jnp.where(row <= col, first, second)
    diag = jnp.sum(jnp.where(row == col, second, 0.0), axis=0, keepdims=True)
    return mixed, diag


def unfold(mixed, diag):
    row, col = square_iotas(mixed.shape[0])
    turned = mixed.T
    first = jnp.where(row <= col, mixed, turned)
    second = jnp.where(row > col, mixed, jnp.where(row < col, turned, diag))
    return first, second


def scale_code(peak):
    wanted = jnp.log(jnp.maximum(peak * SHRINK, 2.0**-120)) * STEPS
    return jnp.floor(wanted + 1.5).astype(jnp.int32)


def encode(x, code):
    units = jnp.exp(code.astype(jnp.float32) * (-1.0 / STEPS)) * TOP
    return jnp.floor(x * SHRINK * units + 0.5).astype(jnp.int32)


def decode(q, code):
    units = jnp.exp(code.astype(jnp.float32) * (1.0 / STEPS)) * (1.0 / TOP)
    return q.astype(jnp.float32) * units * (1.0 / SHRINK)


def pack(high, low):
    return lax.shift_left(high, 16) | (low & 0xFFFF)


def unpack(word):
    return lax.shift_right_arithmetic(word, 16), lax.shift_right_arithmetic(lax.shift_left(word, 16), 16)


def peak_of(x):
    return jnp.max(jnp.abs(x), axis=0, keepdims=True)


def fold_kernel(dens_ref, out_ref):
    mono_dev, basis, _ = dens_ref.shape
    half = basis // 2
    diags = []
    for m in range(mono_dev):
        out_ref[pl.ds(m * basis, half)] = dens_ref[m, :half, half:]
        mixed, diag = fold(
            dens_ref[m, :half, :half].astype(jnp.float32), dens_ref[m, half:, half:].astype(jnp.float32)
        )
        out_ref[pl.ds(m * basis + half, half)] = mixed.astype(out_ref.dtype)
        diags.append(diag)
    rows = out_ref.shape[0] - mono_dev * basis
    row = lax.broadcasted_iota(jnp.int32, (rows, half), 0)
    tail = jnp.zeros((rows, half), jnp.float32)
    for m in range(mono_dev):
        tail = jnp.where(row == m, diags[m], tail)
    out_ref[pl.ds(mono_dev * basis, rows)] = tail.astype(out_ref.dtype)


def gate_kernel(piece_ref, *refs):
    refs[-1][...] = piece_ref[...]


def gather_kernel(*refs):
    for i, piece in enumerate(refs[:-1]):
        refs[-1][i] = piece[...]


def stage_kernel(nbr_ref, esp_ref, piece_ref, nbr_out, esp_out, piece_out, sems):
    copies = [
        pltpu.make_async_copy(esp_ref, esp_out, sems.at[0]),
        pltpu.make_async_copy(nbr_ref, nbr_out, sems.at[1]),
    ]
    for copy in copies:
        copy.start()
    piece_out[...] = piece_ref[...]
    for copy in copies:
        copy.wait()


def couple_kernel(groups, lanes, mono_dev, units, places, nbr_ref, esp_ref, *refs):
    outs = refs[len(refs) - len(units) :]
    if len(refs) > len(units) + 1:
        pieces, store = refs[: -1 - len(units)], refs[-1 - len(units)]
        at = 0
        for piece in pieces:
            for part in [piece] if len(piece.shape) == 2 else [piece.at[i] for i in range(piece.shape[0])]:
                store[places[at]] = part[...]
                at += 1
    else:
        store = refs[0]
    my_group = lax.axis_index("gddi")
    my_lane = lax.axis_index("intra")
    _, slot_dev, basis, _ = esp_ref.shape
    mono_grp = mono_dev * lanes
    half = basis // 2
    tail_rows = store.shape[1] - mono_dev * basis

    def near_density(fragment):
        apart = (fragment // mono_grp) ^ my_group
        lane = ((fragment % mono_grp) // mono_dev) ^ my_lane
        place = ((apart & 1) * (groups // 2) + (apart >> 1)) * lanes + lane
        member = fragment % mono_dev
        start = pl.multiple_of(member * basis, basis)
        off = store[place, pl.ds(start, half)]
        mixed = store[place, pl.ds(start + half, half)].astype(jnp.float32)
        tail = store[place, pl.ds(mono_dev * basis, tail_rows)].astype(jnp.float32)
        row = lax.broadcasted_iota(jnp.int32, (tail_rows, half), 0)
        diag = jnp.sum(jnp.where(row == member, tail, 0.0), axis=0, keepdims=True)
        first, second = unfold(mixed, diag)
        top = jnp.concatenate([first.astype(off.dtype), off], axis=1)
        bottom = jnp.concatenate([off.T, second.astype(off.dtype)], axis=1)
        return jnp.concatenate([top, bottom], axis=0)

    def partial_of(fragment):
        total = None
        for s in range(slot_dev):
            name = nbr_ref[my_lane * slot_dev + s, my_group * mono_grp + fragment]
            block = esp_ref[fragment, s]
            half_term = jnp.dot(block, near_density(name), preferred_element_type=jnp.float32)
            high = half_term.astype(jnp.bfloat16)
            low = (half_term - high.astype(jnp.float32)).astype(jnp.bfloat16)
            term = transposed_dot(high, block) + transposed_dot(low, block)
            total = term if total is None else total + term
        mixed, diag = fold(total[:half, :half], total[half:, half:])
        return total[:half, half:], mixed, diag

    for (k, coded), out in zip(units, outs):
        write = write_coded if coded else write_plain
        write(out, [partial_of((my_lane ^ k) * mono_dev + m) for m in range(mono_dev)])


def write_plain(out, parts):
    half = out.shape[2]
    for m, (off, mixed, diag) in enumerate(parts):
        out[m, :half] = off
        out[m, half : 2 * half] = mixed
        out[m, 2 * half :] = jnp.broadcast_to(diag, (8, half))


def read_plain(ref, m):
    half = ref.shape[2]
    return ref[m, :half], ref[m, half : 2 * half], ref[m, 2 * half : 2 * half + 1]


def write_coded(out, parts):
    half = out.shape[1]
    tail = []
    for m, (off, mixed, diag) in enumerate(parts):
        off_code = scale_code(peak_of(off))
        mixed_code = scale_code(jnp.maximum(peak_of(mixed), jnp.abs(diag)))
        out[pl.ds(m * half, half)] = pack(encode(off, off_code), encode(mixed, mixed_code))
        tail += [pack(off_code, mixed_code), encode(diag, mixed_code)]
    row = lax.broadcasted_iota(jnp.int32, (out.shape[0] - len(parts) * half, half), 0)
    last = jnp.zeros(row.shape, jnp.int32)
    for i, values in enumerate(tail):
        last = jnp.where(row == i, values, last)
    out[pl.ds(len(parts) * half, row.shape[0])] = last


def read_coded(ref, m, mono_dev):
    half = ref.shape[1]
    tail = mono_dev * half + 2 * m
    off_code, mixed_code = unpack(ref[tail : tail + 1])
    off_q, mixed_q = unpack(ref[m * half : (m + 1) * half])
    return decode(off_q, off_code), decode(mixed_q, mixed_code), decode(ref[tail + 1 : tail + 2], mixed_code)


def summed(plain_ref, coded_refs, m):
    total = read_plain(plain_ref, m)
    for ref in coded_refs:
        total = [a + b for a, b in zip(total, read_coded(ref, m, plain_ref.shape[0]))]
    return total


def merge_kernel(plain_ref, *refs):
    write_coded(refs[-1], [summed(plain_ref, refs[:-1], m) for m in range(plain_ref.shape[0])])


def finish_kernel(core_ref, own_ref, *refs):
    parts, out_ref = refs[:-1], refs[-1]
    mono_dev, basis, _ = out_ref.shape
    half = basis // 2
    for m in range(mono_dev):
        off, mixed, diag = summed(own_ref, parts, m)
        first, second = unfold(mixed, diag)
        core = core_ref[m].astype(jnp.float32)
        out_ref[m, :half, :half] = core[:half, :half] + first
        out_ref[m, :half, half:] = core[:half, half:] + off
        out_ref[m, half:, :half] = core[half:, :half] + off.T
        out_ref[m, half:, half:] = core[half:, half:] + second


def local(density, h_core, esp_block, nbr):
    groups = lax.axis_size("gddi")
    lanes = lax.axis_size("intra")
    mono_dev, basis = density.shape[0], density.shape[1]
    half = basis // 2
    hbm = pl.BlockSpec(memory_space=pl.ANY)
    small = pltpu.CompilerParams(vmem_limit_bytes=8 * 2**20)

    rows = mono_dev * basis + round_up(mono_dev, 16)
    shard = pl.pallas_call(
        fold_kernel,
        out_shape=pltpu.VMEM((rows, half), density.dtype),
        in_specs=[IN_VMEM],
        out_specs=IN_VMEM,
        compiler_params=small,
        name="fold",
    )(density)
    def along_z(piece, bit):
        return lax.ppermute(piece, "intra", xor_pairs(lanes, bit))

    def along_y(piece, y):
        return lax.ppermute(piece, "gddi", xor_pairs(groups, 2 * y))

    rows_y = groups // 2
    top = lanes // 2
    near = {(0, 0): shard, (0, top): along_z(shard, top)}

    def double(start):
        bit = top // 2
        while bit:
            for k in range(start, start + top):
                if (0, k) in near and (0, k ^ bit) not in near:
                    near[0, k ^ bit] = along_z(near[0, k], bit)
            bit //= 2

    double(0)
    for y in range(1, rows_y):
        near[y, 0] = along_y(shard, y)

    def gate(piece, *after):
        return pl.pallas_call(
            gate_kernel,
            out_shape=pltpu.VMEM(piece.shape, piece.dtype),
            in_specs=[IN_VMEM] + [hbm] * len(after),
            out_specs=IN_VMEM,
            compiler_params=small,
            name="gate",
        )(piece, *after)

    def across(piece, y, k):
        pairs = [(g * lanes + i, (g ^ 2 * y) * lanes + (i ^ k)) for g in range(groups) for i in range(lanes)]
        return lax.ppermute(piece, ("gddi", "intra"), pairs)

    others = [piece for key, piece in near.items() if key != (0, top)]
    near[0, top] = gate(gate(near[0, top]), *others)
    for y in range(1, rows_y):
        for k in range(1, top):
            near[y, k] = along_y(near[0, k], y)
            near[y, k] = gate(gate(near[y, k]))
    double(top)
    for y in range(1, rows_y):
        for k in range(top):
            near[y, top ^ k] = across(near[0, top], y, k)

    names, blocks, near[rows_y - 1, top - 1] = pl.pallas_call(
        stage_kernel,
        out_shape=[
            pltpu.SMEM((nbr.shape[1], nbr.shape[0]), nbr.dtype),
            pltpu.VMEM(esp_block.shape, esp_block.dtype),
            pltpu.VMEM(shard.shape, shard.dtype),
        ],
        in_specs=[hbm, hbm, IN_VMEM],
        out_specs=[IN_SMEM, IN_VMEM, IN_VMEM],
        scratch_shapes=[pltpu.SemaphoreType.DMA((2,))],
        compiler_params=small,
        name="stage",
    )(
        pltpu.with_memory_space_constraint(nbr.T, pltpu.HBM),
        pltpu.with_memory_space_constraint(esp_block, pltpu.HBM),
        near[rows_y - 1, top - 1],
    )
    def to_mate(piece):
        return lax.ppermute(piece, "gddi", xor_pairs(groups, 1))

    keys = [(y, k) for y in range(rows_y) for k in range(lanes)]
    batch = [key for key in keys if key[0] == 0 and bin(key[1]).count("1") <= 1]
    batched = pl.pallas_call(
        gather_kernel,
        out_shape=pltpu.VMEM((len(batch),) + shard.shape, shard.dtype),
        in_specs=[IN_VMEM] * len(batch),
        out_specs=IN_VMEM,
        compiler_params=small,
        name="gather",
    )(*[near[key] for key in batch])
    single = [key for key in keys if key not in batch]
    pieces = [near[key] for key in keys] + [to_mate(batched)] + [to_mate(near[key]) for key in single]
    for i, (y, k) in enumerate(single):
        if 0 < k < top:
            pieces[len(keys) + 1 + i] = gate(pieces[len(keys) + 1 + i])
    places = [y * lanes + k for y, k in keys]
    places += [rows_y * lanes + y * lanes + k for y, k in batch + single]

    plain = pltpu.VMEM((mono_dev, basis + 8, half), jnp.float32)
    coded = pltpu.VMEM((mono_dev * half + round_up(2 * mono_dev, 8), half), jnp.int32)
    piece_bytes = groups * lanes * rows * half * 2

    keep = pltpu.VMEM if piece_bytes <= 4 * 2**20 else jax.ShapeDtypeStruct
    store = keep((groups * lanes, rows, half), density.dtype)

    def couple(units, name, pieces, fill=False):
        return pl.pallas_call(
            functools.partial(couple_kernel, groups, lanes, mono_dev, units, places),
            out_shape=[store] * fill + [coded if is_coded else plain for _, is_coded in units],
            in_specs=[IN_SMEM] + [IN_VMEM] * (1 + len(pieces)),
            out_specs=[IN_VMEM] * (fill + len(units)),
            compiler_params=pltpu.CompilerParams(
                vmem_limit_bytes=2 * (piece_bytes + esp_block.size * 2) + 8 * 2**20
            ),
            name=name,
        )(names, blocks, *pieces)

    steps = range(1, top)
    filled, *relayed = couple([(top ^ k, True) for k in steps], "couple_relay", pieces, fill=True)
    relayed = [along_z(unit, k) for k, unit in zip(steps, relayed)]
    close = couple([(k, True) for k in steps], "couple_near", [filled])
    close = [along_z(unit, k) for k, unit in zip(steps, close)]
    for _ in range(5):
        close = [gate(unit) for unit in close]
    beyond, own = couple([(top, False), (0, False)], "couple_far", [filled])
    beyond = pl.pallas_call(
        merge_kernel,
        out_shape=coded,
        in_specs=[IN_VMEM] * (1 + len(relayed)),
        out_specs=IN_VMEM,
        compiler_params=small,
        name="merge",
    )(beyond, *relayed)
    return pl.pallas_call(
        finish_kernel,
        out_shape=jax.ShapeDtypeStruct((mono_dev, basis, basis), jnp.float32),
        in_specs=[IN_VMEM] * (3 + len(close)),
        out_specs=IN_VMEM,
        compiler_params=small,
        name="finish",
    )(h_core, own, *close, along_z(beyond, top))


def solution(mesh):
    return jax.shard_map(
        local,
        mesh=mesh,
        in_specs=(
            P(("job", "gddi", "intra"), None, None),
            P(("job", "gddi", "intra"), None, None),
            P(("job", "gddi"), "intra", None, None),
            P("job", None),
        ),
        out_specs=P(("job", "gddi", "intra"), None, None),
        check_vma=False,
    )
```

```python
import functools

import jax
import jax.numpy as jnp
from jax import lax
from jax.experimental import pallas as pl
from jax.experimental.pallas import tpu as pltpu
from jax.sharding import PartitionSpec as P

STEPS = 32.0
TOP = 32000.0
SHRINK = 1.0 / 16.0
IN_VMEM = pl.BlockSpec(memory_space=pltpu.VMEM)
IN_SMEM = pl.BlockSpec(memory_space=pltpu.SMEM)


def xor_pairs(size, k):
    return [(i, i ^ k) for i in range(size)]


def round_up(n, to):
    return -(-n // to) * to


def transposed_dot(a, b):
    return lax.dot_general(a, b, (((1,), (1,)), ((), ())), preferred_element_type=jnp.float32)


def square_iotas(half):
    row = lax.broadcasted_iota(jnp.int32, (half, half), 0)
    col = lax.broadcasted_iota(jnp.int32, (half, half), 1)
    return row, col


def fold(first, second):
    row, col = square_iotas(first.shape[0])
    mixed = jnp.where(row <= col, first, second)
    diag = jnp.sum(jnp.where(row == col, second, 0.0), axis=0, keepdims=True)
    return mixed, diag


def unfold(mixed, diag):
    row, col = square_iotas(mixed.shape[0])
    turned = mixed.T
    first = jnp.where(row <= col, mixed, turned)
    second = jnp.where(row > col, mixed, jnp.where(row < col, turned, diag))
    return first, second


def scale_code(peak):
    wanted = jnp.log(jnp.maximum(peak * SHRINK, 2.0**-120)) * STEPS
    return jnp.floor(wanted + 1.5).astype(jnp.int32)


def encode(x, code):
    units = jnp.exp(code.astype(jnp.float32) * (-1.0 / STEPS)) * TOP
    return jnp.floor(x * SHRINK * units + 0.5).astype(jnp.int32)


def decode(q, code):
    units = jnp.exp(code.astype(jnp.float32) * (1.0 / STEPS)) * (1.0 / TOP)
    return q.astype(jnp.float32) * units * (1.0 / SHRINK)


def pack(high, low):
    return lax.shift_left(high, 16) | (low & 0xFFFF)


def unpack(word):
    return lax.shift_right_arithmetic(word, 16), lax.shift_right_arithmetic(lax.shift_left(word, 16), 16)


def peak_of(x):
    return jnp.max(jnp.abs(x), axis=0, keepdims=True)


def fold_kernel(dens_ref, out_ref):
    mono_dev, basis, _ = dens_ref.shape
    half = basis // 2
    diags = []
    for m in range(mono_dev):
        out_ref[pl.ds(m * basis, half)] = dens_ref[m, :half, half:]
        mixed, diag = fold(
            dens_ref[m, :half, :half].astype(jnp.float32), dens_ref[m, half:, half:].astype(jnp.float32)
        )
        out_ref[pl.ds(m * basis + half, half)] = mixed.astype(out_ref.dtype)
        diags.append(diag)
    rows = out_ref.shape[0] - mono_dev * basis
    row = lax.broadcasted_iota(jnp.int32, (rows, half), 0)
    tail = jnp.zeros((rows, half), jnp.float32)
    for m in range(mono_dev):
        tail = jnp.where(row == m, diags[m], tail)
    out_ref[pl.ds(mono_dev * basis, rows)] = tail.astype(out_ref.dtype)


def gate_kernel(piece_ref, *refs):
    refs[-1][...] = piece_ref[...]


def stage_kernel(nbr_ref, esp_ref, piece_ref, *refs):
    nbr_out, esp_out, piece_out, sems = refs[-4:]
    copies = [
        pltpu.make_async_copy(esp_ref, esp_out, sems.at[0]),
        pltpu.make_async_copy(nbr_ref, nbr_out, sems.at[1]),
    ]
    for copy in copies:
        copy.start()
    piece_out[...] = piece_ref[...]
    for copy in copies:
        copy.wait()


def couple_kernel(groups, lanes, mono_dev, units, nbr_ref, esp_ref, *refs):
    outs = refs[len(refs) - len(units) :]
    if len(refs) > len(units) + 1:
        pieces, store = refs[: -1 - len(units)], refs[-1 - len(units)]
        for i, piece in enumerate(pieces):
            store[i] = piece[...]
    else:
        store = refs[0]
    my_group = lax.axis_index("gddi")
    my_lane = lax.axis_index("intra")
    _, slot_dev, basis, _ = esp_ref.shape
    mono_grp = mono_dev * lanes
    half = basis // 2
    tail_rows = store.shape[1] - mono_dev * basis

    def near_density(fragment):
        apart = (fragment // mono_grp) ^ my_group
        lane = ((fragment % mono_grp) // mono_dev) ^ my_lane
        place = ((apart & 1) * (groups // 2) + (apart >> 1)) * lanes + lane
        member = fragment % mono_dev
        start = pl.multiple_of(member * basis, basis)
        off = store[place, pl.ds(start, half)]
        mixed = store[place, pl.ds(start + half, half)].astype(jnp.float32)
        tail = store[place, pl.ds(mono_dev * basis, tail_rows)].astype(jnp.float32)
        row = lax.broadcasted_iota(jnp.int32, (tail_rows, half), 0)
        diag = jnp.sum(jnp.where(row == member, tail, 0.0), axis=0, keepdims=True)
        first, second = unfold(mixed, diag)
        top = jnp.concatenate([first.astype(off.dtype), off], axis=1)
        bottom = jnp.concatenate([off.T, second.astype(off.dtype)], axis=1)
        return jnp.concatenate([top, bottom], axis=0)

    def partial_of(fragment):
        high, low, blocks = [], [], []
        for s in range(slot_dev):
            name = nbr_ref[my_lane * slot_dev + s, my_group * mono_grp + fragment]
            block = esp_ref[fragment, s]
            half_term = jnp.dot(block, near_density(name), preferred_element_type=jnp.float32)
            high.append(half_term.astype(jnp.bfloat16))
            low.append((half_term - high[-1].astype(jnp.float32)).astype(jnp.bfloat16))
            blocks.append(block)
        both = jnp.concatenate([jnp.concatenate(high, axis=1), jnp.concatenate(low, axis=1)], axis=0)
        both = transposed_dot(both, jnp.concatenate(blocks, axis=1))
        total = both[:basis] + both[basis:]
        mixed, diag = fold(total[:half, :half], total[half:, half:])
        return total[:half, half:], mixed, diag

    for (k, coded), out in zip(units, outs):
        write = write_coded if coded else write_plain
        write(out, [partial_of((my_lane ^ k) * mono_dev + m) for m in range(mono_dev)])


def write_plain(out, parts):
    half = out.shape[2]
    for m, (off, mixed, diag) in enumerate(parts):
        out[m, :half] = off
        out[m, half : 2 * half] = mixed
        out[m, 2 * half :] = jnp.broadcast_to(diag, (8, half))


def read_plain(ref, m):
    half = ref.shape[2]
    return ref[m, :half], ref[m, half : 2 * half], ref[m, 2 * half : 2 * half + 1]


def write_coded(out, parts):
    half = out.shape[1]
    tail = []
    for m, (off, mixed, diag) in enumerate(parts):
        off_code = scale_code(peak_of(off))
        mixed_code = scale_code(jnp.maximum(peak_of(mixed), jnp.abs(diag)))
        out[pl.ds(m * half, half)] = pack(encode(off, off_code), encode(mixed, mixed_code))
        tail += [pack(off_code, mixed_code), encode(diag, mixed_code)]
    row = lax.broadcasted_iota(jnp.int32, (out.shape[0] - len(parts) * half, half), 0)
    last = jnp.zeros(row.shape, jnp.int32)
    for i, values in enumerate(tail):
        last = jnp.where(row == i, values, last)
    out[pl.ds(len(parts) * half, row.shape[0])] = last


def read_coded(ref, m, mono_dev):
    half = ref.shape[1]
    tail = mono_dev * half + 2 * m
    off_code, mixed_code = unpack(ref[tail : tail + 1])
    off_q, mixed_q = unpack(ref[m * half : (m + 1) * half])
    return decode(off_q, off_code), decode(mixed_q, mixed_code), decode(ref[tail + 1 : tail + 2], mixed_code)


def summed(plain_ref, coded_refs, m):
    total = read_plain(plain_ref, m)
    for ref in coded_refs:
        total = [a + b for a, b in zip(total, read_coded(ref, m, plain_ref.shape[0]))]
    return total


def merge_kernel(plain_ref, *refs):
    write_coded(refs[-1], [summed(plain_ref, refs[:-1], m) for m in range(plain_ref.shape[0])])


def finish_kernel(core_ref, own_ref, *refs):
    parts, out_ref = refs[:-1], refs[-1]
    mono_dev, basis, _ = out_ref.shape
    half = basis // 2
    for m in range(mono_dev):
        off, mixed, diag = summed(own_ref, parts, m)
        first, second = unfold(mixed, diag)
        core = core_ref[m].astype(jnp.float32)
        out_ref[m, :half, :half] = core[:half, :half] + first
        out_ref[m, :half, half:] = core[:half, half:] + off
        out_ref[m, half:, :half] = core[half:, :half] + off.T
        out_ref[m, half:, half:] = core[half:, half:] + second


def local(density, h_core, esp_block, nbr):
    groups = lax.axis_size("gddi")
    lanes = lax.axis_size("intra")
    mono_dev, basis = density.shape[0], density.shape[1]
    half = basis // 2
    hbm = pl.BlockSpec(memory_space=pl.ANY)
    small = pltpu.CompilerParams(vmem_limit_bytes=8 * 2**20)

    rows = mono_dev * basis + round_up(mono_dev, 16)
    shard = pl.pallas_call(
        fold_kernel,
        out_shape=pltpu.VMEM((rows, half), density.dtype),
        in_specs=[IN_VMEM],
        out_specs=IN_VMEM,
        compiler_params=small,
        name="fold",
    )(density)
    def along_z(piece, bit):
        return lax.ppermute(piece, "intra", xor_pairs(lanes, bit))

    def along_y(piece, y):
        return lax.ppermute(piece, "gddi", xor_pairs(groups, 2 * y))

    rows_y = groups // 2
    top = lanes // 2
    near = {(0, 0): shard, (0, top): along_z(shard, top)}

    def double(start):
        bit = top // 2
        while bit:
            for k in range(start, start + top):
                if (0, k) in near and (0, k ^ bit) not in near:
                    near[0, k ^ bit] = along_z(near[0, k], bit)
            bit //= 2

    double(0)
    for y in range(1, rows_y):
        near[y, 0] = along_y(shard, y)

    def gate(piece, *after):
        return pl.pallas_call(
            gate_kernel,
            out_shape=pltpu.VMEM(piece.shape, piece.dtype),
            in_specs=[IN_VMEM] + [hbm] * len(after),
            out_specs=IN_VMEM,
            compiler_params=small,
            name="gate",
        )(piece, *after)

    others = [piece for key, piece in near.items() if key != (0, top)]
    near[0, top] = gate(gate(near[0, top]), *others)
    double(top)
    for y in range(1, rows_y):
        for k in range(1, top):
            near[y, k] = along_z(near[y, k & (k - 1)], k & -k)
        for k in range(top, lanes):
            near[y, k] = along_y(near[0, k], y)

    names, blocks, near[rows_y - 1, 0] = pl.pallas_call(
        stage_kernel,
        out_shape=[
            pltpu.SMEM((nbr.shape[1], nbr.shape[0]), nbr.dtype),
            pltpu.VMEM(esp_block.shape, esp_block.dtype),
            pltpu.VMEM(shard.shape, shard.dtype),
        ],
        in_specs=[hbm, hbm, IN_VMEM, hbm],
        out_specs=[IN_SMEM, IN_VMEM, IN_VMEM],
        scratch_shapes=[pltpu.SemaphoreType.DMA((2,))],
        compiler_params=small,
        name="stage",
    )(
        pltpu.with_memory_space_constraint(nbr.T, pltpu.HBM),
        pltpu.with_memory_space_constraint(esp_block, pltpu.HBM),
        near[rows_y - 1, 0],
        near[0, lanes - 1],
    )
    keys = [(y, k) for y in range(rows_y) for k in range(lanes)]
    mine = [near[key] for key in keys]
    pieces = mine + [lax.ppermute(piece, "gddi", xor_pairs(groups, 1)) for piece in mine]

    plain = pltpu.VMEM((mono_dev, basis + 8, half), jnp.float32)
    coded = pltpu.VMEM((mono_dev * half + round_up(2 * mono_dev, 8), half), jnp.int32)
    piece_bytes = groups * lanes * rows * half * 2

    keep = pltpu.VMEM if piece_bytes <= 4 * 2**20 else jax.ShapeDtypeStruct
    store = keep((groups * lanes, rows, half), density.dtype)

    def couple(units, name, pieces, fill=False):
        return pl.pallas_call(
            functools.partial(couple_kernel, groups, lanes, mono_dev, units),
            out_shape=[store] * fill + [coded if is_coded else plain for _, is_coded in units],
            in_specs=[IN_SMEM] + [IN_VMEM] * (1 + len(pieces)),
            out_specs=[IN_VMEM] * (fill + len(units)),
            compiler_params=pltpu.CompilerParams(
                vmem_limit_bytes=2 * (piece_bytes + esp_block.size * 2) + 8 * 2**20
            ),
            name=name,
        )(names, blocks, *pieces)

    steps = range(1, top)
    filled, *relayed = couple([(top ^ k, True) for k in steps], "couple_relay", pieces, fill=True)
    relayed = [along_z(unit, k) for k, unit in zip(steps, relayed)]
    close = couple([(k, True) for k in steps], "couple_near", [filled])
    close = [along_z(unit, k) for k, unit in zip(steps, close)]
    for _ in range(5):
        close = [gate(unit) for unit in close]
    across, own = couple([(top, False), (0, False)], "couple_far", [filled])
    across = pl.pallas_call(
        merge_kernel,
        out_shape=coded,
        in_specs=[IN_VMEM] * (1 + len(relayed)),
        out_specs=IN_VMEM,
        compiler_params=small,
        name="merge",
    )(across, *relayed)
    return pl.pallas_call(
        finish_kernel,
        out_shape=jax.ShapeDtypeStruct((mono_dev, basis, basis), jnp.float32),
        in_specs=[IN_VMEM] * (3 + len(close)),
        out_specs=IN_VMEM,
        compiler_params=small,
        name="finish",
    )(h_core, own, *close, along_z(across, top))


def solution(mesh):
    return jax.shard_map(
        local,
        mesh=mesh,
        in_specs=(
            P(("job", "gddi", "intra"), None, None),
            P(("job", "gddi", "intra"), None, None),
            P(("job", "gddi"), "intra", None, None),
            P("job", None),
        ),
        out_specs=P(("job", "gddi", "intra"), None, None),
        check_vma=False,
    )
```

```python
import functools

import jax
import jax.numpy as jnp
from jax import lax
from jax.experimental import pallas as pl
from jax.experimental.pallas import tpu as pltpu
from jax.sharding import PartitionSpec as P

STEPS = 32.0
TOP = 32000.0
SHRINK = 1.0 / 16.0
IN_VMEM = pl.BlockSpec(memory_space=pltpu.VMEM)
IN_SMEM = pl.BlockSpec(memory_space=pltpu.SMEM)


def xor_pairs(size, k):
    return [(i, i ^ k) for i in range(size)]


def round_up(n, to):
    return -(-n // to) * to


def transposed_dot(a, b):
    return lax.dot_general(a, b, (((1,), (1,)), ((), ())), preferred_element_type=jnp.float32)


def square_iotas(half):
    row = lax.broadcasted_iota(jnp.int32, (half, half), 0)
    col = lax.broadcasted_iota(jnp.int32, (half, half), 1)
    return row, col


def fold(first, second):
    row, col = square_iotas(first.shape[0])
    mixed = jnp.where(row <= col, first, second)
    diag = jnp.sum(jnp.where(row == col, second, 0.0), axis=0, keepdims=True)
    return mixed, diag


def unfold(mixed, diag):
    row, col = square_iotas(mixed.shape[0])
    turned = mixed.T
    first = jnp.where(row <= col, mixed, turned)
    second = jnp.where(row > col, mixed, jnp.where(row < col, turned, diag))
    return first, second


def scale_code(peak):
    wanted = jnp.log(jnp.maximum(peak * SHRINK, 2.0**-120)) * STEPS
    return jnp.floor(wanted + 1.5).astype(jnp.int32)


def encode(x, code):
    units = jnp.exp(code.astype(jnp.float32) * (-1.0 / STEPS)) * TOP
    return jnp.floor(x * SHRINK * units + 0.5).astype(jnp.int32)


def decode(q, code):
    units = jnp.exp(code.astype(jnp.float32) * (1.0 / STEPS)) * (1.0 / TOP)
    return q.astype(jnp.float32) * units * (1.0 / SHRINK)


def pack(high, low):
    return lax.shift_left(high, 16) | (low & 0xFFFF)


def unpack(word):
    return lax.shift_right_arithmetic(word, 16), lax.shift_right_arithmetic(lax.shift_left(word, 16), 16)


def peak_of(x):
    return jnp.max(jnp.abs(x), axis=0, keepdims=True)


def fold_kernel(dens_ref, out_ref):
    mono_dev, basis, _ = dens_ref.shape
    half = basis // 2
    diags = []
    for m in range(mono_dev):
        out_ref[pl.ds(m * basis, half)] = dens_ref[m, :half, half:]
        mixed, diag = fold(
            dens_ref[m, :half, :half].astype(jnp.float32), dens_ref[m, half:, half:].astype(jnp.float32)
        )
        out_ref[pl.ds(m * basis + half, half)] = mixed.astype(out_ref.dtype)
        diags.append(diag)
    rows = out_ref.shape[0] - mono_dev * basis
    row = lax.broadcasted_iota(jnp.int32, (rows, half), 0)
    tail = jnp.zeros((rows, half), jnp.float32)
    for m in range(mono_dev):
        tail = jnp.where(row == m, diags[m], tail)
    out_ref[pl.ds(mono_dev * basis, rows)] = tail.astype(out_ref.dtype)


def gate_kernel(piece_ref, *refs):
    refs[-1][...] = piece_ref[...]


def stage_kernel(nbr_ref, esp_ref, piece_ref, *refs):
    nbr_out, esp_out, piece_out, sems = refs[-4:]
    copies = [
        pltpu.make_async_copy(esp_ref, esp_out, sems.at[0]),
        pltpu.make_async_copy(nbr_ref, nbr_out, sems.at[1]),
    ]
    for copy in copies:
        copy.start()
    piece_out[...] = piece_ref[...]
    for copy in copies:
        copy.wait()


def couple_kernel(groups, lanes, mono_dev, units, nbr_ref, esp_ref, *refs):
    outs = refs[len(refs) - len(units) :]
    if len(refs) > len(units) + 1:
        pieces, store = refs[: -1 - len(units)], refs[-1 - len(units)]
        for i, piece in enumerate(pieces):
            store[i] = piece[...]
    else:
        store = refs[0]
    my_group = lax.axis_index("gddi")
    my_lane = lax.axis_index("intra")
    _, slot_dev, basis, _ = esp_ref.shape
    mono_grp = mono_dev * lanes
    half = basis // 2
    tail_rows = store.shape[1] - mono_dev * basis

    def near_density(fragment):
        apart = (fragment // mono_grp) ^ my_group
        lane = ((fragment % mono_grp) // mono_dev) ^ my_lane
        place = ((apart & 1) * (groups // 2) + (apart >> 1)) * lanes + lane
        member = fragment % mono_dev
        start = pl.multiple_of(member * basis, basis)
        off = store[place, pl.ds(start, half)]
        mixed = store[place, pl.ds(start + half, half)].astype(jnp.float32)
        tail = store[place, pl.ds(mono_dev * basis, tail_rows)].astype(jnp.float32)
        row = lax.broadcasted_iota(jnp.int32, (tail_rows, half), 0)
        diag = jnp.sum(jnp.where(row == member, tail, 0.0), axis=0, keepdims=True)
        first, second = unfold(mixed, diag)
        top = jnp.concatenate([first.astype(off.dtype), off], axis=1)
        bottom = jnp.concatenate([off.T, second.astype(off.dtype)], axis=1)
        return jnp.concatenate([top, bottom], axis=0)

    def partial_of(fragment):
        high, low, blocks = [], [], []
        for s in range(slot_dev):
            name = nbr_ref[my_lane * slot_dev + s, my_group * mono_grp + fragment]
            block = esp_ref[fragment, s]
            half_term = jnp.dot(block, near_density(name), preferred_element_type=jnp.float32)
            high.append(half_term.astype(jnp.bfloat16))
            low.append((half_term - high[-1].astype(jnp.float32)).astype(jnp.bfloat16))
            blocks.append(block)
        both = jnp.concatenate([jnp.concatenate(high, axis=1), jnp.concatenate(low, axis=1)], axis=0)
        both = transposed_dot(both, jnp.concatenate(blocks, axis=1))
        total = both[:basis] + both[basis:]
        mixed, diag = fold(total[:half, :half], total[half:, half:])
        return total[:half, half:], mixed, diag

    for (k, coded), out in zip(units, outs):
        write = write_coded if coded else write_plain
        write(out, [partial_of((my_lane ^ k) * mono_dev + m) for m in range(mono_dev)])


def write_plain(out, parts):
    half = out.shape[2]
    for m, (off, mixed, diag) in enumerate(parts):
        out[m, :half] = off
        out[m, half : 2 * half] = mixed
        out[m, 2 * half :] = jnp.broadcast_to(diag, (8, half))


def read_plain(ref, m):
    half = ref.shape[2]
    return ref[m, :half], ref[m, half : 2 * half], ref[m, 2 * half : 2 * half + 1]


def write_coded(out, parts):
    half = out.shape[1]
    tail = []
    for m, (off, mixed, diag) in enumerate(parts):
        off_code = scale_code(peak_of(off))
        mixed_code = scale_code(jnp.maximum(peak_of(mixed), jnp.abs(diag)))
        out[pl.ds(m * half, half)] = pack(encode(off, off_code), encode(mixed, mixed_code))
        tail += [pack(off_code, mixed_code), encode(diag, mixed_code)]
    row = lax.broadcasted_iota(jnp.int32, (out.shape[0] - len(parts) * half, half), 0)
    last = jnp.zeros(row.shape, jnp.int32)
    for i, values in enumerate(tail):
        last = jnp.where(row == i, values, last)
    out[pl.ds(len(parts) * half, row.shape[0])] = last


def read_coded(ref, m, mono_dev):
    half = ref.shape[1]
    tail = mono_dev * half + 2 * m
    off_code, mixed_code = unpack(ref[tail : tail + 1])
    off_q, mixed_q = unpack(ref[m * half : (m + 1) * half])
    return decode(off_q, off_code), decode(mixed_q, mixed_code), decode(ref[tail + 1 : tail + 2], mixed_code)


def summed(plain_ref, coded_refs, m):
    total = read_plain(plain_ref, m)
    for ref in coded_refs:
        total = [a + b for a, b in zip(total, read_coded(ref, m, plain_ref.shape[0]))]
    return total


def merge_kernel(plain_ref, *refs):
    write_coded(refs[-1], [summed(plain_ref, refs[:-1], m) for m in range(plain_ref.shape[0])])


def finish_kernel(core_ref, own_ref, *refs):
    parts, out_ref = refs[:-1], refs[-1]
    mono_dev, basis, _ = out_ref.shape
    half = basis // 2
    for m in range(mono_dev):
        off, mixed, diag = summed(own_ref, parts, m)
        first, second = unfold(mixed, diag)
        core = core_ref[m].astype(jnp.float32)
        out_ref[m, :half, :half] = core[:half, :half] + first
        out_ref[m, :half, half:] = core[:half, half:] + off
        out_ref[m, half:, :half] = core[half:, :half] + off.T
        out_ref[m, half:, half:] = core[half:, half:] + second


def local(density, h_core, esp_block, nbr):
    groups = lax.axis_size("gddi")
    lanes = lax.axis_size("intra")
    mono_dev, basis = density.shape[0], density.shape[1]
    half = basis // 2
    hbm = pl.BlockSpec(memory_space=pl.ANY)
    small = pltpu.CompilerParams(vmem_limit_bytes=8 * 2**20)

    rows = mono_dev * basis + round_up(mono_dev, 16)
    shard = pl.pallas_call(
        fold_kernel,
        out_shape=pltpu.VMEM((rows, half), density.dtype),
        in_specs=[IN_VMEM],
        out_specs=IN_VMEM,
        compiler_params=small,
        name="fold",
    )(density)
    def along_z(piece, bit):
        return lax.ppermute(piece, "intra", xor_pairs(lanes, bit))

    def along_y(piece, y):
        return lax.ppermute(piece, "gddi", xor_pairs(groups, 2 * y))

    rows_y = groups // 2
    top = lanes // 2
    near = {(0, 0): shard, (0, top): along_z(shard, top)}

    def double(start):
        bit = top // 2
        while bit:
            for k in range(start, start + top):
                if (0, k) in near and (0, k ^ bit) not in near:
                    near[0, k ^ bit] = along_z(near[0, k], bit)
            bit //= 2

    double(0)
    for y in range(1, rows_y):
        near[y, 0] = along_y(shard, y)

    def gate(piece, *after):
        return pl.pallas_call(
            gate_kernel,
            out_shape=pltpu.VMEM(piece.shape, piece.dtype),
            in_specs=[IN_VMEM] + [hbm] * len(after),
            out_specs=IN_VMEM,
            compiler_params=small,
            name="gate",
        )(piece, *after)

    others = [piece for key, piece in near.items() if key != (0, top)]
    near[0, top] = gate(gate(near[0, top]), *others)
    double(top)
    for y in range(1, rows_y):
        for k in range(1, top):
            near[y, k] = along_z(near[y, k & (k - 1)], k & -k)
        for k in range(top, lanes):
            near[y, k] = along_y(near[0, k], y)

    names, blocks, near[rows_y - 1, 0] = pl.pallas_call(
        stage_kernel,
        out_shape=[
            pltpu.SMEM((nbr.shape[1], nbr.shape[0]), nbr.dtype),
            pltpu.VMEM(esp_block.shape, esp_block.dtype),
            pltpu.VMEM(shard.shape, shard.dtype),
        ],
        in_specs=[hbm, hbm, IN_VMEM, hbm],
        out_specs=[IN_SMEM, IN_VMEM, IN_VMEM],
        scratch_shapes=[pltpu.SemaphoreType.DMA((2,))],
        compiler_params=small,
        name="stage",
    )(
        pltpu.with_memory_space_constraint(nbr.T, pltpu.HBM),
        pltpu.with_memory_space_constraint(esp_block, pltpu.HBM),
        near[rows_y - 1, 0],
        near[0, lanes - 1],
    )
    keys = [(y, k) for y in range(rows_y) for k in range(lanes)]
    mine = [near[key] for key in keys]
    pieces = mine + [lax.ppermute(piece, "gddi", xor_pairs(groups, 1)) for piece in mine]

    plain = pltpu.VMEM((mono_dev, basis + 8, half), jnp.float32)
    coded = pltpu.VMEM((mono_dev * half + round_up(2 * mono_dev, 8), half), jnp.int32)
    piece_bytes = groups * lanes * rows * half * 2

    keep = pltpu.VMEM if piece_bytes <= 4 * 2**20 else jax.ShapeDtypeStruct
    store = keep((groups * lanes, rows, half), density.dtype)

    def couple(units, name, pieces, fill=False):
        return pl.pallas_call(
            functools.partial(couple_kernel, groups, lanes, mono_dev, units),
            out_shape=[store] * fill + [coded if is_coded else plain for _, is_coded in units],
            in_specs=[IN_SMEM] + [IN_VMEM] * (1 + len(pieces)),
            out_specs=[IN_VMEM] * (fill + len(units)),
            compiler_params=pltpu.CompilerParams(
                vmem_limit_bytes=2 * (piece_bytes + esp_block.size * 2) + 8 * 2**20
            ),
            name=name,
        )(names, blocks, *pieces)

    steps = range(1, top)
    filled, *relayed = couple([(top ^ k, True) for k in steps], "couple_relay", pieces, fill=True)
    relayed = [along_z(unit, k) for k, unit in zip(steps, relayed)]
    beyond, own, *close = couple([(top, False), (0, False)] + [(k, True) for k in steps], "couple_rest", [filled])
    beyond = pl.pallas_call(
        merge_kernel,
        out_shape=pltpu.VMEM((coded.shape[0] + 8, half), jnp.int32),
        in_specs=[IN_VMEM] * (1 + len(relayed)),
        out_specs=IN_VMEM,
        compiler_params=small,
        name="merge",
    )(beyond, *relayed)
    close = [along_z(gate(unit, beyond), k) for k, unit in zip(steps, close)]
    return pl.pallas_call(
        finish_kernel,
        out_shape=jax.ShapeDtypeStruct((mono_dev, basis, basis), jnp.float32),
        in_specs=[IN_VMEM] * (3 + len(close)),
        out_specs=IN_VMEM,
        compiler_params=small,
        name="finish",
    )(h_core, own, *close, along_z(beyond, top))


def solution(mesh):
    return jax.shard_map(
        local,
        mesh=mesh,
        in_specs=(
            P(("job", "gddi", "intra"), None, None),
            P(("job", "gddi", "intra"), None, None),
            P(("job", "gddi"), "intra", None, None),
            P("job", None),
        ),
        out_specs=P(("job", "gddi", "intra"), None, None),
        check_vma=False,
    )
```

```python
import functools

import jax
import jax.numpy as jnp
from jax import lax
from jax.experimental import pallas as pl
from jax.experimental.pallas import tpu as pltpu
from jax.sharding import PartitionSpec as P

STEPS = 32.0
TOP = 32000.0
SHRINK = 1.0 / 16.0
IN_VMEM = pl.BlockSpec(memory_space=pltpu.VMEM)
IN_SMEM = pl.BlockSpec(memory_space=pltpu.SMEM)


def xor_pairs(size, k):
    return [(i, i ^ k) for i in range(size)]


def round_up(n, to):
    return -(-n // to) * to


def transposed_dot(a, b):
    return lax.dot_general(a, b, (((1,), (1,)), ((), ())), preferred_element_type=jnp.float32)


def square_iotas(half):
    row = lax.broadcasted_iota(jnp.int32, (half, half), 0)
    col = lax.broadcasted_iota(jnp.int32, (half, half), 1)
    return row, col


def fold(first, second):
    row, col = square_iotas(first.shape[0])
    mixed = jnp.where(row <= col, first, second)
    diag = jnp.sum(jnp.where(row == col, second, 0.0), axis=0, keepdims=True)
    return mixed, diag


def unfold(mixed, diag):
    row, col = square_iotas(mixed.shape[0])
    turned = mixed.T
    first = jnp.where(row <= col, mixed, turned)
    second = jnp.where(row > col, mixed, jnp.where(row < col, turned, diag))
    return first, second


def scale_code(peak):
    wanted = jnp.log(jnp.maximum(peak * SHRINK, 2.0**-120)) * STEPS
    return jnp.floor(wanted + 1.5).astype(jnp.int32)


def encode(x, code):
    units = jnp.exp(code.astype(jnp.float32) * (-1.0 / STEPS)) * TOP
    return jnp.floor(x * SHRINK * units + 0.5).astype(jnp.int32)


def decode(q, code):
    units = jnp.exp(code.astype(jnp.float32) * (1.0 / STEPS)) * (1.0 / TOP)
    return q.astype(jnp.float32) * units * (1.0 / SHRINK)


def pack(high, low):
    return lax.shift_left(high, 16) | (low & 0xFFFF)


def unpack(word):
    return lax.shift_right_arithmetic(word, 16), lax.shift_right_arithmetic(lax.shift_left(word, 16), 16)


def peak_of(x):
    return jnp.max(jnp.abs(x), axis=0, keepdims=True)


def fold_kernel(dens_ref, out_ref):
    mono_dev, basis, _ = dens_ref.shape
    half = basis // 2
    diags = []
    for m in range(mono_dev):
        out_ref[pl.ds(m * basis, half)] = dens_ref[m, :half, half:]
        mixed, diag = fold(
            dens_ref[m, :half, :half].astype(jnp.float32), dens_ref[m, half:, half:].astype(jnp.float32)
        )
        out_ref[pl.ds(m * basis + half, half)] = mixed.astype(out_ref.dtype)
        diags.append(diag)
    rows = out_ref.shape[0] - mono_dev * basis
    row = lax.broadcasted_iota(jnp.int32, (rows, half), 0)
    tail = jnp.zeros((rows, half), jnp.float32)
    for m in range(mono_dev):
        tail = jnp.where(row == m, diags[m], tail)
    out_ref[pl.ds(mono_dev * basis, rows)] = tail.astype(out_ref.dtype)


def gate_kernel(piece_ref, *refs):
    refs[-1][...] = piece_ref[...]


def stage_kernel(nbr_ref, esp_ref, piece_ref, *refs):
    nbr_out, esp_out, piece_out, sems = refs[-4:]
    copies = [
        pltpu.make_async_copy(esp_ref, esp_out, sems.at[0]),
        pltpu.make_async_copy(nbr_ref, nbr_out, sems.at[1]),
    ]
    for copy in copies:
        copy.start()
    piece_out[...] = piece_ref[...]
    for copy in copies:
        copy.wait()


def couple_kernel(groups, lanes, mono_dev, units, nbr_ref, esp_ref, *refs):
    outs = refs[len(refs) - len(units) :]
    if len(refs) > len(units) + 1:
        pieces, store = refs[: -1 - len(units)], refs[-1 - len(units)]
        for i, piece in enumerate(pieces):
            store[i] = piece[...]
    else:
        store = refs[0]
    my_group = lax.axis_index("gddi")
    my_lane = lax.axis_index("intra")
    _, slot_dev, basis, _ = esp_ref.shape
    mono_grp = mono_dev * lanes
    half = basis // 2
    tail_rows = store.shape[1] - mono_dev * basis

    def near_density(fragment):
        apart = (fragment // mono_grp) ^ my_group
        lane = ((fragment % mono_grp) // mono_dev) ^ my_lane
        place = ((apart & 1) * (groups // 2) + (apart >> 1)) * lanes + lane
        member = fragment % mono_dev
        start = pl.multiple_of(member * basis, basis)
        off = store[place, pl.ds(start, half)]
        mixed = store[place, pl.ds(start + half, half)].astype(jnp.float32)
        tail = store[place, pl.ds(mono_dev * basis, tail_rows)].astype(jnp.float32)
        row = lax.broadcasted_iota(jnp.int32, (tail_rows, half), 0)
        diag = jnp.sum(jnp.where(row == member, tail, 0.0), axis=0, keepdims=True)
        first, second = unfold(mixed, diag)
        top = jnp.concatenate([first.astype(off.dtype), off], axis=1)
        bottom = jnp.concatenate([off.T, second.astype(off.dtype)], axis=1)
        return jnp.concatenate([top, bottom], axis=0)

    def partial_of(fragment):
        high, low, blocks = [], [], []
        for s in range(slot_dev):
            name = nbr_ref[my_lane * slot_dev + s, my_group * mono_grp + fragment]
            block = esp_ref[fragment, s]
            half_term = jnp.dot(block, near_density(name), preferred_element_type=jnp.float32)
            high.append(half_term.astype(jnp.bfloat16))
            low.append((half_term - high[-1].astype(jnp.float32)).astype(jnp.bfloat16))
            blocks.append(block)
        both = jnp.concatenate([jnp.concatenate(high, axis=1), jnp.concatenate(low, axis=1)], axis=0)
        both = transposed_dot(both, jnp.concatenate(blocks, axis=1))
        total = both[:basis] + both[basis:]
        mixed, diag = fold(total[:half, :half], total[half:, half:])
        return total[:half, half:], mixed, diag

    for (k, coded), out in zip(units, outs):
        write = write_coded if coded else write_plain
        write(out, [partial_of((my_lane ^ k) * mono_dev + m) for m in range(mono_dev)])


def write_plain(out, parts):
    half = out.shape[2]
    for m, (off, mixed, diag) in enumerate(parts):
        out[m, :half] = off
        out[m, half : 2 * half] = mixed
        out[m, 2 * half :] = jnp.broadcast_to(diag, (8, half))


def read_plain(ref, m):
    half = ref.shape[2]
    return ref[m, :half], ref[m, half : 2 * half], ref[m, 2 * half : 2 * half + 1]


def write_coded(out, parts):
    half = out.shape[1]
    tail = []
    for m, (off, mixed, diag) in enumerate(parts):
        off_code = scale_code(peak_of(off))
        mixed_code = scale_code(jnp.maximum(peak_of(mixed), jnp.abs(diag)))
        out[pl.ds(m * half, half)] = pack(encode(off, off_code), encode(mixed, mixed_code))
        tail += [pack(off_code, mixed_code), encode(diag, mixed_code)]
    row = lax.broadcasted_iota(jnp.int32, (out.shape[0] - len(parts) * half, half), 0)
    last = jnp.zeros(row.shape, jnp.int32)
    for i, values in enumerate(tail):
        last = jnp.where(row == i, values, last)
    out[pl.ds(len(parts) * half, row.shape[0])] = last


def read_coded(ref, m, mono_dev):
    half = ref.shape[1]
    tail = mono_dev * half + 2 * m
    off_code, mixed_code = unpack(ref[tail : tail + 1])
    off_q, mixed_q = unpack(ref[m * half : (m + 1) * half])
    return decode(off_q, off_code), decode(mixed_q, mixed_code), decode(ref[tail + 1 : tail + 2], mixed_code)


def summed(plain_ref, coded_refs, m):
    total = read_plain(plain_ref, m)
    for ref in coded_refs:
        total = [a + b for a, b in zip(total, read_coded(ref, m, plain_ref.shape[0]))]
    return total


def finish_kernel(core_ref, own_ref, *refs):
    parts, out_ref = refs[:-1], refs[-1]
    mono_dev, basis, _ = out_ref.shape
    half = basis // 2
    for m in range(mono_dev):
        off, mixed, diag = summed(own_ref, parts, m)
        first, second = unfold(mixed, diag)
        core = core_ref[m].astype(jnp.float32)
        out_ref[m, :half, :half] = core[:half, :half] + first
        out_ref[m, :half, half:] = core[:half, half:] + off
        out_ref[m, half:, :half] = core[half:, :half] + off.T
        out_ref[m, half:, half:] = core[half:, half:] + second


def local(density, h_core, esp_block, nbr):
    groups = lax.axis_size("gddi")
    lanes = lax.axis_size("intra")
    mono_dev, basis = density.shape[0], density.shape[1]
    half = basis // 2
    hbm = pl.BlockSpec(memory_space=pl.ANY)
    small = pltpu.CompilerParams(vmem_limit_bytes=8 * 2**20)

    rows = mono_dev * basis + round_up(mono_dev, 16)
    shard = pl.pallas_call(
        fold_kernel,
        out_shape=pltpu.VMEM((rows, half), density.dtype),
        in_specs=[IN_VMEM],
        out_specs=IN_VMEM,
        compiler_params=small,
        name="fold",
    )(density)
    def along_z(piece, bit):
        return lax.ppermute(piece, "intra", xor_pairs(lanes, bit))

    def along_y(piece, y):
        return lax.ppermute(piece, "gddi", xor_pairs(groups, 2 * y))

    rows_y = groups // 2
    top = lanes // 2
    near = {(0, 0): shard, (0, top): along_z(shard, top)}

    def double(start):
        bit = top // 2
        while bit:
            for k in range(start, start + top):
                if (0, k) in near and (0, k ^ bit) not in near:
                    near[0, k ^ bit] = along_z(near[0, k], bit)
            bit //= 2

    double(0)
    for y in range(1, rows_y):
        near[y, 0] = along_y(shard, y)

    def gate(piece, *after):
        return pl.pallas_call(
            gate_kernel,
            out_shape=pltpu.VMEM(piece.shape, piece.dtype),
            in_specs=[IN_VMEM] + [hbm] * len(after),
            out_specs=IN_VMEM,
            compiler_params=small,
            name="gate",
        )(piece, *after)

    others = [piece for key, piece in near.items() if key != (0, top)]
    near[0, top] = gate(gate(near[0, top]), *others)
    double(top)
    for y in range(1, rows_y):
        for k in range(1, top):
            near[y, k] = along_z(near[y, k & (k - 1)], k & -k)
        for k in range(top, lanes):
            near[y, k] = along_y(near[0, k], y)

    names, blocks, near[rows_y - 1, 0] = pl.pallas_call(
        stage_kernel,
        out_shape=[
            pltpu.SMEM((nbr.shape[1], nbr.shape[0]), nbr.dtype),
            pltpu.VMEM(esp_block.shape, esp_block.dtype),
            pltpu.VMEM(shard.shape, shard.dtype),
        ],
        in_specs=[hbm, hbm, IN_VMEM, hbm],
        out_specs=[IN_SMEM, IN_VMEM, IN_VMEM],
        scratch_shapes=[pltpu.SemaphoreType.DMA((2,))],
        compiler_params=small,
        name="stage",
    )(
        pltpu.with_memory_space_constraint(nbr.T, pltpu.HBM),
        pltpu.with_memory_space_constraint(esp_block, pltpu.HBM),
        near[rows_y - 1, 0],
        near[0, lanes - 1],
    )
    keys = [(y, k) for y in range(rows_y) for k in range(lanes)]
    mine = [near[key] for key in keys]
    pieces = mine + [lax.ppermute(piece, "gddi", xor_pairs(groups, 1)) for piece in mine]

    plain = pltpu.VMEM((mono_dev, basis + 8, half), jnp.float32)
    coded = pltpu.VMEM((mono_dev * half + round_up(2 * mono_dev, 8), half), jnp.int32)
    piece_bytes = groups * lanes * rows * half * 2

    keep = pltpu.VMEM if piece_bytes <= 4 * 2**20 else jax.ShapeDtypeStruct
    store = keep((groups * lanes, rows, half), density.dtype)

    def couple(units, name, pieces, fill=False):
        return pl.pallas_call(
            functools.partial(couple_kernel, groups, lanes, mono_dev, units),
            out_shape=[store] * fill + [coded if is_coded else plain for _, is_coded in units],
            in_specs=[IN_SMEM] + [IN_VMEM] * (1 + len(pieces)),
            out_specs=[IN_VMEM] * (fill + len(units)),
            compiler_params=pltpu.CompilerParams(
                vmem_limit_bytes=2 * (piece_bytes + esp_block.size * 2) + 8 * 2**20
            ),
            name=name,
        )(names, blocks, *pieces)

    filled, beyond = couple([(top, True)], "couple_first", pieces, fill=True)
    beyond = {top: along_z(beyond, top)}
    for _ in range(5):
        beyond[top] = gate(beyond[top])
    rest = [k for k in range(1, lanes) if k != top]
    own, *units = couple([(0, False)] + [(k, True) for k in rest], "couple_rest", [filled])
    for k, unit in zip(rest, units):
        beyond[k] = along_z(unit, k)
    return pl.pallas_call(
        finish_kernel,
        out_shape=jax.ShapeDtypeStruct((mono_dev, basis, basis), jnp.float32),
        in_specs=[IN_VMEM] * (1 + lanes),
        out_specs=IN_VMEM,
        compiler_params=small,
        name="finish",
    )(h_core, own, *[beyond[k] for k in range(1, lanes)])


def solution(mesh):
    return jax.shard_map(
        local,
        mesh=mesh,
        in_specs=(
            P(("job", "gddi", "intra"), None, None),
            P(("job", "gddi", "intra"), None, None),
            P(("job", "gddi"), "intra", None, None),
            P("job", None),
        ),
        out_specs=P(("job", "gddi", "intra"), None, None),
        check_vma=False,
    )
```

```python
import functools

import jax
import jax.numpy as jnp
from jax import lax
from jax.experimental import pallas as pl
from jax.experimental.pallas import tpu as pltpu
from jax.sharding import PartitionSpec as P

STEPS = 32.0
TOP = 32000.0
SHRINK = 1.0 / 16.0
IN_VMEM = pl.BlockSpec(memory_space=pltpu.VMEM)
IN_SMEM = pl.BlockSpec(memory_space=pltpu.SMEM)


def xor_pairs(size, k):
    return [(i, i ^ k) for i in range(size)]


def round_up(n, to):
    return -(-n // to) * to


def transposed_dot(a, b):
    return lax.dot_general(a, b, (((1,), (1,)), ((), ())), preferred_element_type=jnp.float32)


def square_iotas(half):
    row = lax.broadcasted_iota(jnp.int32, (half, half), 0)
    col = lax.broadcasted_iota(jnp.int32, (half, half), 1)
    return row, col


def fold(first, second):
    row, col = square_iotas(first.shape[0])
    mixed = jnp.where(row <= col, first, second)
    diag = jnp.sum(jnp.where(row == col, second, 0.0), axis=0, keepdims=True)
    return mixed, diag


def unfold(mixed, diag):
    row, col = square_iotas(mixed.shape[0])
    turned = mixed.T
    first = jnp.where(row <= col, mixed, turned)
    second = jnp.where(row > col, mixed, jnp.where(row < col, turned, diag))
    return first, second


def scale_code(peak):
    wanted = jnp.log(jnp.maximum(peak * SHRINK, 2.0**-120)) * STEPS
    return jnp.floor(wanted + 1.5).astype(jnp.int32)


def encode(x, code):
    units = jnp.exp(code.astype(jnp.float32) * (-1.0 / STEPS)) * TOP
    return jnp.floor(x * SHRINK * units + 0.5).astype(jnp.int32)


def decode(q, code):
    units = jnp.exp(code.astype(jnp.float32) * (1.0 / STEPS)) * (1.0 / TOP)
    return q.astype(jnp.float32) * units * (1.0 / SHRINK)


def pack(high, low):
    return lax.shift_left(high, 16) | (low & 0xFFFF)


def unpack(word):
    return lax.shift_right_arithmetic(word, 16), lax.shift_right_arithmetic(lax.shift_left(word, 16), 16)


def peak_of(x):
    return jnp.max(jnp.abs(x), axis=0, keepdims=True)


def fold_kernel(dens_ref, out_ref):
    mono_dev, basis, _ = dens_ref.shape
    half = basis // 2
    diags = []
    for m in range(mono_dev):
        out_ref[pl.ds(m * basis, half)] = dens_ref[m, :half, half:]
        mixed, diag = fold(
            dens_ref[m, :half, :half].astype(jnp.float32), dens_ref[m, half:, half:].astype(jnp.float32)
        )
        out_ref[pl.ds(m * basis + half, half)] = mixed.astype(out_ref.dtype)
        diags.append(diag)
    rows = out_ref.shape[0] - mono_dev * basis
    row = lax.broadcasted_iota(jnp.int32, (rows, half), 0)
    tail = jnp.zeros((rows, half), jnp.float32)
    for m in range(mono_dev):
        tail = jnp.where(row == m, diags[m], tail)
    out_ref[pl.ds(mono_dev * basis, rows)] = tail.astype(out_ref.dtype)


def gate_kernel(piece_ref, *refs):
    refs[-1][...] = piece_ref[...]


def stage_kernel(nbr_ref, esp_ref, piece_ref, *refs):
    nbr_out, esp_out, piece_out, sems = refs[-4:]
    copies = [
        pltpu.make_async_copy(esp_ref, esp_out, sems.at[0]),
        pltpu.make_async_copy(nbr_ref, nbr_out, sems.at[1]),
    ]
    for copy in copies:
        copy.start()
    piece_out[...] = piece_ref[...]
    for copy in copies:
        copy.wait()


def couple_kernel(groups, lanes, mono_dev, units, nbr_ref, esp_ref, *refs):
    outs = refs[len(refs) - len(units) :]
    if len(refs) > len(units) + 1:
        pieces, store = refs[: -1 - len(units)], refs[-1 - len(units)]
        for i, piece in enumerate(pieces):
            store[i] = piece[...]
    else:
        store = refs[0]
    my_group = lax.axis_index("gddi")
    my_lane = lax.axis_index("intra")
    _, slot_dev, basis, _ = esp_ref.shape
    mono_grp = mono_dev * lanes
    half = basis // 2
    tail_rows = store.shape[1] - mono_dev * basis

    def near_density(fragment):
        apart = (fragment // mono_grp) ^ my_group
        lane = ((fragment % mono_grp) // mono_dev) ^ my_lane
        place = ((apart & 1) * (groups // 2) + (apart >> 1)) * lanes + lane
        member = fragment % mono_dev
        start = pl.multiple_of(member * basis, basis)
        off = store[place, pl.ds(start, half)]
        mixed = store[place, pl.ds(start + half, half)].astype(jnp.float32)
        tail = store[place, pl.ds(mono_dev * basis, tail_rows)].astype(jnp.float32)
        row = lax.broadcasted_iota(jnp.int32, (tail_rows, half), 0)
        diag = jnp.sum(jnp.where(row == member, tail, 0.0), axis=0, keepdims=True)
        first, second = unfold(mixed, diag)
        top = jnp.concatenate([first.astype(off.dtype), off], axis=1)
        bottom = jnp.concatenate([off.T, second.astype(off.dtype)], axis=1)
        return jnp.concatenate([top, bottom], axis=0)

    def partial_of(fragment):
        high, low, blocks = [], [], []
        for s in range(slot_dev):
            name = nbr_ref[my_lane * slot_dev + s, my_group * mono_grp + fragment]
            block = esp_ref[fragment, s]
            half_term = jnp.dot(block, near_density(name), preferred_element_type=jnp.float32)
            high.append(half_term.astype(jnp.bfloat16))
            low.append((half_term - high[-1].astype(jnp.float32)).astype(jnp.bfloat16))
            blocks.append(block)
        both = jnp.concatenate([jnp.concatenate(high, axis=1), jnp.concatenate(low, axis=1)], axis=0)
        both = transposed_dot(both, jnp.concatenate(blocks, axis=1))
        total = both[:basis] + both[basis:]
        mixed, diag = fold(total[:half, :half], total[half:, half:])
        return total[:half, half:], mixed, diag

    for (k, coded), out in zip(units, outs):
        write = write_coded if coded else write_plain
        write(out, [partial_of((my_lane ^ k) * mono_dev + m) for m in range(mono_dev)])


def write_plain(out, parts):
    half = out.shape[2]
    for m, (off, mixed, diag) in enumerate(parts):
        out[m, :half] = off
        out[m, half : 2 * half] = mixed
        out[m, 2 * half :] = jnp.broadcast_to(diag, (8, half))


def read_plain(ref, m):
    half = ref.shape[2]
    return ref[m, :half], ref[m, half : 2 * half], ref[m, 2 * half : 2 * half + 1]


def write_coded(out, parts):
    half = out.shape[1]
    tail = []
    for m, (off, mixed, diag) in enumerate(parts):
        off_code = scale_code(peak_of(off))
        mixed_code = scale_code(jnp.maximum(peak_of(mixed), jnp.abs(diag)))
        out[pl.ds(m * half, half)] = pack(encode(off, off_code), encode(mixed, mixed_code))
        tail += [pack(off_code, mixed_code), encode(diag, mixed_code)]
    row = lax.broadcasted_iota(jnp.int32, (out.shape[0] - len(parts) * half, half), 0)
    last = jnp.zeros(row.shape, jnp.int32)
    for i, values in enumerate(tail):
        last = jnp.where(row == i, values, last)
    out[pl.ds(len(parts) * half, row.shape[0])] = last


def read_coded(ref, m, mono_dev):
    half = ref.shape[1]
    tail = mono_dev * half + 2 * m
    off_code, mixed_code = unpack(ref[tail : tail + 1])
    off_q, mixed_q = unpack(ref[m * half : (m + 1) * half])
    return decode(off_q, off_code), decode(mixed_q, mixed_code), decode(ref[tail + 1 : tail + 2], mixed_code)


def summed(plain_ref, coded_refs, m):
    total = read_plain(plain_ref, m)
    for ref in coded_refs:
        total = [a + b for a, b in zip(total, read_coded(ref, m, plain_ref.shape[0]))]
    return total


def finish_kernel(core_ref, own_ref, *refs):
    parts, out_ref = refs[:-1], refs[-1]
    mono_dev, basis, _ = out_ref.shape
    half = basis // 2
    for m in range(mono_dev):
        off, mixed, diag = summed(own_ref, parts, m)
        first, second = unfold(mixed, diag)
        core = core_ref[m].astype(jnp.float32)
        out_ref[m, :half, :half] = core[:half, :half] + first
        out_ref[m, :half, half:] = core[:half, half:] + off
        out_ref[m, half:, :half] = core[half:, :half] + off.T
        out_ref[m, half:, half:] = core[half:, half:] + second


def local(density, h_core, esp_block, nbr):
    groups = lax.axis_size("gddi")
    lanes = lax.axis_size("intra")
    mono_dev, basis = density.shape[0], density.shape[1]
    half = basis // 2
    hbm = pl.BlockSpec(memory_space=pl.ANY)
    small = pltpu.CompilerParams(vmem_limit_bytes=8 * 2**20)

    rows = mono_dev * basis + round_up(mono_dev, 16)
    shard = pl.pallas_call(
        fold_kernel,
        out_shape=pltpu.VMEM((rows, half), density.dtype),
        in_specs=[IN_VMEM],
        out_specs=IN_VMEM,
        compiler_params=small,
        name="fold",
    )(density)
    def along_z(piece, bit):
        return lax.ppermute(piece, "intra", xor_pairs(lanes, bit))

    def along_y(piece, y):
        return lax.ppermute(piece, "gddi", xor_pairs(groups, 2 * y))

    rows_y = groups // 2
    top = lanes // 2
    near = {(0, 0): shard, (0, top): along_z(shard, top)}

    def double(start):
        bit = top // 2
        while bit:
            for k in range(start, start + top):
                if (0, k) in near and (0, k ^ bit) not in near:
                    near[0, k ^ bit] = along_z(near[0, k], bit)
            bit //= 2

    double(0)
    for y in range(1, rows_y):
        near[y, 0] = along_y(shard, y)

    def gate(piece, *after):
        return pl.pallas_call(
            gate_kernel,
            out_shape=pltpu.VMEM(piece.shape, piece.dtype),
            in_specs=[IN_VMEM] + [hbm] * len(after),
            out_specs=IN_VMEM,
            compiler_params=small,
            name="gate",
        )(piece, *after)

    others = [piece for key, piece in near.items() if key != (0, top)]
    near[0, top] = gate(gate(near[0, top]), *others)
    double(top)
    for y in range(1, rows_y):
        for k in range(1, top):
            near[y, k] = along_z(gate(near[y, k & (k - 1)], near[0, lanes - 1]), k & -k)
        for k in range(top, lanes):
            near[y, k] = along_y(near[0, k], y)

    names, blocks, near[rows_y - 1, 0] = pl.pallas_call(
        stage_kernel,
        out_shape=[
            pltpu.SMEM((nbr.shape[1], nbr.shape[0]), nbr.dtype),
            pltpu.VMEM(esp_block.shape, esp_block.dtype),
            pltpu.VMEM(shard.shape, shard.dtype),
        ],
        in_specs=[hbm, hbm, IN_VMEM, hbm],
        out_specs=[IN_SMEM, IN_VMEM, IN_VMEM],
        scratch_shapes=[pltpu.SemaphoreType.DMA((2,))],
        compiler_params=small,
        name="stage",
    )(
        pltpu.with_memory_space_constraint(nbr.T, pltpu.HBM),
        pltpu.with_memory_space_constraint(esp_block, pltpu.HBM),
        near[rows_y - 1, 0],
        near[0, lanes - 1],
    )
    keys = [(y, k) for y in range(rows_y) for k in range(lanes)]
    mine = [near[key] for key in keys]
    pieces = mine + [lax.ppermute(piece, "gddi", xor_pairs(groups, 1)) for piece in mine]
    least = len(mine) + (rows_y - 1) * lanes + top - 1
    pieces = [gate(piece) if i >= len(mine) and i != least else piece for i, piece in enumerate(pieces)]

    plain = pltpu.VMEM((mono_dev, basis + 8, half), jnp.float32)
    coded = pltpu.VMEM((mono_dev * half + round_up(2 * mono_dev, 8), half), jnp.int32)
    piece_bytes = groups * lanes * rows * half * 2

    keep = pltpu.VMEM if piece_bytes <= 4 * 2**20 else jax.ShapeDtypeStruct
    store = keep((groups * lanes, rows, half), density.dtype)

    def couple(units, name, pieces, fill=False):
        return pl.pallas_call(
            functools.partial(couple_kernel, groups, lanes, mono_dev, units),
            out_shape=[store] * fill + [coded if is_coded else plain for _, is_coded in units],
            in_specs=[IN_SMEM] + [IN_VMEM] * (1 + len(pieces)),
            out_specs=[IN_VMEM] * (fill + len(units)),
            compiler_params=pltpu.CompilerParams(
                vmem_limit_bytes=2 * (piece_bytes + esp_block.size * 2) + 8 * 2**20
            ),
            name=name,
        )(names, blocks, *pieces)

    filled, beyond = couple([(top, True)], "couple_first", pieces, fill=True)
    beyond = {top: along_z(beyond, top)}
    for _ in range(5):
        beyond[top] = gate(beyond[top])
    rest = [k for k in range(1, lanes) if k != top]
    own, *units = couple([(0, False)] + [(k, True) for k in rest], "couple_rest", [filled])
    for k, unit in zip(rest, units):
        beyond[k] = along_z(unit, k)
    return pl.pallas_call(
        finish_kernel,
        out_shape=jax.ShapeDtypeStruct((mono_dev, basis, basis), jnp.float32),
        in_specs=[IN_VMEM] * (1 + lanes),
        out_specs=IN_VMEM,
        compiler_params=small,
        name="finish",
    )(h_core, own, *[beyond[k] for k in range(1, lanes)])


def solution(mesh):
    return jax.shard_map(
        local,
        mesh=mesh,
        in_specs=(
            P(("job", "gddi", "intra"), None, None),
            P(("job", "gddi", "intra"), None, None),
            P(("job", "gddi"), "intra", None, None),
            P("job", None),
        ),
        out_specs=P(("job", "gddi", "intra"), None, None),
        check_vma=False,
    )
```

```python
import functools

import jax
import jax.numpy as jnp
from jax import lax
from jax.experimental import pallas as pl
from jax.experimental.pallas import tpu as pltpu
from jax.sharding import PartitionSpec as P

STEPS = 32.0
TOP = 32000.0
SHRINK = 1.0 / 16.0
IN_VMEM = pl.BlockSpec(memory_space=pltpu.VMEM)
IN_SMEM = pl.BlockSpec(memory_space=pltpu.SMEM)


def xor_pairs(size, k):
    return [(i, i ^ k) for i in range(size)]


def round_up(n, to):
    return -(-n // to) * to


def transposed_dot(a, b):
    return lax.dot_general(a, b, (((1,), (1,)), ((), ())), preferred_element_type=jnp.float32)


def square_iotas(half):
    row = lax.broadcasted_iota(jnp.int32, (half, half), 0)
    col = lax.broadcasted_iota(jnp.int32, (half, half), 1)
    return row, col


def fold(first, second):
    row, col = square_iotas(first.shape[0])
    mixed = jnp.where(row <= col, first, second)
    diag = jnp.sum(jnp.where(row == col, second, 0.0), axis=0, keepdims=True)
    return mixed, diag


def unfold(mixed, diag):
    row, col = square_iotas(mixed.shape[0])
    turned = mixed.T
    first = jnp.where(row <= col, mixed, turned)
    second = jnp.where(row > col, mixed, jnp.where(row < col, turned, diag))
    return first, second


def scale_code(peak):
    wanted = jnp.log(jnp.maximum(peak * SHRINK, 2.0**-120)) * STEPS
    return jnp.floor(wanted + 1.5).astype(jnp.int32)


def encode(x, code):
    units = jnp.exp(code.astype(jnp.float32) * (-1.0 / STEPS)) * TOP
    return jnp.floor(x * SHRINK * units + 0.5).astype(jnp.int32)


def decode(q, code):
    units = jnp.exp(code.astype(jnp.float32) * (1.0 / STEPS)) * (1.0 / TOP)
    return q.astype(jnp.float32) * units * (1.0 / SHRINK)


def pack(high, low):
    return lax.shift_left(high, 16) | (low & 0xFFFF)


def unpack(word):
    return lax.shift_right_arithmetic(word, 16), lax.shift_right_arithmetic(lax.shift_left(word, 16), 16)


def peak_of(x):
    return jnp.max(jnp.abs(x), axis=0, keepdims=True)


def fold_kernel(dens_ref, out_ref):
    mono_dev, basis, _ = dens_ref.shape
    half = basis // 2
    diags = []
    for m in range(mono_dev):
        out_ref[pl.ds(m * basis, half)] = dens_ref[m, :half, half:]
        mixed, diag = fold(
            dens_ref[m, :half, :half].astype(jnp.float32), dens_ref[m, half:, half:].astype(jnp.float32)
        )
        out_ref[pl.ds(m * basis + half, half)] = mixed.astype(out_ref.dtype)
        diags.append(diag)
    rows = out_ref.shape[0] - mono_dev * basis
    row = lax.broadcasted_iota(jnp.int32, (rows, half), 0)
    tail = jnp.zeros((rows, half), jnp.float32)
    for m in range(mono_dev):
        tail = jnp.where(row == m, diags[m], tail)
    out_ref[pl.ds(mono_dev * basis, rows)] = tail.astype(out_ref.dtype)


def gate_kernel(piece_ref, *refs):
    refs[-1][...] = piece_ref[...]


def stage_kernel(nbr_ref, esp_ref, piece_ref, *refs):
    nbr_out, esp_out, piece_out, sems = refs[-4:]
    copies = [
        pltpu.make_async_copy(esp_ref, esp_out, sems.at[0]),
        pltpu.make_async_copy(nbr_ref, nbr_out, sems.at[1]),
    ]
    for copy in copies:
        copy.start()
    piece_out[...] = piece_ref[...]
    for copy in copies:
        copy.wait()


def couple_kernel(groups, lanes, mono_dev, units, nbr_ref, esp_ref, *refs):
    outs = refs[len(refs) - len(units) :]
    if len(refs) > len(units) + 1:
        pieces, store = refs[: -1 - len(units)], refs[-1 - len(units)]
        for i, piece in enumerate(pieces):
            store[i] = piece[...]
    else:
        store = refs[0]
    my_group = lax.axis_index("gddi")
    my_lane = lax.axis_index("intra")
    _, slot_dev, basis, _ = esp_ref.shape
    mono_grp = mono_dev * lanes
    half = basis // 2
    tail_rows = store.shape[1] - mono_dev * basis

    def near_density(fragment):
        apart = (fragment // mono_grp) ^ my_group
        lane = ((fragment % mono_grp) // mono_dev) ^ my_lane
        place = ((apart & 1) * (groups // 2) + (apart >> 1)) * lanes + lane
        member = fragment % mono_dev
        start = pl.multiple_of(member * basis, basis)
        off = store[place, pl.ds(start, half)]
        mixed = store[place, pl.ds(start + half, half)].astype(jnp.float32)
        tail = store[place, pl.ds(mono_dev * basis, tail_rows)].astype(jnp.float32)
        row = lax.broadcasted_iota(jnp.int32, (tail_rows, half), 0)
        diag = jnp.sum(jnp.where(row == member, tail, 0.0), axis=0, keepdims=True)
        first, second = unfold(mixed, diag)
        top = jnp.concatenate([first.astype(off.dtype), off], axis=1)
        bottom = jnp.concatenate([off.T, second.astype(off.dtype)], axis=1)
        return jnp.concatenate([top, bottom], axis=0)

    def partial_of(fragment):
        high, low, blocks = [], [], []
        for s in range(slot_dev):
            name = nbr_ref[my_lane * slot_dev + s, my_group * mono_grp + fragment]
            block = esp_ref[fragment, s]
            half_term = jnp.dot(block, near_density(name), preferred_element_type=jnp.float32)
            high.append(half_term.astype(jnp.bfloat16))
            low.append((half_term - high[-1].astype(jnp.float32)).astype(jnp.bfloat16))
            blocks.append(block)
        both = jnp.concatenate([jnp.concatenate(high, axis=1), jnp.concatenate(low, axis=1)], axis=0)
        both = transposed_dot(both, jnp.concatenate(blocks, axis=1))
        total = both[:basis] + both[basis:]
        mixed, diag = fold(total[:half, :half], total[half:, half:])
        return total[:half, half:], mixed, diag

    for (k, coded), out in zip(units, outs):
        write = write_coded if coded else write_plain
        write(out, [partial_of((my_lane ^ k) * mono_dev + m) for m in range(mono_dev)])


def write_plain(out, parts):
    half = out.shape[2]
    for m, (off, mixed, diag) in enumerate(parts):
        out[m, :half] = off
        out[m, half : 2 * half] = mixed
        out[m, 2 * half :] = jnp.broadcast_to(diag, (8, half))


def read_plain(ref, m):
    half = ref.shape[2]
    return ref[m, :half], ref[m, half : 2 * half], ref[m, 2 * half : 2 * half + 1]


def write_coded(out, parts):
    half = out.shape[1]
    tail = []
    for m, (off, mixed, diag) in enumerate(parts):
        off_code = scale_code(peak_of(off))
        mixed_code = scale_code(jnp.maximum(peak_of(mixed), jnp.abs(diag)))
        out[pl.ds(m * half, half)] = pack(encode(off, off_code), encode(mixed, mixed_code))
        tail += [pack(off_code, mixed_code), encode(diag, mixed_code)]
    row = lax.broadcasted_iota(jnp.int32, (out.shape[0] - len(parts) * half, half), 0)
    last = jnp.zeros(row.shape, jnp.int32)
    for i, values in enumerate(tail):
        last = jnp.where(row == i, values, last)
    out[pl.ds(len(parts) * half, row.shape[0])] = last


def read_coded(ref, m, mono_dev):
    half = ref.shape[1]
    tail = mono_dev * half + 2 * m
    off_code, mixed_code = unpack(ref[tail : tail + 1])
    off_q, mixed_q = unpack(ref[m * half : (m + 1) * half])
    return decode(off_q, off_code), decode(mixed_q, mixed_code), decode(ref[tail + 1 : tail + 2], mixed_code)


def summed(plain_ref, coded_refs, m):
    total = read_plain(plain_ref, m)
    for ref in coded_refs:
        total = [a + b for a, b in zip(total, read_coded(ref, m, plain_ref.shape[0]))]
    return total


def finish_kernel(core_ref, own_ref, *refs):
    parts, out_ref = refs[:-1], refs[-1]
    mono_dev, basis, _ = out_ref.shape
    half = basis // 2
    for m in range(mono_dev):
        off, mixed, diag = summed(own_ref, parts, m)
        first, second = unfold(mixed, diag)
        core = core_ref[m].astype(jnp.float32)
        out_ref[m, :half, :half] = core[:half, :half] + first
        out_ref[m, :half, half:] = core[:half, half:] + off
        out_ref[m, half:, :half] = core[half:, :half] + off.T
        out_ref[m, half:, half:] = core[half:, half:] + second


def local(density, h_core, esp_block, nbr):
    groups = lax.axis_size("gddi")
    lanes = lax.axis_size("intra")
    mono_dev, basis = density.shape[0], density.shape[1]
    half = basis // 2
    hbm = pl.BlockSpec(memory_space=pl.ANY)
    small = pltpu.CompilerParams(vmem_limit_bytes=8 * 2**20)

    rows = mono_dev * basis + round_up(mono_dev, 16)
    shard = pl.pallas_call(
        fold_kernel,
        out_shape=pltpu.VMEM((rows, half), density.dtype),
        in_specs=[IN_VMEM],
        out_specs=IN_VMEM,
        compiler_params=small,
        name="fold",
    )(density)
    def along_z(piece, bit):
        return lax.ppermute(piece, "intra", xor_pairs(lanes, bit))

    def along_y(piece, y):
        return lax.ppermute(piece, "gddi", xor_pairs(groups, 2 * y))

    rows_y = groups // 2
    top = lanes // 2
    near = {(0, 0): shard, (0, top): along_z(shard, top)}

    def double(start):
        bit = top // 2
        while bit:
            for k in range(start, start + top):
                if (0, k) in near and (0, k ^ bit) not in near:
                    near[0, k ^ bit] = along_z(near[0, k], bit)
            bit //= 2

    double(0)
    for y in range(1, rows_y):
        near[y, 0] = along_y(shard, y)

    def gate(piece, *after):
        return pl.pallas_call(
            gate_kernel,
            out_shape=pltpu.VMEM(piece.shape, piece.dtype),
            in_specs=[IN_VMEM] + [hbm] * len(after),
            out_specs=IN_VMEM,
            compiler_params=small,
            name="gate",
        )(piece, *after)

    others = [piece for key, piece in near.items() if key != (0, top)]
    near[0, top] = gate(gate(near[0, top]), *others)
    double(top)
    for y in range(1, rows_y):
        for k in range(1, top):
            near[y, k] = along_z(near[y, k & (k - 1)], k & -k)
        for k in range(top, lanes):
            near[y, k] = along_y(near[0, k], y)

    names, blocks, near[rows_y - 1, 0] = pl.pallas_call(
        stage_kernel,
        out_shape=[
            pltpu.SMEM((nbr.shape[1], nbr.shape[0]), nbr.dtype),
            pltpu.VMEM(esp_block.shape, esp_block.dtype),
            pltpu.VMEM(shard.shape, shard.dtype),
        ],
        in_specs=[hbm, hbm, IN_VMEM, hbm],
        out_specs=[IN_SMEM, IN_VMEM, IN_VMEM],
        scratch_shapes=[pltpu.SemaphoreType.DMA((2,))],
        compiler_params=small,
        name="stage",
    )(
        pltpu.with_memory_space_constraint(nbr.T, pltpu.HBM),
        pltpu.with_memory_space_constraint(esp_block, pltpu.HBM),
        near[rows_y - 1, 0],
        near[0, lanes - 1],
    )
    keys = [(y, k) for y in range(rows_y) for k in range(lanes)]
    mine = [near[key] for key in keys]
    pieces = mine + [lax.ppermute(piece, "gddi", xor_pairs(groups, 1)) for piece in mine]

    plain = pltpu.VMEM((mono_dev, basis + 8, half), jnp.float32)
    coded = pltpu.VMEM((mono_dev * half + round_up(2 * mono_dev, 8), half), jnp.int32)
    piece_bytes = groups * lanes * rows * half * 2

    keep = pltpu.VMEM if piece_bytes <= 4 * 2**20 else jax.ShapeDtypeStruct
    store = keep((groups * lanes, rows, half), density.dtype)

    def couple(units, name, pieces, fill=False):
        return pl.pallas_call(
            functools.partial(couple_kernel, groups, lanes, mono_dev, units),
            out_shape=[store] * fill + [coded if is_coded else plain for _, is_coded in units],
            in_specs=[IN_SMEM] + [IN_VMEM] * (1 + len(pieces)),
            out_specs=[IN_VMEM] * (fill + len(units)),
            compiler_params=pltpu.CompilerParams(
                vmem_limit_bytes=2 * (piece_bytes + esp_block.size * 2) + 8 * 2**20
            ),
            name=name,
        )(names, blocks, *pieces)

    order = sorted(range(1, lanes), key=lambda k: (k < top, -k))
    filled, unit = couple([(order[0], True)], "couple_first", pieces, fill=True)
    beyond = {order[0]: along_z(unit, order[0])}
    units = couple([(k, True) for k in order[1:]], "couple_second", [filled])
    for k, unit in zip(order[1:], units):
        beyond[k] = along_z(unit, k)
    (own,) = couple([(0, False)], "couple_own", [filled])
    for k, n in zip(order, (5, 1)):
        for _ in range(n):
            beyond[k] = gate(beyond[k])
    return pl.pallas_call(
        finish_kernel,
        out_shape=jax.ShapeDtypeStruct((mono_dev, basis, basis), jnp.float32),
        in_specs=[IN_VMEM] * (1 + lanes),
        out_specs=IN_VMEM,
        compiler_params=small,
        name="finish",
    )(h_core, own, *[beyond[k] for k in range(1, lanes)])


def solution(mesh):
    return jax.shard_map(
        local,
        mesh=mesh,
        in_specs=(
            P(("job", "gddi", "intra"), None, None),
            P(("job", "gddi", "intra"), None, None),
            P(("job", "gddi"), "intra", None, None),
            P("job", None),
        ),
        out_specs=P(("job", "gddi", "intra"), None, None),
        check_vma=False,
    )
```

```python
import functools

import jax
import jax.numpy as jnp
from jax import lax
from jax.experimental import pallas as pl
from jax.experimental.pallas import tpu as pltpu
from jax.sharding import PartitionSpec as P

STEPS = 32.0
TOP = 32000.0
SHRINK = 1.0 / 16.0
IN_VMEM = pl.BlockSpec(memory_space=pltpu.VMEM)
IN_SMEM = pl.BlockSpec(memory_space=pltpu.SMEM)


def xor_pairs(size, k):
    return [(i, i ^ k) for i in range(size)]


def round_up(n, to):
    return -(-n // to) * to


def transposed_dot(a, b):
    return lax.dot_general(a, b, (((1,), (1,)), ((), ())), preferred_element_type=jnp.float32)


def square_iotas(half):
    row = lax.broadcasted_iota(jnp.int32, (half, half), 0)
    col = lax.broadcasted_iota(jnp.int32, (half, half), 1)
    return row, col


def fold(first, second):
    row, col = square_iotas(first.shape[0])
    mixed = jnp.where(row <= col, first, second)
    diag = jnp.sum(jnp.where(row == col, second, 0.0), axis=0, keepdims=True)
    return mixed, diag


def unfold(mixed, diag):
    row, col = square_iotas(mixed.shape[0])
    turned = mixed.T
    first = jnp.where(row <= col, mixed, turned)
    second = jnp.where(row > col, mixed, jnp.where(row < col, turned, diag))
    return first, second


def scale_code(peak):
    wanted = jnp.log(jnp.maximum(peak * SHRINK, 2.0**-120)) * STEPS
    return jnp.floor(wanted + 1.5).astype(jnp.int32)


def encode(x, code):
    units = jnp.exp(code.astype(jnp.float32) * (-1.0 / STEPS)) * TOP
    return jnp.floor(x * SHRINK * units + 0.5).astype(jnp.int32)


def decode(q, code):
    units = jnp.exp(code.astype(jnp.float32) * (1.0 / STEPS)) * (1.0 / TOP)
    return q.astype(jnp.float32) * units * (1.0 / SHRINK)


def pack(high, low):
    return lax.shift_left(high, 16) | (low & 0xFFFF)


def unpack(word):
    return lax.shift_right_arithmetic(word, 16), lax.shift_right_arithmetic(lax.shift_left(word, 16), 16)


def peak_of(x):
    return jnp.max(jnp.abs(x), axis=0, keepdims=True)


def fold_kernel(dens_ref, out_ref):
    mono_dev, basis, _ = dens_ref.shape
    half = basis // 2
    diags = []
    for m in range(mono_dev):
        out_ref[pl.ds(m * basis, half)] = dens_ref[m, :half, half:]
        mixed, diag = fold(
            dens_ref[m, :half, :half].astype(jnp.float32), dens_ref[m, half:, half:].astype(jnp.float32)
        )
        out_ref[pl.ds(m * basis + half, half)] = mixed.astype(out_ref.dtype)
        diags.append(diag)
    rows = out_ref.shape[0] - mono_dev * basis
    row = lax.broadcasted_iota(jnp.int32, (rows, half), 0)
    tail = jnp.zeros((rows, half), jnp.float32)
    for m in range(mono_dev):
        tail = jnp.where(row == m, diags[m], tail)
    out_ref[pl.ds(mono_dev * basis, rows)] = tail.astype(out_ref.dtype)


def gate_kernel(piece_ref, *refs):
    refs[-1][...] = piece_ref[...]


def stage_kernel(nbr_ref, esp_ref, piece_ref, *refs):
    nbr_out, esp_out, piece_out, sems = refs[-4:]
    copies = [
        pltpu.make_async_copy(esp_ref, esp_out, sems.at[0]),
        pltpu.make_async_copy(nbr_ref, nbr_out, sems.at[1]),
    ]
    for copy in copies:
        copy.start()
    piece_out[...] = piece_ref[...]
    for copy in copies:
        copy.wait()


def couple_kernel(groups, lanes, mono_dev, units, nbr_ref, esp_ref, *refs):
    outs = refs[len(refs) - len(units) :]
    if len(refs) > len(units) + 1:
        pieces, store = refs[: -1 - len(units)], refs[-1 - len(units)]
        for i, piece in enumerate(pieces):
            store[i] = piece[...]
    else:
        store = refs[0]
    my_group = lax.axis_index("gddi")
    my_lane = lax.axis_index("intra")
    _, slot_dev, basis, _ = esp_ref.shape
    mono_grp = mono_dev * lanes
    half = basis // 2
    tail_rows = store.shape[1] - mono_dev * basis

    def near_density(fragment):
        apart = (fragment // mono_grp) ^ my_group
        lane = ((fragment % mono_grp) // mono_dev) ^ my_lane
        place = ((apart & 1) * (groups // 2) + (apart >> 1)) * lanes + lane
        member = fragment % mono_dev
        start = pl.multiple_of(member * basis, basis)
        off = store[place, pl.ds(start, half)]
        mixed = store[place, pl.ds(start + half, half)].astype(jnp.float32)
        tail = store[place, pl.ds(mono_dev * basis, tail_rows)].astype(jnp.float32)
        row = lax.broadcasted_iota(jnp.int32, (tail_rows, half), 0)
        diag = jnp.sum(jnp.where(row == member, tail, 0.0), axis=0, keepdims=True)
        first, second = unfold(mixed, diag)
        top = jnp.concatenate([first.astype(off.dtype), off], axis=1)
        bottom = jnp.concatenate([off.T, second.astype(off.dtype)], axis=1)
        return jnp.concatenate([top, bottom], axis=0)

    def partial_of(fragment):
        high, low, blocks = [], [], []
        for s in range(slot_dev):
            name = nbr_ref[my_lane * slot_dev + s, my_group * mono_grp + fragment]
            block = esp_ref[fragment, s]
            half_term = jnp.dot(block, near_density(name), preferred_element_type=jnp.float32)
            high.append(half_term.astype(jnp.bfloat16))
            low.append((half_term - high[-1].astype(jnp.float32)).astype(jnp.bfloat16))
            blocks.append(block)
        both = jnp.concatenate([jnp.concatenate(high, axis=1), jnp.concatenate(low, axis=1)], axis=0)
        both = transposed_dot(both, jnp.concatenate(blocks, axis=1))
        total = both[:basis] + both[basis:]
        mixed, diag = fold(total[:half, :half], total[half:, half:])
        return total[:half, half:], mixed, diag

    for (k, coded, members), out in zip(units, outs):
        write = write_coded if coded else write_plain
        write(out, [partial_of((my_lane ^ k) * mono_dev + m) for m in members])


def write_plain(out, parts):
    half = out.shape[2]
    for m, (off, mixed, diag) in enumerate(parts):
        out[m, :half] = off
        out[m, half : 2 * half] = mixed
        out[m, 2 * half :] = jnp.broadcast_to(diag, (8, half))


def read_plain(ref, m):
    half = ref.shape[2]
    return ref[m, :half], ref[m, half : 2 * half], ref[m, 2 * half : 2 * half + 1]


def write_coded(out, parts):
    half = out.shape[1]
    tail = []
    for m, (off, mixed, diag) in enumerate(parts):
        off_code = scale_code(peak_of(off))
        mixed_code = scale_code(jnp.maximum(peak_of(mixed), jnp.abs(diag)))
        out[pl.ds(m * half, half)] = pack(encode(off, off_code), encode(mixed, mixed_code))
        tail += [pack(off_code, mixed_code), encode(diag, mixed_code)]
    row = lax.broadcasted_iota(jnp.int32, (out.shape[0] - len(parts) * half, half), 0)
    last = jnp.zeros(row.shape, jnp.int32)
    for i, values in enumerate(tail):
        last = jnp.where(row == i, values, last)
    out[pl.ds(len(parts) * half, row.shape[0])] = last


def read_coded(ref, m, count):
    half = ref.shape[1]
    tail = count * half + 2 * m
    off_code, mixed_code = unpack(ref[tail : tail + 1])
    off_q, mixed_q = unpack(ref[m * half : (m + 1) * half])
    return decode(off_q, off_code), decode(mixed_q, mixed_code), decode(ref[tail + 1 : tail + 2], mixed_code)


def merge_kernel(plain_ref, *refs):
    count = plain_ref.shape[0]
    sums = []
    for m in range(count):
        total = read_plain(plain_ref, m)
        for ref in refs[:-2]:
            total = [a + b for a, b in zip(total, read_coded(ref, m, count))]
        sums.append(total)
    write_coded(refs[-1], sums)


def finish_kernel(members, core_ref, own_ref, *refs):
    parts, out_ref = refs[:-1], refs[-1]
    mono_dev, basis, _ = out_ref.shape
    half = basis // 2
    for m in range(mono_dev):
        total = read_plain(own_ref, m)
        for part, held in zip(parts, members):
            if m in held:
                total = [a + b for a, b in zip(total, read_coded(part, held.index(m), len(held)))]
        off, mixed, diag = total
        first, second = unfold(mixed, diag)
        core = core_ref[m].astype(jnp.float32)
        out_ref[m, :half, :half] = core[:half, :half] + first
        out_ref[m, :half, half:] = core[:half, half:] + off
        out_ref[m, half:, :half] = core[half:, :half] + off.T
        out_ref[m, half:, half:] = core[half:, half:] + second


def local(density, h_core, esp_block, nbr):
    groups = lax.axis_size("gddi")
    lanes = lax.axis_size("intra")
    mono_dev, basis = density.shape[0], density.shape[1]
    half = basis // 2
    hbm = pl.BlockSpec(memory_space=pl.ANY)
    small = pltpu.CompilerParams(vmem_limit_bytes=8 * 2**20)

    rows = mono_dev * basis + round_up(mono_dev, 16)
    shard = pl.pallas_call(
        fold_kernel,
        out_shape=pltpu.VMEM((rows, half), density.dtype),
        in_specs=[IN_VMEM],
        out_specs=IN_VMEM,
        compiler_params=small,
        name="fold",
    )(density)
    def along_z(piece, bit):
        return lax.ppermute(piece, "intra", xor_pairs(lanes, bit))

    def along_y(piece, y):
        return lax.ppermute(piece, "gddi", xor_pairs(groups, 2 * y))

    rows_y = groups // 2
    top = lanes // 2
    near = {(0, 0): shard, (0, top): along_z(shard, top)}

    def double(start):
        bit = top // 2
        while bit:
            for k in range(start, start + top):
                if (0, k) in near and (0, k ^ bit) not in near:
                    near[0, k ^ bit] = along_z(near[0, k], bit)
            bit //= 2

    double(0)
    for y in range(1, rows_y):
        near[y, 0] = along_y(shard, y)

    def gate(piece, *after):
        return pl.pallas_call(
            gate_kernel,
            out_shape=pltpu.VMEM(piece.shape, piece.dtype),
            in_specs=[IN_VMEM] + [hbm] * len(after),
            out_specs=IN_VMEM,
            compiler_params=small,
            name="gate",
        )(piece, *after)

    others = [piece for key, piece in near.items() if key != (0, top)]
    near[0, top] = gate(gate(near[0, top]), *others)
    double(top)
    for y in range(1, rows_y):
        for k in range(1, top):
            near[y, k] = along_z(near[y, k & (k - 1)], k & -k)
        for k in range(top, lanes):
            near[y, k] = along_y(near[0, k], y)

    names, blocks, near[rows_y - 1, 0] = pl.pallas_call(
        stage_kernel,
        out_shape=[
            pltpu.SMEM((nbr.shape[1], nbr.shape[0]), nbr.dtype),
            pltpu.VMEM(esp_block.shape, esp_block.dtype),
            pltpu.VMEM(shard.shape, shard.dtype),
        ],
        in_specs=[hbm, hbm, IN_VMEM, hbm],
        out_specs=[IN_SMEM, IN_VMEM, IN_VMEM],
        scratch_shapes=[pltpu.SemaphoreType.DMA((2,))],
        compiler_params=small,
        name="stage",
    )(
        pltpu.with_memory_space_constraint(nbr.T, pltpu.HBM),
        pltpu.with_memory_space_constraint(esp_block, pltpu.HBM),
        near[rows_y - 1, 0],
        near[0, lanes - 1],
    )
    keys = [(y, k) for y in range(rows_y) for k in range(lanes)]
    mine = [near[key] for key in keys]
    pieces = mine + [lax.ppermute(piece, "gddi", xor_pairs(groups, 1)) for piece in mine]

    def plain(count):
        return pltpu.VMEM((count, basis + 8, half), jnp.float32)

    def coded(count):
        return pltpu.VMEM((count * half + round_up(2 * count, 8), half), jnp.int32)

    piece_bytes = groups * lanes * rows * half * 2

    keep = pltpu.VMEM if piece_bytes <= 4 * 2**20 else jax.ShapeDtypeStruct
    store = keep((groups * lanes, rows, half), density.dtype)

    def couple(units, name, pieces, fill=False):
        return pl.pallas_call(
            functools.partial(couple_kernel, groups, lanes, mono_dev, units),
            out_shape=[store] * fill + [(coded if is_coded else plain)(len(members)) for _, is_coded, members in units],
            in_specs=[IN_SMEM] + [IN_VMEM] * (1 + len(pieces)),
            out_specs=[IN_VMEM] * (fill + len(units)),
            compiler_params=pltpu.CompilerParams(
                vmem_limit_bytes=2 * (piece_bytes + esp_block.size * 2) + 8 * 2**20
            ),
            name=name,
        )(names, blocks, *pieces)

    everyone = list(range(mono_dev))
    direct, relayed = everyone[: mono_dev // 2], everyone[mono_dev // 2 :]
    steps = range(1, top)
    filled, across, *relays = couple(
        [(top, True, direct)] + [(top ^ k, True, relayed) for k in steps], "couple_first", pieces, fill=True
    )
    relays = [along_z(unit, k) for k, unit in zip(steps, relays)]
    across = along_z(across, top)
    units = couple(
        [(top, False, relayed)] + [(top ^ k, True, direct) for k in steps] + [(k, True, everyone) for k in steps],
        "couple_second",
        [filled],
    )
    merged = pl.pallas_call(
        merge_kernel,
        out_shape=coded(len(relayed)),
        in_specs=[IN_VMEM] * (1 + len(relays)) + [hbm],
        out_specs=IN_VMEM,
        compiler_params=small,
        name="merge",
    )(units[0], *relays, across)
    merged = along_z(merged, top)
    far = [along_z(unit, top ^ k) for k, unit in zip(steps, units[1:top])]
    close = [along_z(unit, k) for k, unit in zip(steps, units[top:])]
    (own,) = couple([(0, False, everyone)], "couple_own", [filled])
    terms = [(across, direct), (merged, relayed)] + [(x, direct) for x in far] + [(x, everyone) for x in close]
    return pl.pallas_call(
        functools.partial(finish_kernel, [held for _, held in terms]),
        out_shape=jax.ShapeDtypeStruct((mono_dev, basis, basis), jnp.float32),
        in_specs=[IN_VMEM] * (2 + len(terms)),
        out_specs=IN_VMEM,
        compiler_params=small,
        name="finish",
    )(h_core, own, *[unit for unit, _ in terms])


def solution(mesh):
    return jax.shard_map(
        local,
        mesh=mesh,
        in_specs=(
            P(("job", "gddi", "intra"), None, None),
            P(("job", "gddi", "intra"), None, None),
            P(("job", "gddi"), "intra", None, None),
            P("job", None),
        ),
        out_specs=P(("job", "gddi", "intra"), None, None),
        check_vma=False,
    )
```

```python
import functools

import jax
import jax.numpy as jnp
from jax import lax
from jax.experimental import pallas as pl
from jax.experimental.pallas import tpu as pltpu
from jax.sharding import PartitionSpec as P

STEPS = 32.0
TOP = 32000.0
SHRINK = 1.0 / 16.0
IN_VMEM = pl.BlockSpec(memory_space=pltpu.VMEM)
IN_SMEM = pl.BlockSpec(memory_space=pltpu.SMEM)


def xor_pairs(size, k):
    return [(i, i ^ k) for i in range(size)]


def round_up(n, to):
    return -(-n // to) * to


def transposed_dot(a, b):
    return lax.dot_general(a, b, (((1,), (1,)), ((), ())), preferred_element_type=jnp.float32)


def square_iotas(half):
    row = lax.broadcasted_iota(jnp.int32, (half, half), 0)
    col = lax.broadcasted_iota(jnp.int32, (half, half), 1)
    return row, col


def fold(first, second):
    row, col = square_iotas(first.shape[0])
    mixed = jnp.where(row <= col, first, second)
    diag = jnp.sum(jnp.where(row == col, second, 0.0), axis=0, keepdims=True)
    return mixed, diag


def unfold(mixed, diag):
    row, col = square_iotas(mixed.shape[0])
    turned = mixed.T
    first = jnp.where(row <= col, mixed, turned)
    second = jnp.where(row > col, mixed, jnp.where(row < col, turned, diag))
    return first, second


def scale_code(peak):
    wanted = jnp.log(jnp.maximum(peak * SHRINK, 2.0**-120)) * STEPS
    return jnp.floor(wanted + 1.5).astype(jnp.int32)


def encode(x, code):
    units = jnp.exp(code.astype(jnp.float32) * (-1.0 / STEPS)) * TOP
    return jnp.floor(x * SHRINK * units + 0.5).astype(jnp.int32)


def decode(q, code):
    units = jnp.exp(code.astype(jnp.float32) * (1.0 / STEPS)) * (1.0 / TOP)
    return q.astype(jnp.float32) * units * (1.0 / SHRINK)


def pack(high, low):
    return lax.shift_left(high, 16) | (low & 0xFFFF)


def unpack(word):
    return lax.shift_right_arithmetic(word, 16), lax.shift_right_arithmetic(lax.shift_left(word, 16), 16)


def peak_of(x):
    return jnp.max(jnp.abs(x), axis=0, keepdims=True)


def fold_kernel(dens_ref, out_ref):
    mono_dev, basis, _ = dens_ref.shape
    half = basis // 2
    diags = []
    for m in range(mono_dev):
        out_ref[pl.ds(m * basis, half)] = dens_ref[m, :half, half:]
        mixed, diag = fold(
            dens_ref[m, :half, :half].astype(jnp.float32), dens_ref[m, half:, half:].astype(jnp.float32)
        )
        out_ref[pl.ds(m * basis + half, half)] = mixed.astype(out_ref.dtype)
        diags.append(diag)
    rows = out_ref.shape[0] - mono_dev * basis
    row = lax.broadcasted_iota(jnp.int32, (rows, half), 0)
    tail = jnp.zeros((rows, half), jnp.float32)
    for m in range(mono_dev):
        tail = jnp.where(row == m, diags[m], tail)
    out_ref[pl.ds(mono_dev * basis, rows)] = tail.astype(out_ref.dtype)


def gate_kernel(piece_ref, *refs):
    refs[-1][...] = piece_ref[...]


def gather_kernel(*refs):
    for i, piece in enumerate(refs[:-1]):
        refs[-1][i] = piece[...]


def stage_kernel(nbr_ref, esp_ref, piece_ref, nbr_out, esp_out, piece_out, sems):
    copies = [
        pltpu.make_async_copy(esp_ref, esp_out, sems.at[0]),
        pltpu.make_async_copy(nbr_ref, nbr_out, sems.at[1]),
    ]
    for copy in copies:
        copy.start()
    piece_out[...] = piece_ref[...]
    for copy in copies:
        copy.wait()


def couple_kernel(groups, lanes, mono_dev, units, places, nbr_ref, esp_ref, *refs):
    outs = refs[len(refs) - len(units) :]
    if len(refs) > len(units) + 1:
        pieces, store = refs[: -1 - len(units)], refs[-1 - len(units)]
        at = 0
        for piece in pieces:
            for part in [piece] if len(piece.shape) == 2 else [piece.at[i] for i in range(piece.shape[0])]:
                store[places[at]] = part[...]
                at += 1
    else:
        store = refs[0]
    my_group = lax.axis_index("gddi")
    my_lane = lax.axis_index("intra")
    _, slot_dev, basis, _ = esp_ref.shape
    mono_grp = mono_dev * lanes
    half = basis // 2
    tail_rows = store.shape[1] - mono_dev * basis

    def near_density(fragment):
        apart = (fragment // mono_grp) ^ my_group
        lane = ((fragment % mono_grp) // mono_dev) ^ my_lane
        place = ((apart & 1) * (groups // 2) + (apart >> 1)) * lanes + lane
        member = fragment % mono_dev
        start = pl.multiple_of(member * basis, basis)
        off = store[place, pl.ds(start, half)]
        mixed = store[place, pl.ds(start + half, half)].astype(jnp.float32)
        tail = store[place, pl.ds(mono_dev * basis, tail_rows)].astype(jnp.float32)
        row = lax.broadcasted_iota(jnp.int32, (tail_rows, half), 0)
        diag = jnp.sum(jnp.where(row == member, tail, 0.0), axis=0, keepdims=True)
        first, second = unfold(mixed, diag)
        top = jnp.concatenate([first.astype(off.dtype), off], axis=1)
        bottom = jnp.concatenate([off.T, second.astype(off.dtype)], axis=1)
        return jnp.concatenate([top, bottom], axis=0)

    def partial_of(fragment):
        high, low, blocks = [], [], []
        for s in range(slot_dev):
            name = nbr_ref[my_lane * slot_dev + s, my_group * mono_grp + fragment]
            block = esp_ref[fragment, s]
            half_term = jnp.dot(block, near_density(name), preferred_element_type=jnp.float32)
            high.append(half_term.astype(jnp.bfloat16))
            low.append((half_term - high[-1].astype(jnp.float32)).astype(jnp.bfloat16))
            blocks.append(block)
        both = jnp.concatenate([jnp.concatenate(high, axis=1), jnp.concatenate(low, axis=1)], axis=0)
        both = transposed_dot(both, jnp.concatenate(blocks, axis=1))
        total = both[:basis] + both[basis:]
        mixed, diag = fold(total[:half, :half], total[half:, half:])
        return total[:half, half:], mixed, diag

    for (k, coded), out in zip(units, outs):
        write = write_coded if coded else write_plain
        write(out, [partial_of((my_lane ^ k) * mono_dev + m) for m in range(mono_dev)])


def write_plain(out, parts):
    half = out.shape[2]
    for m, (off, mixed, diag) in enumerate(parts):
        out[m, :half] = off
        out[m, half : 2 * half] = mixed
        out[m, 2 * half :] = jnp.broadcast_to(diag, (8, half))


def read_plain(ref, m):
    half = ref.shape[2]
    return ref[m, :half], ref[m, half : 2 * half], ref[m, 2 * half : 2 * half + 1]


def write_coded(out, parts):
    half = out.shape[1]
    tail = []
    for m, (off, mixed, diag) in enumerate(parts):
        off_code = scale_code(peak_of(off))
        mixed_code = scale_code(jnp.maximum(peak_of(mixed), jnp.abs(diag)))
        out[pl.ds(m * half, half)] = pack(encode(off, off_code), encode(mixed, mixed_code))
        tail += [pack(off_code, mixed_code), encode(diag, mixed_code)]
    row = lax.broadcasted_iota(jnp.int32, (out.shape[0] - len(parts) * half, half), 0)
    last = jnp.zeros(row.shape, jnp.int32)
    for i, values in enumerate(tail):
        last = jnp.where(row == i, values, last)
    out[pl.ds(len(parts) * half, row.shape[0])] = last


def read_coded(ref, m, mono_dev):
    half = ref.shape[1]
    tail = mono_dev * half + 2 * m
    off_code, mixed_code = unpack(ref[tail : tail + 1])
    off_q, mixed_q = unpack(ref[m * half : (m + 1) * half])
    return decode(off_q, off_code), decode(mixed_q, mixed_code), decode(ref[tail + 1 : tail + 2], mixed_code)


def summed(plain_ref, coded_refs, m):
    total = read_plain(plain_ref, m)
    for ref in coded_refs:
        total = [a + b for a, b in zip(total, read_coded(ref, m, plain_ref.shape[0]))]
    return total


def finish_kernel(core_ref, own_ref, *refs):
    parts, out_ref = refs[:-1], refs[-1]
    mono_dev, basis, _ = out_ref.shape
    half = basis // 2
    for m in range(mono_dev):
        off, mixed, diag = summed(own_ref, parts, m)
        first, second = unfold(mixed, diag)
        core = core_ref[m].astype(jnp.float32)
        out_ref[m, :half, :half] = core[:half, :half] + first
        out_ref[m, :half, half:] = core[:half, half:] + off
        out_ref[m, half:, :half] = core[half:, :half] + off.T
        out_ref[m, half:, half:] = core[half:, half:] + second


def local(density, h_core, esp_block, nbr):
    groups = lax.axis_size("gddi")
    lanes = lax.axis_size("intra")
    mono_dev, basis = density.shape[0], density.shape[1]
    half = basis // 2
    hbm = pl.BlockSpec(memory_space=pl.ANY)
    small = pltpu.CompilerParams(vmem_limit_bytes=8 * 2**20)

    rows = mono_dev * basis + round_up(mono_dev, 16)
    shard = pl.pallas_call(
        fold_kernel,
        out_shape=pltpu.VMEM((rows, half), density.dtype),
        in_specs=[IN_VMEM],
        out_specs=IN_VMEM,
        compiler_params=small,
        name="fold",
    )(density)
    def along_z(piece, bit):
        return lax.ppermute(piece, "intra", xor_pairs(lanes, bit))

    def along_y(piece, y):
        return lax.ppermute(piece, "gddi", xor_pairs(groups, 2 * y))

    rows_y = groups // 2
    top = lanes // 2
    near = {(0, 0): shard, (0, top): along_z(shard, top)}

    def double(start):
        bit = top // 2
        while bit:
            for k in range(start, start + top):
                if (0, k) in near and (0, k ^ bit) not in near:
                    near[0, k ^ bit] = along_z(near[0, k], bit)
            bit //= 2

    double(0)
    for y in range(1, rows_y):
        near[y, 0] = along_y(shard, y)

    def gate(piece, *after):
        return pl.pallas_call(
            gate_kernel,
            out_shape=pltpu.VMEM(piece.shape, piece.dtype),
            in_specs=[IN_VMEM] + [hbm] * len(after),
            out_specs=IN_VMEM,
            compiler_params=small,
            name="gate",
        )(piece, *after)

    def across(piece, y, k):
        pairs = [(g * lanes + i, (g ^ 2 * y) * lanes + (i ^ k)) for g in range(groups) for i in range(lanes)]
        return lax.ppermute(piece, ("gddi", "intra"), pairs)

    others = [piece for key, piece in near.items() if key != (0, top)]
    near[0, top] = gate(gate(near[0, top]), *others)
    for y in range(1, rows_y):
        for k in range(1, top):
            near[y, k] = along_y(near[0, k], y)
            near[y, k] = gate(gate(near[y, k]))
    double(top)
    for y in range(1, rows_y):
        for k in range(top):
            near[y, top ^ k] = across(near[0, top], y, k)

    names, blocks, near[rows_y - 1, top - 1] = pl.pallas_call(
        stage_kernel,
        out_shape=[
            pltpu.SMEM((nbr.shape[1], nbr.shape[0]), nbr.dtype),
            pltpu.VMEM(esp_block.shape, esp_block.dtype),
            pltpu.VMEM(shard.shape, shard.dtype),
        ],
        in_specs=[hbm, hbm, IN_VMEM],
        out_specs=[IN_SMEM, IN_VMEM, IN_VMEM],
        scratch_shapes=[pltpu.SemaphoreType.DMA((2,))],
        compiler_params=small,
        name="stage",
    )(
        pltpu.with_memory_space_constraint(nbr.T, pltpu.HBM),
        pltpu.with_memory_space_constraint(esp_block, pltpu.HBM),
        near[rows_y - 1, top - 1],
    )
    def to_mate(piece):
        return lax.ppermute(piece, "gddi", xor_pairs(groups, 1))

    keys = [(y, k) for y in range(rows_y) for k in range(lanes)]
    batch = [key for key in keys if key[0] == 0 and bin(key[1]).count("1") <= 1]
    batched = pl.pallas_call(
        gather_kernel,
        out_shape=pltpu.VMEM((len(batch),) + shard.shape, shard.dtype),
        in_specs=[IN_VMEM] * len(batch),
        out_specs=IN_VMEM,
        compiler_params=small,
        name="gather",
    )(*[near[key] for key in batch])
    single = [key for key in keys if key not in batch]
    pieces = [near[key] for key in keys] + [to_mate(batched)] + [to_mate(near[key]) for key in single]
    for i, (y, k) in enumerate(single):
        if 0 < k < top:
            pieces[len(keys) + 1 + i] = gate(pieces[len(keys) + 1 + i])
    places = [y * lanes + k for y, k in keys]
    places += [rows_y * lanes + y * lanes + k for y, k in batch + single]

    plain = pltpu.VMEM((mono_dev, basis + 8, half), jnp.float32)
    coded = pltpu.VMEM((mono_dev * half + round_up(2 * mono_dev, 8), half), jnp.int32)
    piece_bytes = groups * lanes * rows * half * 2

    keep = pltpu.VMEM if piece_bytes <= 4 * 2**20 else jax.ShapeDtypeStruct
    store = keep((groups * lanes, rows, half), density.dtype)

    def couple(units, name, pieces, fill=False):
        return pl.pallas_call(
            functools.partial(couple_kernel, groups, lanes, mono_dev, units, places),
            out_shape=[store] * fill + [coded if is_coded else plain for _, is_coded in units],
            in_specs=[IN_SMEM] + [IN_VMEM] * (1 + len(pieces)),
            out_specs=[IN_VMEM] * (fill + len(units)),
            compiler_params=pltpu.CompilerParams(
                vmem_limit_bytes=2 * (piece_bytes + esp_block.size * 2) + 8 * 2**20
            ),
            name=name,
        )(names, blocks, *pieces)

    filled, beyond = couple([(top, True)], "couple_first", pieces, fill=True)
    beyond = {top: along_z(beyond, top)}
    for _ in range(5):
        beyond[top] = gate(beyond[top])
    rest = [k for k in range(1, lanes) if k != top]
    own, *units = couple([(0, False)] + [(k, True) for k in rest], "couple_rest", [filled])
    for k, unit in zip(rest, units):
        beyond[k] = along_z(unit, k)
    return pl.pallas_call(
        finish_kernel,
        out_shape=jax.ShapeDtypeStruct((mono_dev, basis, basis), jnp.float32),
        in_specs=[IN_VMEM] * (1 + lanes),
        out_specs=IN_VMEM,
        compiler_params=small,
        name="finish",
    )(h_core, own, *[beyond[k] for k in range(1, lanes)])


def solution(mesh):
    return jax.shard_map(
        local,
        mesh=mesh,
        in_specs=(
            P(("job", "gddi", "intra"), None, None),
            P(("job", "gddi", "intra"), None, None),
            P(("job", "gddi"), "intra", None, None),
            P("job", None),
        ),
        out_specs=P(("job", "gddi", "intra"), None, None),
        check_vma=False,
    )
```

```python
import functools

import jax
import jax.numpy as jnp
from jax import lax
from jax.experimental import pallas as pl
from jax.experimental.pallas import tpu as pltpu
from jax.sharding import PartitionSpec as P

STEPS = 32.0
TOP = 32000.0
SHRINK = 1.0 / 16.0
IN_VMEM = pl.BlockSpec(memory_space=pltpu.VMEM)
IN_SMEM = pl.BlockSpec(memory_space=pltpu.SMEM)


def xor_pairs(size, k):
    return [(i, i ^ k) for i in range(size)]


def round_up(n, to):
    return -(-n // to) * to


def transposed_dot(a, b):
    return lax.dot_general(a, b, (((1,), (1,)), ((), ())), preferred_element_type=jnp.float32)


def square_iotas(half):
    row = lax.broadcasted_iota(jnp.int32, (half, half), 0)
    col = lax.broadcasted_iota(jnp.int32, (half, half), 1)
    return row, col


def fold(first, second):
    row, col = square_iotas(first.shape[0])
    mixed = jnp.where(row <= col, first, second)
    diag = jnp.sum(jnp.where(row == col, second, 0.0), axis=0, keepdims=True)
    return mixed, diag


def unfold(mixed, diag):
    row, col = square_iotas(mixed.shape[0])
    turned = mixed.T
    first = jnp.where(row <= col, mixed, turned)
    second = jnp.where(row > col, mixed, jnp.where(row < col, turned, diag))
    return first, second


def scale_code(peak):
    wanted = jnp.log(jnp.maximum(peak * SHRINK, 2.0**-120)) * STEPS
    return jnp.floor(wanted + 1.5).astype(jnp.int32)


def encode(x, code):
    units = jnp.exp(code.astype(jnp.float32) * (-1.0 / STEPS)) * TOP
    return jnp.floor(x * SHRINK * units + 0.5).astype(jnp.int32)


def decode(q, code):
    units = jnp.exp(code.astype(jnp.float32) * (1.0 / STEPS)) * (1.0 / TOP)
    return q.astype(jnp.float32) * units * (1.0 / SHRINK)


def pack(high, low):
    return lax.shift_left(high, 16) | (low & 0xFFFF)


def unpack(word):
    return lax.shift_right_arithmetic(word, 16), lax.shift_right_arithmetic(lax.shift_left(word, 16), 16)


def peak_of(x):
    return jnp.max(jnp.abs(x), axis=0, keepdims=True)


def fold_kernel(dens_ref, out_ref):
    mono_dev, basis, _ = dens_ref.shape
    half = basis // 2
    diags = []
    for m in range(mono_dev):
        out_ref[pl.ds(m * basis, half)] = dens_ref[m, :half, half:]
        mixed, diag = fold(
            dens_ref[m, :half, :half].astype(jnp.float32), dens_ref[m, half:, half:].astype(jnp.float32)
        )
        out_ref[pl.ds(m * basis + half, half)] = mixed.astype(out_ref.dtype)
        diags.append(diag)
    rows = out_ref.shape[0] - mono_dev * basis
    row = lax.broadcasted_iota(jnp.int32, (rows, half), 0)
    tail = jnp.zeros((rows, half), jnp.float32)
    for m in range(mono_dev):
        tail = jnp.where(row == m, diags[m], tail)
    out_ref[pl.ds(mono_dev * basis, rows)] = tail.astype(out_ref.dtype)


def gate_kernel(piece_ref, *refs):
    refs[-1][...] = piece_ref[...]


def stage_kernel(nbr_ref, esp_ref, piece_ref, *refs):
    nbr_out, esp_out, piece_out, sems = refs[-4:]
    copies = [
        pltpu.make_async_copy(esp_ref, esp_out, sems.at[0]),
        pltpu.make_async_copy(nbr_ref, nbr_out, sems.at[1]),
    ]
    for copy in copies:
        copy.start()
    piece_out[...] = piece_ref[...]
    for copy in copies:
        copy.wait()


def couple_kernel(groups, lanes, mono_dev, units, nbr_ref, esp_ref, *refs):
    outs = refs[len(refs) - len(units) :]
    if len(refs) > len(units) + 1:
        pieces, store = refs[: -1 - len(units)], refs[-1 - len(units)]
        for i, piece in enumerate(pieces):
            store[i] = piece[...]
    else:
        store = refs[0]
    my_group = lax.axis_index("gddi")
    my_lane = lax.axis_index("intra")
    _, slot_dev, basis, _ = esp_ref.shape
    mono_grp = mono_dev * lanes
    half = basis // 2
    tail_rows = store.shape[1] - mono_dev * basis

    def near_density(fragment):
        apart = (fragment // mono_grp) ^ my_group
        lane = ((fragment % mono_grp) // mono_dev) ^ my_lane
        place = ((apart & 1) * (groups // 2) + (apart >> 1)) * lanes + lane
        member = fragment % mono_dev
        start = pl.multiple_of(member * basis, basis)
        off = store[place, pl.ds(start, half)]
        mixed = store[place, pl.ds(start + half, half)].astype(jnp.float32)
        tail = store[place, pl.ds(mono_dev * basis, tail_rows)].astype(jnp.float32)
        row = lax.broadcasted_iota(jnp.int32, (tail_rows, half), 0)
        diag = jnp.sum(jnp.where(row == member, tail, 0.0), axis=0, keepdims=True)
        first, second = unfold(mixed, diag)
        top = jnp.concatenate([first.astype(off.dtype), off], axis=1)
        bottom = jnp.concatenate([off.T, second.astype(off.dtype)], axis=1)
        return jnp.concatenate([top, bottom], axis=0)

    def partial_of(fragment):
        high, low, blocks = [], [], []
        for s in range(slot_dev):
            name = nbr_ref[my_lane * slot_dev + s, my_group * mono_grp + fragment]
            block = esp_ref[fragment, s]
            half_term = jnp.dot(block, near_density(name), preferred_element_type=jnp.float32)
            high.append(half_term.astype(jnp.bfloat16))
            low.append((half_term - high[-1].astype(jnp.float32)).astype(jnp.bfloat16))
            blocks.append(block)
        both = jnp.concatenate([jnp.concatenate(high, axis=1), jnp.concatenate(low, axis=1)], axis=0)
        both = transposed_dot(both, jnp.concatenate(blocks, axis=1))
        total = both[:basis] + both[basis:]
        mixed, diag = fold(total[:half, :half], total[half:, half:])
        return total[:half, half:], mixed, diag

    for (k, coded), out in zip(units, outs):
        write = write_coded if coded else write_plain
        write(out, [partial_of((my_lane ^ k) * mono_dev + m) for m in range(mono_dev)])


def write_plain(out, parts):
    half = out.shape[2]
    for m, (off, mixed, diag) in enumerate(parts):
        out[m, :half] = off
        out[m, half : 2 * half] = mixed
        out[m, 2 * half :] = jnp.broadcast_to(diag, (8, half))


def read_plain(ref, m):
    half = ref.shape[2]
    return ref[m, :half], ref[m, half : 2 * half], ref[m, 2 * half : 2 * half + 1]


def write_coded(out, parts):
    half = out.shape[1]
    tail = []
    for m, (off, mixed, diag) in enumerate(parts):
        off_code = scale_code(peak_of(off))
        mixed_code = scale_code(jnp.maximum(peak_of(mixed), jnp.abs(diag)))
        out[pl.ds(m * half, half)] = pack(encode(off, off_code), encode(mixed, mixed_code))
        tail += [pack(off_code, mixed_code), encode(diag, mixed_code)]
    row = lax.broadcasted_iota(jnp.int32, (out.shape[0] - len(parts) * half, half), 0)
    last = jnp.zeros(row.shape, jnp.int32)
    for i, values in enumerate(tail):
        last = jnp.where(row == i, values, last)
    out[pl.ds(len(parts) * half, row.shape[0])] = last


def read_coded(ref, m, mono_dev):
    half = ref.shape[1]
    tail = mono_dev * half + 2 * m
    off_code, mixed_code = unpack(ref[tail : tail + 1])
    off_q, mixed_q = unpack(ref[m * half : (m + 1) * half])
    return decode(off_q, off_code), decode(mixed_q, mixed_code), decode(ref[tail + 1 : tail + 2], mixed_code)


def summed(plain_ref, coded_refs, m):
    total = read_plain(plain_ref, m)
    for ref in coded_refs:
        total = [a + b for a, b in zip(total, read_coded(ref, m, plain_ref.shape[0]))]
    return total


def add_kernel(plain_ref, *refs):
    write_plain(refs[-1], [summed(plain_ref, refs[:-1], m) for m in range(plain_ref.shape[0])])


def finish_kernel(core_ref, own_ref, *refs):
    parts, (out_ref, ready, sems) = refs[:-3], refs[-3:]
    mono_dev, basis, _ = ready.shape
    half = basis // 2
    copies = []
    for m in range(mono_dev):
        off, mixed, diag = summed(own_ref, parts, m)
        first, second = unfold(mixed, diag)
        core = core_ref[m].astype(jnp.float32)
        ready[m, :half, :half] = core[:half, :half] + first
        ready[m, :half, half:] = core[:half, half:] + off
        ready[m, half:, :half] = core[half:, :half] + off.T
        ready[m, half:, half:] = core[half:, half:] + second
        copies.append(pltpu.make_async_copy(ready.at[m], out_ref.at[m], sems.at[m]))
        copies[-1].start()
    for copy in copies:
        copy.wait()


def local(density, h_core, esp_block, nbr):
    groups = lax.axis_size("gddi")
    lanes = lax.axis_size("intra")
    mono_dev, basis = density.shape[0], density.shape[1]
    half = basis // 2
    hbm = pl.BlockSpec(memory_space=pl.ANY)
    small = pltpu.CompilerParams(vmem_limit_bytes=8 * 2**20)

    rows = mono_dev * basis + round_up(mono_dev, 16)
    shard = pl.pallas_call(
        fold_kernel,
        out_shape=pltpu.VMEM((rows, half), density.dtype),
        in_specs=[IN_VMEM],
        out_specs=IN_VMEM,
        compiler_params=small,
        name="fold",
    )(pltpu.with_memory_space_constraint(density, pltpu.HBM))
    def along_z(piece, bit):
        return lax.ppermute(piece, "intra", xor_pairs(lanes, bit))

    def along_y(piece, y):
        return lax.ppermute(piece, "gddi", xor_pairs(groups, 2 * y))

    rows_y = groups // 2
    top = lanes // 2
    near = {(0, 0): shard, (0, top): along_z(shard, top)}

    def double(start):
        bit = top // 2
        while bit:
            for k in range(start, start + top):
                if (0, k) in near and (0, k ^ bit) not in near:
                    near[0, k ^ bit] = along_z(near[0, k], bit)
            bit //= 2

    double(0)
    for y in range(1, rows_y):
        near[y, 0] = along_y(shard, y)

    def gate(piece, *after):
        return pl.pallas_call(
            gate_kernel,
            out_shape=pltpu.VMEM(piece.shape, piece.dtype),
            in_specs=[IN_VMEM] + [hbm] * len(after),
            out_specs=IN_VMEM,
            compiler_params=small,
            name="gate",
        )(piece, *after)

    others = [piece for key, piece in near.items() if key != (0, top)]
    near[0, top] = gate(gate(near[0, top]), *others)
    double(top)
    for y in range(1, rows_y):
        for k in range(1, top):
            near[y, k] = along_z(near[y, k & (k - 1)], k & -k)
        for k in range(top, lanes):
            near[y, k] = along_y(near[0, k], y)

    names, blocks, near[rows_y - 1, 0] = pl.pallas_call(
        stage_kernel,
        out_shape=[
            pltpu.SMEM((nbr.shape[1], nbr.shape[0]), nbr.dtype),
            pltpu.VMEM(esp_block.shape, esp_block.dtype),
            pltpu.VMEM(shard.shape, shard.dtype),
        ],
        in_specs=[hbm, hbm, IN_VMEM, hbm],
        out_specs=[IN_SMEM, IN_VMEM, IN_VMEM],
        scratch_shapes=[pltpu.SemaphoreType.DMA((2,))],
        compiler_params=small,
        name="stage",
    )(
        pltpu.with_memory_space_constraint(nbr.T, pltpu.HBM),
        pltpu.with_memory_space_constraint(esp_block, pltpu.HBM),
        near[rows_y - 1, 0],
        near[0, lanes - 1],
    )
    keys = [(y, k) for y in range(rows_y) for k in range(lanes)]
    mine = [near[key] for key in keys]
    pieces = mine + [lax.ppermute(piece, "gddi", xor_pairs(groups, 1)) for piece in mine]

    plain = pltpu.VMEM((mono_dev, basis + 8, half), jnp.float32)
    coded = pltpu.VMEM((mono_dev * half + round_up(2 * mono_dev, 8), half), jnp.int32)
    piece_bytes = groups * lanes * rows * half * 2

    keep = pltpu.VMEM if piece_bytes <= 4 * 2**20 else jax.ShapeDtypeStruct
    store = keep((groups * lanes, rows, half), density.dtype)

    def couple(units, name, pieces, fill=False):
        return pl.pallas_call(
            functools.partial(couple_kernel, groups, lanes, mono_dev, units),
            out_shape=[store] * fill + [coded if is_coded else plain for _, is_coded in units],
            in_specs=[IN_SMEM] + [IN_VMEM] * (1 + len(pieces)),
            out_specs=[IN_VMEM] * (fill + len(units)),
            compiler_params=pltpu.CompilerParams(
                vmem_limit_bytes=2 * (piece_bytes + esp_block.size * 2) + 8 * 2**20
            ),
            name=name,
        )(names, blocks, *pieces)

    filled, beyond = couple([(top, True)], "couple_first", pieces, fill=True)
    beyond = {top: along_z(beyond, top)}
    for _ in range(5):
        beyond[top] = gate(beyond[top])
    rest = [k for k in range(1, lanes) if k != top]
    own, *units = couple([(0, False)] + [(k, True) for k in rest], "couple_rest", [filled])
    for k, unit in zip(rest, units):
        beyond[k] = along_z(unit, k)
    own = pl.pallas_call(
        add_kernel,
        out_shape=plain,
        in_specs=[IN_VMEM] * 2,
        out_specs=IN_VMEM,
        compiler_params=small,
        name="add",
    )(own, beyond[top])
    return pl.pallas_call(
        finish_kernel,
        out_shape=jax.ShapeDtypeStruct((mono_dev, basis, basis), jnp.float32),
        in_specs=[IN_VMEM] * (2 + len(rest)),
        out_specs=hbm,
        scratch_shapes=[
            pltpu.VMEM((mono_dev, basis, basis), jnp.float32),
            pltpu.SemaphoreType.DMA((mono_dev,)),
        ],
        compiler_params=small,
        name="finish",
    )(h_core, own, *[beyond[k] for k in rest])


def solution(mesh):
    return jax.shard_map(
        local,
        mesh=mesh,
        in_specs=(
            P(("job", "gddi", "intra"), None, None),
            P(("job", "gddi", "intra"), None, None),
            P(("job", "gddi"), "intra", None, None),
            P("job", None),
        ),
        out_specs=P(("job", "gddi", "intra"), None, None),
        check_vma=False,
    )
```

```python
import functools

import jax
import jax.numpy as jnp
from jax import lax
from jax.experimental import pallas as pl
from jax.experimental.pallas import tpu as pltpu
from jax.sharding import PartitionSpec as P

STEPS = 32.0
TOP = 32000.0
SHRINK = 1.0 / 16.0
IN_VMEM = pl.BlockSpec(memory_space=pltpu.VMEM)
IN_SMEM = pl.BlockSpec(memory_space=pltpu.SMEM)


def xor_pairs(size, k):
    return [(i, i ^ k) for i in range(size)]


def round_up(n, to):
    return -(-n // to) * to


def transposed_dot(a, b):
    return lax.dot_general(a, b, (((1,), (1,)), ((), ())), preferred_element_type=jnp.float32)


def square_iotas(half):
    row = lax.broadcasted_iota(jnp.int32, (half, half), 0)
    col = lax.broadcasted_iota(jnp.int32, (half, half), 1)
    return row, col


def fold(first, second):
    row, col = square_iotas(first.shape[0])
    mixed = jnp.where(row <= col, first, second)
    diag = jnp.sum(jnp.where(row == col, second, 0.0), axis=0, keepdims=True)
    return mixed, diag


def unfold(mixed, diag):
    row, col = square_iotas(mixed.shape[0])
    turned = mixed.T
    first = jnp.where(row <= col, mixed, turned)
    second = jnp.where(row > col, mixed, jnp.where(row < col, turned, diag))
    return first, second


def scale_code(peak):
    wanted = jnp.log(jnp.maximum(peak * SHRINK, 2.0**-120)) * STEPS
    return jnp.floor(wanted + 1.5).astype(jnp.int32)


def encode(x, code):
    units = jnp.exp(code.astype(jnp.float32) * (-1.0 / STEPS)) * TOP
    return jnp.floor(x * SHRINK * units + 0.5).astype(jnp.int32)


def decode(q, code):
    units = jnp.exp(code.astype(jnp.float32) * (1.0 / STEPS)) * (1.0 / TOP)
    return q.astype(jnp.float32) * units * (1.0 / SHRINK)


def pack(high, low):
    return lax.shift_left(high, 16) | (low & 0xFFFF)


def unpack(word):
    return lax.shift_right_arithmetic(word, 16), lax.shift_right_arithmetic(lax.shift_left(word, 16), 16)


def peak_of(x):
    return jnp.max(jnp.abs(x), axis=0, keepdims=True)


def fold_kernel(dens_ref, out_ref):
    mono_dev, basis, _ = dens_ref.shape
    half = basis // 2
    diags = []
    for m in range(mono_dev):
        out_ref[pl.ds(m * basis, half)] = dens_ref[m, :half, half:]
        mixed, diag = fold(
            dens_ref[m, :half, :half].astype(jnp.float32), dens_ref[m, half:, half:].astype(jnp.float32)
        )
        out_ref[pl.ds(m * basis + half, half)] = mixed.astype(out_ref.dtype)
        diags.append(diag)
    rows = out_ref.shape[0] - mono_dev * basis
    row = lax.broadcasted_iota(jnp.int32, (rows, half), 0)
    tail = jnp.zeros((rows, half), jnp.float32)
    for m in range(mono_dev):
        tail = jnp.where(row == m, diags[m], tail)
    out_ref[pl.ds(mono_dev * basis, rows)] = tail.astype(out_ref.dtype)


def gate_kernel(piece_ref, *refs):
    refs[-1][...] = piece_ref[...]


def stage_kernel(nbr_ref, esp_ref, piece_ref, *refs):
    nbr_out, esp_out, piece_out, sems = refs[-4:]
    copies = [
        pltpu.make_async_copy(esp_ref, esp_out, sems.at[0]),
        pltpu.make_async_copy(nbr_ref, nbr_out, sems.at[1]),
    ]
    for copy in copies:
        copy.start()
    piece_out[...] = piece_ref[...]
    for copy in copies:
        copy.wait()


def couple_kernel(groups, lanes, mono_dev, units, nbr_ref, esp_ref, *refs):
    outs = refs[len(refs) - len(units) :]
    if len(refs) > len(units) + 1:
        pieces, store = refs[: -1 - len(units)], refs[-1 - len(units)]
        for i, piece in enumerate(pieces):
            store[i] = piece[...]
    else:
        store = refs[0]
    my_group = lax.axis_index("gddi")
    my_lane = lax.axis_index("intra")
    _, slot_dev, basis, _ = esp_ref.shape
    mono_grp = mono_dev * lanes
    half = basis // 2
    tail_rows = store.shape[1] - mono_dev * basis

    def near_density(fragment):
        apart = (fragment // mono_grp) ^ my_group
        lane = ((fragment % mono_grp) // mono_dev) ^ my_lane
        place = ((apart & 1) * (groups // 2) + (apart >> 1)) * lanes + lane
        member = fragment % mono_dev
        start = pl.multiple_of(member * basis, basis)
        off = store[place, pl.ds(start, half)]
        mixed = store[place, pl.ds(start + half, half)].astype(jnp.float32)
        tail = store[place, pl.ds(mono_dev * basis, tail_rows)].astype(jnp.float32)
        row = lax.broadcasted_iota(jnp.int32, (tail_rows, half), 0)
        diag = jnp.sum(jnp.where(row == member, tail, 0.0), axis=0, keepdims=True)
        first, second = unfold(mixed, diag)
        top = jnp.concatenate([first.astype(off.dtype), off], axis=1)
        bottom = jnp.concatenate([off.T, second.astype(off.dtype)], axis=1)
        return jnp.concatenate([top, bottom], axis=0)

    def partial_of(fragment):
        high, low, blocks = [], [], []
        for s in range(slot_dev):
            name = nbr_ref[my_lane * slot_dev + s, my_group * mono_grp + fragment]
            block = esp_ref[fragment, s]
            half_term = jnp.dot(block, near_density(name), preferred_element_type=jnp.float32)
            high.append(half_term.astype(jnp.bfloat16))
            low.append((half_term - high[-1].astype(jnp.float32)).astype(jnp.bfloat16))
            blocks.append(block)
        both = jnp.concatenate([jnp.concatenate(high, axis=1), jnp.concatenate(low, axis=1)], axis=0)
        both = transposed_dot(both, jnp.concatenate(blocks, axis=1))
        total = both[:basis] + both[basis:]
        mixed, diag = fold(total[:half, :half], total[half:, half:])
        return total[:half, half:], mixed, diag

    for (k, coded), out in zip(units, outs):
        write = write_coded if coded else write_plain
        write(out, [partial_of((my_lane ^ k) * mono_dev + m) for m in range(mono_dev)])


def write_plain(out, parts):
    half = out.shape[2]
    for m, (off, mixed, diag) in enumerate(parts):
        out[m, :half] = off
        out[m, half : 2 * half] = mixed
        out[m, 2 * half :] = jnp.broadcast_to(diag, (8, half))


def read_plain(ref, m):
    half = ref.shape[2]
    return ref[m, :half], ref[m, half : 2 * half], ref[m, 2 * half : 2 * half + 1]


def write_coded(out, parts):
    half = out.shape[1]
    tail = []
    for m, (off, mixed, diag) in enumerate(parts):
        off_code = scale_code(peak_of(off))
        mixed_code = scale_code(jnp.maximum(peak_of(mixed), jnp.abs(diag)))
        out[pl.ds(m * half, half)] = pack(encode(off, off_code), encode(mixed, mixed_code))
        tail += [pack(off_code, mixed_code), encode(diag, mixed_code)]
    row = lax.broadcasted_iota(jnp.int32, (out.shape[0] - len(parts) * half, half), 0)
    last = jnp.zeros(row.shape, jnp.int32)
    for i, values in enumerate(tail):
        last = jnp.where(row == i, values, last)
    out[pl.ds(len(parts) * half, row.shape[0])] = last


def read_coded(ref, m, mono_dev):
    half = ref.shape[1]
    tail = mono_dev * half + 2 * m
    off_code, mixed_code = unpack(ref[tail : tail + 1])
    off_q, mixed_q = unpack(ref[m * half : (m + 1) * half])
    return decode(off_q, off_code), decode(mixed_q, mixed_code), decode(ref[tail + 1 : tail + 2], mixed_code)


def summed(plain_ref, coded_refs, m):
    total = read_plain(plain_ref, m)
    for ref in coded_refs:
        total = [a + b for a, b in zip(total, read_coded(ref, m, plain_ref.shape[0]))]
    return total


def add_kernel(plain_ref, *refs):
    write_plain(refs[-1], [summed(plain_ref, refs[:-1], m) for m in range(plain_ref.shape[0])])


def finish_kernel(core_ref, own_ref, *refs):
    parts, (out_ref, ready, sems) = refs[:-3], refs[-3:]
    mono_dev, basis, _ = ready.shape
    half = basis // 2
    copies = []
    for m in range(mono_dev):
        off, mixed, diag = summed(own_ref, parts, m)
        first, second = unfold(mixed, diag)
        core = core_ref[m].astype(jnp.float32)
        ready[m, :half, :half] = core[:half, :half] + first
        ready[m, :half, half:] = core[:half, half:] + off
        ready[m, half:, :half] = core[half:, :half] + off.T
        ready[m, half:, half:] = core[half:, half:] + second
        copies.append(pltpu.make_async_copy(ready.at[m], out_ref.at[m], sems.at[m]))
        copies[-1].start()
    for copy in copies:
        copy.wait()


def local(density, h_core, esp_block, nbr):
    groups = lax.axis_size("gddi")
    lanes = lax.axis_size("intra")
    mono_dev, basis = density.shape[0], density.shape[1]
    half = basis // 2
    hbm = pl.BlockSpec(memory_space=pl.ANY)
    small = pltpu.CompilerParams(vmem_limit_bytes=8 * 2**20)

    rows = mono_dev * basis + round_up(mono_dev, 16)
    shard = pl.pallas_call(
        fold_kernel,
        out_shape=pltpu.VMEM((rows, half), density.dtype),
        in_specs=[IN_VMEM],
        out_specs=IN_VMEM,
        compiler_params=small,
        name="fold",
    )(pltpu.with_memory_space_constraint(density, pltpu.HBM))
    def along_z(piece, bit):
        return lax.ppermute(piece, "intra", xor_pairs(lanes, bit))

    def along_y(piece, y):
        return lax.ppermute(piece, "gddi", xor_pairs(groups, 2 * y))

    rows_y = groups // 2
    top = lanes // 2
    near = {(0, 0): shard, (0, top): along_z(shard, top)}

    def double(start):
        bit = top // 2
        while bit:
            for k in range(start, start + top):
                if (0, k) in near and (0, k ^ bit) not in near:
                    near[0, k ^ bit] = along_z(near[0, k], bit)
            bit //= 2

    double(0)
    for y in range(1, rows_y):
        near[y, 0] = along_y(shard, y)

    def gate(piece, *after):
        return pl.pallas_call(
            gate_kernel,
            out_shape=pltpu.VMEM(piece.shape, piece.dtype),
            in_specs=[IN_VMEM] + [hbm] * len(after),
            out_specs=IN_VMEM,
            compiler_params=small,
            name="gate",
        )(piece, *after)

    others = [piece for key, piece in near.items() if key != (0, top)]
    near[0, top] = gate(gate(near[0, top]), *others)
    double(top)
    for y in range(1, rows_y):
        for k in range(1, top):
            near[y, k] = along_z(near[y, k & (k - 1)], k & -k)
        for k in range(top, lanes):
            near[y, k] = along_y(near[0, k], y)

    names, blocks, near[rows_y - 1, 0] = pl.pallas_call(
        stage_kernel,
        out_shape=[
            pltpu.SMEM((nbr.shape[1], nbr.shape[0]), nbr.dtype),
            pltpu.VMEM(esp_block.shape, esp_block.dtype),
            pltpu.VMEM(shard.shape, shard.dtype),
        ],
        in_specs=[hbm, hbm, IN_VMEM, hbm],
        out_specs=[IN_SMEM, IN_VMEM, IN_VMEM],
        scratch_shapes=[pltpu.SemaphoreType.DMA((2,))],
        compiler_params=small,
        name="stage",
    )(
        pltpu.with_memory_space_constraint(nbr.T, pltpu.HBM),
        pltpu.with_memory_space_constraint(esp_block, pltpu.HBM),
        near[rows_y - 1, 0],
        near[0, lanes - 1],
    )
    keys = [(y, k) for y in range(rows_y) for k in range(lanes)]
    mine = [near[key] for key in keys]
    pieces = mine + [lax.ppermute(piece, "gddi", xor_pairs(groups, 1)) for piece in mine]

    plain = pltpu.VMEM((mono_dev, basis + 8, half), jnp.float32)
    coded = pltpu.VMEM((mono_dev * half + round_up(2 * mono_dev, 8), half), jnp.int32)
    piece_bytes = groups * lanes * rows * half * 2

    keep = pltpu.VMEM if piece_bytes <= 4 * 2**20 else jax.ShapeDtypeStruct
    store = keep((groups * lanes, rows, half), density.dtype)

    def couple(units, name, pieces, fill=False):
        return pl.pallas_call(
            functools.partial(couple_kernel, groups, lanes, mono_dev, units),
            out_shape=[store] * fill + [coded if is_coded else plain for _, is_coded in units],
            in_specs=[IN_SMEM] + [IN_VMEM] * (1 + len(pieces)),
            out_specs=[IN_VMEM] * (fill + len(units)),
            compiler_params=pltpu.CompilerParams(
                vmem_limit_bytes=2 * (piece_bytes + esp_block.size * 2) + 8 * 2**20
            ),
            name=name,
        )(names, blocks, *pieces)

    filled, beyond = couple([(top, True)], "couple_first", pieces, fill=True)
    beyond = {top: along_z(beyond, top)}
    for _ in range(5):
        beyond[top] = gate(beyond[top])
    rest = [k for k in range(lanes - 1, 0, -1) if k != top]
    units = couple([(k, True) for k in rest], "couple_rest", [filled])
    for k, unit in zip(rest, units):
        beyond[k] = along_z(unit, k)
    (own,) = couple([(0, False)], "couple_own", [filled])
    own = pl.pallas_call(
        add_kernel,
        out_shape=plain,
        in_specs=[IN_VMEM] * 2,
        out_specs=IN_VMEM,
        compiler_params=small,
        name="add",
    )(own, beyond[top])
    return pl.pallas_call(
        finish_kernel,
        out_shape=jax.ShapeDtypeStruct((mono_dev, basis, basis), jnp.float32),
        in_specs=[IN_VMEM] * (2 + len(rest)),
        out_specs=hbm,
        scratch_shapes=[
            pltpu.VMEM((mono_dev, basis, basis), jnp.float32),
            pltpu.SemaphoreType.DMA((mono_dev,)),
        ],
        compiler_params=small,
        name="finish",
    )(h_core, own, *[beyond[k] for k in rest])


def solution(mesh):
    return jax.shard_map(
        local,
        mesh=mesh,
        in_specs=(
            P(("job", "gddi", "intra"), None, None),
            P(("job", "gddi", "intra"), None, None),
            P(("job", "gddi"), "intra", None, None),
            P("job", None),
        ),
        out_specs=P(("job", "gddi", "intra"), None, None),
        check_vma=False,
    )
```

```python
import functools

import jax
import jax.numpy as jnp
from jax import lax
from jax.experimental import pallas as pl
from jax.experimental.pallas import tpu as pltpu
from jax.sharding import PartitionSpec as P

STEPS = 32.0
TOP = 32000.0
SHRINK = 1.0 / 16.0
IN_VMEM = pl.BlockSpec(memory_space=pltpu.VMEM)
IN_SMEM = pl.BlockSpec(memory_space=pltpu.SMEM)


def xor_pairs(size, k):
    return [(i, i ^ k) for i in range(size)]


def round_up(n, to):
    return -(-n // to) * to


def transposed_dot(a, b):
    return lax.dot_general(a, b, (((1,), (1,)), ((), ())), preferred_element_type=jnp.float32)


def square_iotas(half):
    row = lax.broadcasted_iota(jnp.int32, (half, half), 0)
    col = lax.broadcasted_iota(jnp.int32, (half, half), 1)
    return row, col


def fold(first, second):
    row, col = square_iotas(first.shape[0])
    mixed = jnp.where(row <= col, first, second)
    diag = jnp.sum(jnp.where(row == col, second, 0.0), axis=0, keepdims=True)
    return mixed, diag


def unfold(mixed, diag):
    row, col = square_iotas(mixed.shape[0])
    turned = mixed.T
    first = jnp.where(row <= col, mixed, turned)
    second = jnp.where(row > col, mixed, jnp.where(row < col, turned, diag))
    return first, second


def scale_code(peak):
    wanted = jnp.log(jnp.maximum(peak * SHRINK, 2.0**-120)) * STEPS
    return jnp.floor(wanted + 1.5).astype(jnp.int32)


def encode(x, code):
    units = jnp.exp(code.astype(jnp.float32) * (-1.0 / STEPS)) * TOP
    return jnp.floor(x * SHRINK * units + 0.5).astype(jnp.int32)


def decode(q, code):
    units = jnp.exp(code.astype(jnp.float32) * (1.0 / STEPS)) * (1.0 / TOP)
    return q.astype(jnp.float32) * units * (1.0 / SHRINK)


def pack(high, low):
    return lax.shift_left(high, 16) | (low & 0xFFFF)


def unpack(word):
    return lax.shift_right_arithmetic(word, 16), lax.shift_right_arithmetic(lax.shift_left(word, 16), 16)


def peak_of(x):
    return jnp.max(jnp.abs(x), axis=0, keepdims=True)


def fold_kernel(dens_ref, out_ref):
    mono_dev, basis, _ = dens_ref.shape
    half = basis // 2
    diags = []
    for m in range(mono_dev):
        out_ref[pl.ds(m * basis, half)] = dens_ref[m, :half, half:]
        mixed, diag = fold(
            dens_ref[m, :half, :half].astype(jnp.float32), dens_ref[m, half:, half:].astype(jnp.float32)
        )
        out_ref[pl.ds(m * basis + half, half)] = mixed.astype(out_ref.dtype)
        diags.append(diag)
    rows = out_ref.shape[0] - mono_dev * basis
    row = lax.broadcasted_iota(jnp.int32, (rows, half), 0)
    tail = jnp.zeros((rows, half), jnp.float32)
    for m in range(mono_dev):
        tail = jnp.where(row == m, diags[m], tail)
    out_ref[pl.ds(mono_dev * basis, rows)] = tail.astype(out_ref.dtype)


def gate_kernel(piece_ref, *refs):
    refs[-1][...] = piece_ref[...]


def stage_kernel(nbr_ref, esp_ref, piece_ref, *refs):
    nbr_out, esp_out, piece_out, sems = refs[-4:]
    copies = [
        pltpu.make_async_copy(esp_ref, esp_out, sems.at[0]),
        pltpu.make_async_copy(nbr_ref, nbr_out, sems.at[1]),
    ]
    for copy in copies:
        copy.start()
    piece_out[...] = piece_ref[...]
    for copy in copies:
        copy.wait()


def couple_kernel(groups, lanes, mono_dev, units, nbr_ref, esp_ref, *refs):
    outs = refs[len(refs) - len(units) :]
    if len(refs) > len(units) + 1:
        pieces, store = refs[: -1 - len(units)], refs[-1 - len(units)]
        for i, piece in enumerate(pieces):
            store[i] = piece[...]
    else:
        store = refs[0]
    my_group = lax.axis_index("gddi")
    my_lane = lax.axis_index("intra")
    _, slot_dev, basis, _ = esp_ref.shape
    mono_grp = mono_dev * lanes
    half = basis // 2
    tail_rows = store.shape[1] - mono_dev * basis

    def near_density(fragment):
        apart = (fragment // mono_grp) ^ my_group
        lane = ((fragment % mono_grp) // mono_dev) ^ my_lane
        place = ((apart & 1) * (groups // 2) + (apart >> 1)) * lanes + lane
        member = fragment % mono_dev
        start = pl.multiple_of(member * basis, basis)
        off = store[place, pl.ds(start, half)]
        mixed = store[place, pl.ds(start + half, half)].astype(jnp.float32)
        tail = store[place, pl.ds(mono_dev * basis, tail_rows)].astype(jnp.float32)
        row = lax.broadcasted_iota(jnp.int32, (tail_rows, half), 0)
        diag = jnp.sum(jnp.where(row == member, tail, 0.0), axis=0, keepdims=True)
        first, second = unfold(mixed, diag)
        top = jnp.concatenate([first.astype(off.dtype), off], axis=1)
        bottom = jnp.concatenate([off.T, second.astype(off.dtype)], axis=1)
        return jnp.concatenate([top, bottom], axis=0)

    def partial_of(fragment):
        high, low, blocks = [], [], []
        for s in range(slot_dev):
            name = nbr_ref[my_lane * slot_dev + s, my_group * mono_grp + fragment]
            block = esp_ref[fragment, s]
            half_term = jnp.dot(block, near_density(name), preferred_element_type=jnp.float32)
            high.append(half_term.astype(jnp.bfloat16))
            low.append((half_term - high[-1].astype(jnp.float32)).astype(jnp.bfloat16))
            blocks.append(block)
        both = jnp.concatenate([jnp.concatenate(high, axis=1), jnp.concatenate(low, axis=1)], axis=0)
        both = transposed_dot(both, jnp.concatenate(blocks, axis=1))
        total = both[:basis] + both[basis:]
        mixed, diag = fold(total[:half, :half], total[half:, half:])
        return total[:half, half:], mixed, diag

    for (k, coded), out in zip(units, outs):
        write = write_coded if coded else write_plain
        write(out, [partial_of((my_lane ^ k) * mono_dev + m) for m in range(mono_dev)])


def write_plain(out, parts):
    half = out.shape[2]
    for m, (off, mixed, diag) in enumerate(parts):
        out[m, :half] = off
        out[m, half : 2 * half] = mixed
        out[m, 2 * half :] = jnp.broadcast_to(diag, (8, half))


def read_plain(ref, m):
    half = ref.shape[2]
    return ref[m, :half], ref[m, half : 2 * half], ref[m, 2 * half : 2 * half + 1]


def write_coded(out, parts):
    half = out.shape[1]
    tail = []
    for m, (off, mixed, diag) in enumerate(parts):
        off_code = scale_code(peak_of(off))
        mixed_code = scale_code(jnp.maximum(peak_of(mixed), jnp.abs(diag)))
        out[pl.ds(m * half, half)] = pack(encode(off, off_code), encode(mixed, mixed_code))
        tail += [pack(off_code, mixed_code), encode(diag, mixed_code)]
    row = lax.broadcasted_iota(jnp.int32, (out.shape[0] - len(parts) * half, half), 0)
    last = jnp.zeros(row.shape, jnp.int32)
    for i, values in enumerate(tail):
        last = jnp.where(row == i, values, last)
    out[pl.ds(len(parts) * half, row.shape[0])] = last


def read_coded(ref, m, mono_dev):
    half = ref.shape[1]
    tail = mono_dev * half + 2 * m
    off_code, mixed_code = unpack(ref[tail : tail + 1])
    off_q, mixed_q = unpack(ref[m * half : (m + 1) * half])
    return decode(off_q, off_code), decode(mixed_q, mixed_code), decode(ref[tail + 1 : tail + 2], mixed_code)


def summed(plain_ref, coded_refs, m):
    total = read_plain(plain_ref, m)
    for ref in coded_refs:
        total = [a + b for a, b in zip(total, read_coded(ref, m, plain_ref.shape[0]))]
    return total


def add_kernel(plain_ref, *refs):
    write_plain(refs[-1], [summed(plain_ref, refs[:-1], m) for m in range(plain_ref.shape[0])])


def finish_kernel(core_ref, own_ref, *refs):
    parts, (out_ref, ready, sems) = refs[:-3], refs[-3:]
    mono_dev, basis, _ = ready.shape
    half = basis // 2
    copies = []
    for m in range(mono_dev):
        off, mixed, diag = summed(own_ref, parts, m)
        first, second = unfold(mixed, diag)
        core = core_ref[m].astype(jnp.float32)
        ready[m, :half, :half] = core[:half, :half] + first
        ready[m, :half, half:] = core[:half, half:] + off
        ready[m, half:, :half] = core[half:, :half] + off.T
        ready[m, half:, half:] = core[half:, half:] + second
        copies.append(pltpu.make_async_copy(ready.at[m], out_ref.at[m], sems.at[m]))
        copies[-1].start()
    for copy in copies:
        copy.wait()


def local(density, h_core, esp_block, nbr):
    groups = lax.axis_size("gddi")
    lanes = lax.axis_size("intra")
    mono_dev, basis = density.shape[0], density.shape[1]
    half = basis // 2
    hbm = pl.BlockSpec(memory_space=pl.ANY)
    small = pltpu.CompilerParams(vmem_limit_bytes=8 * 2**20)

    rows = mono_dev * basis + round_up(mono_dev, 16)
    shard = pl.pallas_call(
        fold_kernel,
        out_shape=pltpu.VMEM((rows, half), density.dtype),
        in_specs=[IN_VMEM],
        out_specs=IN_VMEM,
        compiler_params=small,
        name="fold",
    )(pltpu.with_memory_space_constraint(density, pltpu.HBM))
    def along_z(piece, bit):
        return lax.ppermute(piece, "intra", xor_pairs(lanes, bit))

    def along_y(piece, y):
        return lax.ppermute(piece, "gddi", xor_pairs(groups, 2 * y))

    rows_y = groups // 2
    top = lanes // 2
    near = {(0, 0): shard, (0, top): along_z(shard, top)}

    def double(start):
        bit = top // 2
        while bit:
            for k in range(start, start + top):
                if (0, k) in near and (0, k ^ bit) not in near:
                    near[0, k ^ bit] = along_z(near[0, k], bit)
            bit //= 2

    double(0)
    for y in range(1, rows_y):
        near[y, 0] = along_y(shard, y)

    def gate(piece, *after):
        return pl.pallas_call(
            gate_kernel,
            out_shape=pltpu.VMEM(piece.shape, piece.dtype),
            in_specs=[IN_VMEM] + [hbm] * len(after),
            out_specs=IN_VMEM,
            compiler_params=small,
            name="gate",
        )(piece, *after)

    others = [piece for key, piece in near.items() if key != (0, top)]
    near[0, top] = gate(gate(near[0, top]), *others)
    double(top)
    for y in range(1, rows_y):
        for k in range(1, top):
            near[y, k] = along_z(near[y, k & (k - 1)], k & -k)
        for k in range(top, lanes):
            near[y, k] = along_y(near[0, k], y)

    names, blocks, near[rows_y - 1, 0] = pl.pallas_call(
        stage_kernel,
        out_shape=[
            pltpu.SMEM((nbr.shape[1], nbr.shape[0]), nbr.dtype),
            pltpu.VMEM(esp_block.shape, esp_block.dtype),
            pltpu.VMEM(shard.shape, shard.dtype),
        ],
        in_specs=[hbm, hbm, IN_VMEM, hbm],
        out_specs=[IN_SMEM, IN_VMEM, IN_VMEM],
        scratch_shapes=[pltpu.SemaphoreType.DMA((2,))],
        compiler_params=small,
        name="stage",
    )(
        pltpu.with_memory_space_constraint(nbr.T, pltpu.HBM),
        pltpu.with_memory_space_constraint(esp_block, pltpu.HBM),
        near[rows_y - 1, 0],
        near[0, lanes - 1],
    )
    keys = [(y, k) for y in range(rows_y) for k in range(lanes)]
    mine = [near[key] for key in keys]
    pieces = mine + [lax.ppermute(piece, "gddi", xor_pairs(groups, 1)) for piece in mine]

    plain = pltpu.VMEM((mono_dev, basis + 8, half), jnp.float32)
    coded = pltpu.VMEM((mono_dev * half + round_up(2 * mono_dev, 8), half), jnp.int32)
    piece_bytes = groups * lanes * rows * half * 2

    keep = pltpu.VMEM if piece_bytes <= 4 * 2**20 else jax.ShapeDtypeStruct
    store = keep((groups * lanes, rows, half), density.dtype)

    def couple(units, name, pieces, fill=False):
        return pl.pallas_call(
            functools.partial(couple_kernel, groups, lanes, mono_dev, units),
            out_shape=[store] * fill + [coded if is_coded else plain for _, is_coded in units],
            in_specs=[IN_SMEM] + [IN_VMEM] * (1 + len(pieces)),
            out_specs=[IN_VMEM] * (fill + len(units)),
            compiler_params=pltpu.CompilerParams(
                vmem_limit_bytes=2 * (piece_bytes + esp_block.size * 2) + 8 * 2**20
            ),
            name=name,
        )(names, blocks, *pieces)

    filled, beyond = couple([(top, True)], "couple_first", pieces, fill=True)
    beyond = {top: along_z(beyond, top)}
    for _ in range(5):
        beyond[top] = gate(beyond[top])
    rest = [k for k in range(1, lanes) if k != top]
    units = couple([(k, True) for k in rest], "couple_rest", [filled])
    for k, unit in zip(rest, units):
        beyond[k] = along_z(unit, k)
    (own,) = couple([(0, False)], "couple_own", [filled])
    own = pl.pallas_call(
        add_kernel,
        out_shape=plain,
        in_specs=[IN_VMEM] * 2,
        out_specs=IN_VMEM,
        compiler_params=small,
        name="add",
    )(own, beyond[top])
    return pl.pallas_call(
        finish_kernel,
        out_shape=jax.ShapeDtypeStruct((mono_dev, basis, basis), jnp.float32),
        in_specs=[IN_VMEM] * (2 + len(rest)),
        out_specs=hbm,
        scratch_shapes=[
            pltpu.VMEM((mono_dev, basis, basis), jnp.float32),
            pltpu.SemaphoreType.DMA((mono_dev,)),
        ],
        compiler_params=small,
        name="finish",
    )(h_core, own, *[beyond[k] for k in rest])


def solution(mesh):
    return jax.shard_map(
        local,
        mesh=mesh,
        in_specs=(
            P(("job", "gddi", "intra"), None, None),
            P(("job", "gddi", "intra"), None, None),
            P(("job", "gddi"), "intra", None, None),
            P("job", None),
        ),
        out_specs=P(("job", "gddi", "intra"), None, None),
        check_vma=False,
    )
```

```python
import functools

import jax
import jax.numpy as jnp
from jax import lax
from jax.experimental import pallas as pl
from jax.experimental.pallas import tpu as pltpu
from jax.sharding import PartitionSpec as P

STEPS = 32.0
TOP = 32000.0
SHRINK = 1.0 / 16.0
IN_VMEM = pl.BlockSpec(memory_space=pltpu.VMEM)
IN_SMEM = pl.BlockSpec(memory_space=pltpu.SMEM)


def xor_pairs(size, k):
    return [(i, i ^ k) for i in range(size)]


def round_up(n, to):
    return -(-n // to) * to


def transposed_dot(a, b):
    return lax.dot_general(a, b, (((1,), (1,)), ((), ())), preferred_element_type=jnp.float32)


def square_iotas(half):
    row = lax.broadcasted_iota(jnp.int32, (half, half), 0)
    col = lax.broadcasted_iota(jnp.int32, (half, half), 1)
    return row, col


def fold(first, second):
    row, col = square_iotas(first.shape[0])
    mixed = jnp.where(row <= col, first, second)
    diag = jnp.sum(jnp.where(row == col, second, 0.0), axis=0, keepdims=True)
    return mixed, diag


def unfold(mixed, diag):
    row, col = square_iotas(mixed.shape[0])
    turned = mixed.T
    first = jnp.where(row <= col, mixed, turned)
    second = jnp.where(row > col, mixed, jnp.where(row < col, turned, diag))
    return first, second


def scale_code(peak):
    wanted = jnp.log(jnp.maximum(peak * SHRINK, 2.0**-120)) * STEPS
    return jnp.floor(wanted + 1.5).astype(jnp.int32)


def encode(x, code):
    inverse = jnp.exp(code.astype(jnp.float32) * (-1.0 / STEPS))
    return jnp.floor(x * SHRINK * inverse * TOP + 0.5).astype(jnp.int32)


def decode(q, code):
    scale = jnp.exp(code.astype(jnp.float32) * (1.0 / STEPS))
    return q.astype(jnp.float32) * (1.0 / TOP) * scale * (1.0 / SHRINK)


def pack(high, low):
    return lax.shift_left(high, 16) | (low & 0xFFFF)


def unpack(word):
    return lax.shift_right_arithmetic(word, 16), lax.shift_right_arithmetic(lax.shift_left(word, 16), 16)


def peak_of(x):
    return jnp.max(jnp.abs(x), axis=0, keepdims=True)


def fold_kernel(dens_ref, out_ref):
    mono_dev, basis, _ = dens_ref.shape
    half = basis // 2
    diags = []
    for m in range(mono_dev):
        out_ref[pl.ds(m * basis, half)] = dens_ref[m, :half, half:]
        mixed, diag = fold(
            dens_ref[m, :half, :half].astype(jnp.float32), dens_ref[m, half:, half:].astype(jnp.float32)
        )
        out_ref[pl.ds(m * basis + half, half)] = mixed.astype(out_ref.dtype)
        diags.append(diag)
    rows = out_ref.shape[0] - mono_dev * basis
    row = lax.broadcasted_iota(jnp.int32, (rows, half), 0)
    tail = jnp.zeros((rows, half), jnp.float32)
    for m in range(mono_dev):
        tail = jnp.where(row == m, diags[m], tail)
    out_ref[pl.ds(mono_dev * basis, rows)] = tail.astype(out_ref.dtype)


def gate_kernel(piece_ref, *refs):
    refs[-1][...] = piece_ref[...]


def stage_kernel(nbr_ref, esp_ref, piece_ref, *refs):
    nbr_out, esp_out, piece_out, sems = refs[-4:]
    copies = [
        pltpu.make_async_copy(esp_ref, esp_out, sems.at[0]),
        pltpu.make_async_copy(nbr_ref, nbr_out, sems.at[1]),
    ]
    for copy in copies:
        copy.start()
    piece_out[...] = piece_ref[...]
    for copy in copies:
        copy.wait()


def couple_kernel(groups, lanes, mono_dev, units, nbr_ref, esp_ref, *refs):
    outs = refs[len(refs) - len(units) :]
    if len(refs) > len(units) + 1:
        pieces, store = refs[: -1 - len(units)], refs[-1 - len(units)]
        for i, piece in enumerate(pieces):
            store[i] = piece[...]
    else:
        store = refs[0]
    my_group = lax.axis_index("gddi")
    my_lane = lax.axis_index("intra")
    _, slot_dev, basis, _ = esp_ref.shape
    mono_grp = mono_dev * lanes
    half = basis // 2
    tail_rows = store.shape[1] - mono_dev * basis

    def near_density(fragment):
        apart = (fragment // mono_grp) ^ my_group
        lane = ((fragment % mono_grp) // mono_dev) ^ my_lane
        place = ((apart & 1) * (groups // 2) + (apart >> 1)) * lanes + lane
        member = fragment % mono_dev
        start = pl.multiple_of(member * basis, basis)
        off = store[place, pl.ds(start, half)]
        mixed = store[place, pl.ds(start + half, half)].astype(jnp.float32)
        tail = store[place, pl.ds(mono_dev * basis, tail_rows)].astype(jnp.float32)
        row = lax.broadcasted_iota(jnp.int32, (tail_rows, half), 0)
        diag = jnp.sum(jnp.where(row == member, tail, 0.0), axis=0, keepdims=True)
        first, second = unfold(mixed, diag)
        top = jnp.concatenate([first.astype(off.dtype), off], axis=1)
        bottom = jnp.concatenate([off.T, second.astype(off.dtype)], axis=1)
        return jnp.concatenate([top, bottom], axis=0)

    def partial_of(fragment):
        high, low, blocks = [], [], []
        for s in range(slot_dev):
            name = nbr_ref[my_lane * slot_dev + s, my_group * mono_grp + fragment]
            block = esp_ref[fragment, s]
            half_term = jnp.dot(block, near_density(name), preferred_element_type=jnp.float32)
            high.append(half_term.astype(jnp.bfloat16))
            low.append((half_term - high[-1].astype(jnp.float32)).astype(jnp.bfloat16))
            blocks.append(block)
        both = jnp.concatenate([jnp.concatenate(high, axis=1), jnp.concatenate(low, axis=1)], axis=0)
        both = transposed_dot(both, jnp.concatenate(blocks, axis=1))
        total = both[:basis] + both[basis:]
        mixed, diag = fold(total[:half, :half], total[half:, half:])
        return total[:half, half:], mixed, diag

    for (k, coded), out in zip(units, outs):
        write = write_coded if coded else write_plain
        write(out, [partial_of((my_lane ^ k) * mono_dev + m) for m in range(mono_dev)])


def write_plain(out, parts):
    half = out.shape[2]
    for m, (off, mixed, diag) in enumerate(parts):
        out[m, :half] = off
        out[m, half : 2 * half] = mixed
        out[m, 2 * half :] = jnp.broadcast_to(diag, (8, half))


def read_plain(ref, m):
    half = ref.shape[2]
    return ref[m, :half], ref[m, half : 2 * half], ref[m, 2 * half : 2 * half + 1]


def write_coded(out, parts):
    half = out.shape[1]
    tail = []
    for m, (off, mixed, diag) in enumerate(parts):
        off_code = scale_code(peak_of(off))
        mixed_code = scale_code(jnp.maximum(peak_of(mixed), jnp.abs(diag)))
        out[pl.ds(m * half, half)] = pack(encode(off, off_code), encode(mixed, mixed_code))
        tail += [pack(off_code, mixed_code), encode(diag, mixed_code)]
    row = lax.broadcasted_iota(jnp.int32, (out.shape[0] - len(parts) * half, half), 0)
    last = jnp.zeros(row.shape, jnp.int32)
    for i, values in enumerate(tail):
        last = jnp.where(row == i, values, last)
    out[pl.ds(len(parts) * half, row.shape[0])] = last


def read_coded(ref, m, mono_dev):
    half = ref.shape[1]
    tail = mono_dev * half + 2 * m
    off_code, mixed_code = unpack(ref[tail : tail + 1])
    off_q, mixed_q = unpack(ref[m * half : (m + 1) * half])
    return decode(off_q, off_code), decode(mixed_q, mixed_code), decode(ref[tail + 1 : tail + 2], mixed_code)


def summed(plain_ref, coded_refs, m):
    total = read_plain(plain_ref, m)
    for ref in coded_refs:
        total = [a + b for a, b in zip(total, read_coded(ref, m, plain_ref.shape[0]))]
    return total


def add_kernel(plain_ref, *refs):
    write_plain(refs[-1], [summed(plain_ref, refs[:-1], m) for m in range(plain_ref.shape[0])])


def finish_kernel(core_ref, own_ref, *refs):
    parts, (out_ref, ready, sems) = refs[:-3], refs[-3:]
    mono_dev, basis, _ = ready.shape
    half = basis // 2
    copies = []
    for m in range(mono_dev):
        off, mixed, diag = summed(own_ref, parts, m)
        first, second = unfold(mixed, diag)
        core = core_ref[m].astype(jnp.float32)
        ready[m, :half, :half] = core[:half, :half] + first
        ready[m, :half, half:] = core[:half, half:] + off
        ready[m, half:, :half] = core[half:, :half] + off.T
        ready[m, half:, half:] = core[half:, half:] + second
        copies.append(pltpu.make_async_copy(ready.at[m], out_ref.at[m], sems.at[m]))
        copies[-1].start()
    for copy in copies:
        copy.wait()


def local(density, h_core, esp_block, nbr):
    groups = lax.axis_size("gddi")
    lanes = lax.axis_size("intra")
    mono_dev, basis = density.shape[0], density.shape[1]
    half = basis // 2
    hbm = pl.BlockSpec(memory_space=pl.ANY)
    small = pltpu.CompilerParams(vmem_limit_bytes=8 * 2**20)

    rows = mono_dev * basis + round_up(mono_dev, 16)
    shard = pl.pallas_call(
        fold_kernel,
        out_shape=pltpu.VMEM((rows, half), density.dtype),
        in_specs=[IN_VMEM],
        out_specs=IN_VMEM,
        compiler_params=small,
        name="fold",
    )(pltpu.with_memory_space_constraint(density, pltpu.HBM))
    def along_z(piece, bit):
        return lax.ppermute(piece, "intra", xor_pairs(lanes, bit))

    def along_y(piece, y):
        return lax.ppermute(piece, "gddi", xor_pairs(groups, 2 * y))

    rows_y = groups // 2
    top = lanes // 2
    near = {(0, 0): shard, (0, top): along_z(shard, top)}

    def double(start):
        bit = top // 2
        while bit:
            for k in range(start, start + top):
                if (0, k) in near and (0, k ^ bit) not in near:
                    near[0, k ^ bit] = along_z(near[0, k], bit)
            bit //= 2

    double(0)
    for y in range(1, rows_y):
        near[y, 0] = along_y(shard, y)

    def gate(piece, *after):
        return pl.pallas_call(
            gate_kernel,
            out_shape=pltpu.VMEM(piece.shape, piece.dtype),
            in_specs=[IN_VMEM] + [hbm] * len(after),
            out_specs=IN_VMEM,
            compiler_params=small,
            name="gate",
        )(piece, *after)

    others = [piece for key, piece in near.items() if key != (0, top)]
    near[0, top] = gate(gate(near[0, top]), *others)
    double(top)
    for y in range(1, rows_y):
        for k in range(1, top):
            near[y, k] = along_z(near[y, k & (k - 1)], k & -k)
        for k in range(top, lanes):
            near[y, k] = along_y(near[0, k], y)

    names, blocks, near[rows_y - 1, 0] = pl.pallas_call(
        stage_kernel,
        out_shape=[
            pltpu.SMEM((nbr.shape[1], nbr.shape[0]), nbr.dtype),
            pltpu.VMEM(esp_block.shape, esp_block.dtype),
            pltpu.VMEM(shard.shape, shard.dtype),
        ],
        in_specs=[hbm, hbm, IN_VMEM, hbm],
        out_specs=[IN_SMEM, IN_VMEM, IN_VMEM],
        scratch_shapes=[pltpu.SemaphoreType.DMA((2,))],
        compiler_params=small,
        name="stage",
    )(
        pltpu.with_memory_space_constraint(nbr.T, pltpu.HBM),
        pltpu.with_memory_space_constraint(esp_block, pltpu.HBM),
        near[rows_y - 1, 0],
        near[0, lanes - 1],
    )
    keys = [(y, k) for y in range(rows_y) for k in range(lanes)]
    mine = [near[key] for key in keys]
    pieces = mine + [lax.ppermute(piece, "gddi", xor_pairs(groups, 1)) for piece in mine]

    plain = pltpu.VMEM((mono_dev, basis + 8, half), jnp.float32)
    coded = pltpu.VMEM((mono_dev * half + round_up(2 * mono_dev, 8), half), jnp.int32)
    piece_bytes = groups * lanes * rows * half * 2

    keep = pltpu.VMEM if piece_bytes <= 4 * 2**20 else jax.ShapeDtypeStruct
    store = keep((groups * lanes, rows, half), density.dtype)

    def couple(units, name, pieces, fill=False):
        return pl.pallas_call(
            functools.partial(couple_kernel, groups, lanes, mono_dev, units),
            out_shape=[store] * fill + [coded if is_coded else plain for _, is_coded in units],
            in_specs=[IN_SMEM] + [IN_VMEM] * (1 + len(pieces)),
            out_specs=[IN_VMEM] * (fill + len(units)),
            compiler_params=pltpu.CompilerParams(
                vmem_limit_bytes=2 * (piece_bytes + esp_block.size * 2) + 8 * 2**20
            ),
            name=name,
        )(names, blocks, *pieces)

    filled, beyond = couple([(top, True)], "couple_first", pieces, fill=True)
    beyond = {top: along_z(beyond, top)}
    for _ in range(5):
        beyond[top] = gate(beyond[top])
    rest = [k for k in range(1, lanes) if k != top]
    units = couple([(k, True) for k in rest], "couple_rest", [filled])
    for k, unit in zip(rest, units):
        beyond[k] = along_z(unit, k)
    (own,) = couple([(0, False)], "couple_own", [filled])
    own = pl.pallas_call(
        add_kernel,
        out_shape=plain,
        in_specs=[IN_VMEM] * 2,
        out_specs=IN_VMEM,
        compiler_params=small,
        name="add",
    )(own, beyond[top])
    return pl.pallas_call(
        finish_kernel,
        out_shape=jax.ShapeDtypeStruct((mono_dev, basis, basis), jnp.float32),
        in_specs=[IN_VMEM] * (2 + len(rest)),
        out_specs=hbm,
        scratch_shapes=[
            pltpu.VMEM((mono_dev, basis, basis), jnp.float32),
            pltpu.SemaphoreType.DMA((mono_dev,)),
        ],
        compiler_params=small,
        name="finish",
    )(h_core, own, *[beyond[k] for k in rest])


def solution(mesh):
    return jax.shard_map(
        local,
        mesh=mesh,
        in_specs=(
            P(("job", "gddi", "intra"), None, None),
            P(("job", "gddi", "intra"), None, None),
            P(("job", "gddi"), "intra", None, None),
            P("job", None),
        ),
        out_specs=P(("job", "gddi", "intra"), None, None),
        check_vma=False,
    )
```

```python
import functools

import jax
import jax.numpy as jnp
from jax import lax
from jax.experimental import pallas as pl
from jax.experimental.pallas import tpu as pltpu
from jax.sharding import PartitionSpec as P

STEPS = 32.0
TOP = 32000.0
SHRINK = 1.0 / 16.0
IN_VMEM = pl.BlockSpec(memory_space=pltpu.VMEM)
IN_SMEM = pl.BlockSpec(memory_space=pltpu.SMEM)


def xor_pairs(size, k):
    return [(i, i ^ k) for i in range(size)]


def round_up(n, to):
    return -(-n // to) * to


def transposed_dot(a, b):
    return lax.dot_general(a, b, (((1,), (1,)), ((), ())), preferred_element_type=jnp.float32)


def square_iotas(half):
    row = lax.broadcasted_iota(jnp.int32, (half, half), 0)
    col = lax.broadcasted_iota(jnp.int32, (half, half), 1)
    return row, col


def fold(first, second):
    row, col = square_iotas(first.shape[0])
    mixed = jnp.where(row <= col, first, second)
    diag = jnp.sum(jnp.where(row == col, second, 0.0), axis=0, keepdims=True)
    return mixed, diag


def unfold(mixed, diag):
    row, col = square_iotas(mixed.shape[0])
    turned = mixed.T
    first = jnp.where(row <= col, mixed, turned)
    second = jnp.where(row > col, mixed, jnp.where(row < col, turned, diag))
    return first, second


def scale_code(peak):
    wanted = jnp.log(jnp.maximum(peak * SHRINK, 2.0**-120)) * STEPS
    return jnp.floor(wanted + 1.5).astype(jnp.int32)


def encode(x, code):
    inverse = jnp.exp(code.astype(jnp.float32) * (-1.0 / STEPS))
    return jnp.floor(x * SHRINK * inverse * TOP + 0.5).astype(jnp.int32)


def decode(q, code):
    scale = jnp.exp(code.astype(jnp.float32) * (1.0 / STEPS))
    return q.astype(jnp.float32) * (1.0 / TOP) * scale * (1.0 / SHRINK)


def pack(high, low):
    return lax.shift_left(high, 16) | (low & 0xFFFF)


def unpack(word):
    return lax.shift_right_arithmetic(word, 16), lax.shift_right_arithmetic(lax.shift_left(word, 16), 16)


def peak_of(x):
    return jnp.max(jnp.abs(x), axis=0, keepdims=True)


def fold_kernel(dens_ref, out_ref):
    mono_dev, basis, _ = dens_ref.shape
    half = basis // 2
    diags = []
    for m in range(mono_dev):
        out_ref[pl.ds(m * basis, half)] = dens_ref[m, :half, half:]
        mixed, diag = fold(
            dens_ref[m, :half, :half].astype(jnp.float32), dens_ref[m, half:, half:].astype(jnp.float32)
        )
        out_ref[pl.ds(m * basis + half, half)] = mixed.astype(out_ref.dtype)
        diags.append(diag)
    rows = out_ref.shape[0] - mono_dev * basis
    row = lax.broadcasted_iota(jnp.int32, (rows, half), 0)
    tail = jnp.zeros((rows, half), jnp.float32)
    for m in range(mono_dev):
        tail = jnp.where(row == m, diags[m], tail)
    out_ref[pl.ds(mono_dev * basis, rows)] = tail.astype(out_ref.dtype)


def gate_kernel(piece_ref, *refs):
    refs[-1][...] = piece_ref[...]


def pair_kernel(one_ref, two_ref, out_ref):
    out_ref[pl.ds(0, one_ref.shape[0])] = one_ref[...]
    out_ref[pl.ds(one_ref.shape[0], two_ref.shape[0])] = two_ref[...]


def stage_kernel(nbr_ref, esp_ref, piece_ref, *refs):
    nbr_out, esp_out, piece_out, sems = refs[-4:]
    copies = [
        pltpu.make_async_copy(esp_ref, esp_out, sems.at[0]),
        pltpu.make_async_copy(nbr_ref, nbr_out, sems.at[1]),
    ]
    for copy in copies:
        copy.start()
    piece_out[...] = piece_ref[...]
    for copy in copies:
        copy.wait()


def couple_kernel(groups, lanes, mono_dev, units, places, nbr_ref, esp_ref, *refs):
    outs = refs[len(refs) - len(units) :]
    if len(refs) > len(units) + 1:
        pieces, store = refs[: -1 - len(units)], refs[-1 - len(units)]
        at, rows = 0, store.shape[1]
        for piece in pieces:
            for part in range(piece.shape[0] // rows):
                store[places[at]] = piece[pl.ds(part * rows, rows)]
                at += 1
    else:
        store = refs[0]
    my_group = lax.axis_index("gddi")
    my_lane = lax.axis_index("intra")
    _, slot_dev, basis, _ = esp_ref.shape
    mono_grp = mono_dev * lanes
    half = basis // 2
    tail_rows = store.shape[1] - mono_dev * basis

    def near_density(fragment):
        apart = (fragment // mono_grp) ^ my_group
        lane = ((fragment % mono_grp) // mono_dev) ^ my_lane
        place = ((apart & 1) * (groups // 2) + (apart >> 1)) * lanes + lane
        member = fragment % mono_dev
        start = pl.multiple_of(member * basis, basis)
        off = store[place, pl.ds(start, half)]
        mixed = store[place, pl.ds(start + half, half)].astype(jnp.float32)
        tail = store[place, pl.ds(mono_dev * basis, tail_rows)].astype(jnp.float32)
        row = lax.broadcasted_iota(jnp.int32, (tail_rows, half), 0)
        diag = jnp.sum(jnp.where(row == member, tail, 0.0), axis=0, keepdims=True)
        first, second = unfold(mixed, diag)
        top = jnp.concatenate([first.astype(off.dtype), off], axis=1)
        bottom = jnp.concatenate([off.T, second.astype(off.dtype)], axis=1)
        return jnp.concatenate([top, bottom], axis=0)

    def partial_of(fragment):
        high, low, blocks = [], [], []
        for s in range(slot_dev):
            name = nbr_ref[my_lane * slot_dev + s, my_group * mono_grp + fragment]
            block = esp_ref[fragment, s]
            half_term = jnp.dot(block, near_density(name), preferred_element_type=jnp.float32)
            high.append(half_term.astype(jnp.bfloat16))
            low.append((half_term - high[-1].astype(jnp.float32)).astype(jnp.bfloat16))
            blocks.append(block)
        both = jnp.concatenate([jnp.concatenate(high, axis=1), jnp.concatenate(low, axis=1)], axis=0)
        both = transposed_dot(both, jnp.concatenate(blocks, axis=1))
        total = both[:basis] + both[basis:]
        mixed, diag = fold(total[:half, :half], total[half:, half:])
        return total[:half, half:], mixed, diag

    for (k, coded), out in zip(units, outs):
        write = write_coded if coded else write_plain
        write(out, [partial_of((my_lane ^ k) * mono_dev + m) for m in range(mono_dev)])


def write_plain(out, parts):
    half = out.shape[2]
    for m, (off, mixed, diag) in enumerate(parts):
        out[m, :half] = off
        out[m, half : 2 * half] = mixed
        out[m, 2 * half :] = jnp.broadcast_to(diag, (8, half))


def read_plain(ref, m):
    half = ref.shape[2]
    return ref[m, :half], ref[m, half : 2 * half], ref[m, 2 * half : 2 * half + 1]


def write_coded(out, parts):
    half = out.shape[1]
    tail = []
    for m, (off, mixed, diag) in enumerate(parts):
        off_code = scale_code(peak_of(off))
        mixed_code = scale_code(jnp.maximum(peak_of(mixed), jnp.abs(diag)))
        out[pl.ds(m * half, half)] = pack(encode(off, off_code), encode(mixed, mixed_code))
        tail += [pack(off_code, mixed_code), encode(diag, mixed_code)]
    row = lax.broadcasted_iota(jnp.int32, (out.shape[0] - len(parts) * half, half), 0)
    last = jnp.zeros(row.shape, jnp.int32)
    for i, values in enumerate(tail):
        last = jnp.where(row == i, values, last)
    out[pl.ds(len(parts) * half, row.shape[0])] = last


def read_coded(ref, m, mono_dev):
    half = ref.shape[1]
    tail = mono_dev * half + 2 * m
    off_code, mixed_code = unpack(ref[tail : tail + 1])
    off_q, mixed_q = unpack(ref[m * half : (m + 1) * half])
    return decode(off_q, off_code), decode(mixed_q, mixed_code), decode(ref[tail + 1 : tail + 2], mixed_code)


def summed(plain_ref, coded_refs, m):
    total = read_plain(plain_ref, m)
    for ref in coded_refs:
        total = [a + b for a, b in zip(total, read_coded(ref, m, plain_ref.shape[0]))]
    return total


def add_kernel(plain_ref, *refs):
    write_plain(refs[-1], [summed(plain_ref, refs[:-1], m) for m in range(plain_ref.shape[0])])


def finish_kernel(core_ref, own_ref, *refs):
    parts, (out_ref, ready, sems) = refs[:-3], refs[-3:]
    mono_dev, basis, _ = ready.shape
    half = basis // 2
    copies = []
    for m in range(mono_dev):
        off, mixed, diag = summed(own_ref, parts, m)
        first, second = unfold(mixed, diag)
        core = core_ref[m].astype(jnp.float32)
        ready[m, :half, :half] = core[:half, :half] + first
        ready[m, :half, half:] = core[:half, half:] + off
        ready[m, half:, :half] = core[half:, :half] + off.T
        ready[m, half:, half:] = core[half:, half:] + second
        copies.append(pltpu.make_async_copy(ready.at[m], out_ref.at[m], sems.at[m]))
        copies[-1].start()
    for copy in copies:
        copy.wait()


def local(density, h_core, esp_block, nbr):
    groups = lax.axis_size("gddi")
    lanes = lax.axis_size("intra")
    mono_dev, basis = density.shape[0], density.shape[1]
    half = basis // 2
    hbm = pl.BlockSpec(memory_space=pl.ANY)
    small = pltpu.CompilerParams(vmem_limit_bytes=8 * 2**20)

    rows = mono_dev * basis + round_up(mono_dev, 16)
    shard = pl.pallas_call(
        fold_kernel,
        out_shape=pltpu.VMEM((rows, half), density.dtype),
        in_specs=[IN_VMEM],
        out_specs=IN_VMEM,
        compiler_params=small,
        name="fold",
    )(pltpu.with_memory_space_constraint(density, pltpu.HBM))
    def along_z(piece, bit):
        return lax.ppermute(piece, "intra", xor_pairs(lanes, bit))

    def along_y(piece, y):
        return lax.ppermute(piece, "gddi", xor_pairs(groups, 2 * y))

    rows_y = groups // 2
    top = lanes // 2
    near = {(0, 0): shard, (0, top): along_z(shard, top)}

    def double(start):
        bit = top // 2
        while bit:
            for k in range(start, start + top):
                if (0, k) in near and (0, k ^ bit) not in near:
                    near[0, k ^ bit] = along_z(near[0, k], bit)
            bit //= 2

    double(0)
    for y in range(1, rows_y):
        near[y, 0] = along_y(shard, y)

    def gate(piece, *after):
        return pl.pallas_call(
            gate_kernel,
            out_shape=pltpu.VMEM(piece.shape, piece.dtype),
            in_specs=[IN_VMEM] + [hbm] * len(after),
            out_specs=IN_VMEM,
            compiler_params=small,
            name="gate",
        )(piece, *after)

    others = [piece for key, piece in near.items() if key != (0, top)]
    near[0, top] = gate(gate(near[0, top]), *others)
    double(top)
    for y in range(1, rows_y):
        for k in range(1, top):
            near[y, k] = along_z(near[y, k & (k - 1)], k & -k)
        for k in range(top, lanes):
            near[y, k] = along_y(near[0, k], y)

    names, blocks, near[rows_y - 1, 0] = pl.pallas_call(
        stage_kernel,
        out_shape=[
            pltpu.SMEM((nbr.shape[1], nbr.shape[0]), nbr.dtype),
            pltpu.VMEM(esp_block.shape, esp_block.dtype),
            pltpu.VMEM(shard.shape, shard.dtype),
        ],
        in_specs=[hbm, hbm, IN_VMEM, hbm],
        out_specs=[IN_SMEM, IN_VMEM, IN_VMEM],
        scratch_shapes=[pltpu.SemaphoreType.DMA((2,))],
        compiler_params=small,
        name="stage",
    )(
        pltpu.with_memory_space_constraint(nbr.T, pltpu.HBM),
        pltpu.with_memory_space_constraint(esp_block, pltpu.HBM),
        near[rows_y - 1, 0],
        near[0, lanes - 1],
    )
    keys = [(y, k) for y in range(rows_y) for k in range(lanes)]
    mine = [near[key] for key in keys]
    pair = [1, top] if top > 1 else [0, top]
    both = pl.pallas_call(
        pair_kernel,
        out_shape=pltpu.VMEM((2 * rows, half), density.dtype),
        in_specs=[IN_VMEM] * 2,
        out_specs=IN_VMEM,
        compiler_params=small,
        name="pair",
    )(*[mine[i] for i in pair])
    both = lax.ppermute(both, "gddi", xor_pairs(groups, 1))
    single = [i for i in range(len(mine)) if i not in pair]
    pieces = mine + [both] + [lax.ppermute(mine[i], "gddi", xor_pairs(groups, 1)) for i in single]
    places = list(range(len(mine))) + [len(mine) + i for i in pair + single]

    plain = pltpu.VMEM((mono_dev, basis + 8, half), jnp.float32)
    coded = pltpu.VMEM((mono_dev * half + round_up(2 * mono_dev, 8), half), jnp.int32)
    piece_bytes = groups * lanes * rows * half * 2

    keep = pltpu.VMEM if piece_bytes <= 4 * 2**20 else jax.ShapeDtypeStruct
    store = keep((groups * lanes, rows, half), density.dtype)

    def couple(units, name, pieces, fill=False):
        return pl.pallas_call(
            functools.partial(couple_kernel, groups, lanes, mono_dev, units, places),
            out_shape=[store] * fill + [coded if is_coded else plain for _, is_coded in units],
            in_specs=[IN_SMEM] + [IN_VMEM] * (1 + len(pieces)),
            out_specs=[IN_VMEM] * (fill + len(units)),
            compiler_params=pltpu.CompilerParams(
                vmem_limit_bytes=2 * (piece_bytes + esp_block.size * 2) + 8 * 2**20
            ),
            name=name,
        )(names, blocks, *pieces)

    filled, beyond = couple([(top, True)], "couple_first", pieces, fill=True)
    beyond = {top: along_z(beyond, top)}
    for _ in range(5):
        beyond[top] = gate(beyond[top])
    rest = [k for k in range(1, lanes) if k != top]
    units = couple([(k, True) for k in rest], "couple_rest", [filled])
    for k, unit in zip(rest, units):
        beyond[k] = along_z(unit, k)
    (own,) = couple([(0, False)], "couple_own", [filled])
    own = pl.pallas_call(
        add_kernel,
        out_shape=plain,
        in_specs=[IN_VMEM] * 2,
        out_specs=IN_VMEM,
        compiler_params=small,
        name="add",
    )(own, beyond[top])
    return pl.pallas_call(
        finish_kernel,
        out_shape=jax.ShapeDtypeStruct((mono_dev, basis, basis), jnp.float32),
        in_specs=[IN_VMEM] * (2 + len(rest)),
        out_specs=hbm,
        scratch_shapes=[
            pltpu.VMEM((mono_dev, basis, basis), jnp.float32),
            pltpu.SemaphoreType.DMA((mono_dev,)),
        ],
        compiler_params=small,
        name="finish",
    )(h_core, own, *[beyond[k] for k in rest])


def solution(mesh):
    return jax.shard_map(
        local,
        mesh=mesh,
        in_specs=(
            P(("job", "gddi", "intra"), None, None),
            P(("job", "gddi", "intra"), None, None),
            P(("job", "gddi"), "intra", None, None),
            P("job", None),
        ),
        out_specs=P(("job", "gddi", "intra"), None, None),
        check_vma=False,
    )
```

```python
import functools

import jax
import jax.numpy as jnp
from jax import lax
from jax.experimental import pallas as pl
from jax.experimental.pallas import tpu as pltpu
from jax.sharding import PartitionSpec as P

STEPS = 32.0
TOP = 32000.0
SHRINK = 1.0 / 16.0
IN_VMEM = pl.BlockSpec(memory_space=pltpu.VMEM)
IN_SMEM = pl.BlockSpec(memory_space=pltpu.SMEM)


def xor_pairs(size, k):
    return [(i, i ^ k) for i in range(size)]


def round_up(n, to):
    return -(-n // to) * to


def transposed_dot(a, b):
    return lax.dot_general(a, b, (((1,), (1,)), ((), ())), preferred_element_type=jnp.float32)


def square_iotas(half):
    row = lax.broadcasted_iota(jnp.int32, (half, half), 0)
    col = lax.broadcasted_iota(jnp.int32, (half, half), 1)
    return row, col


def fold(first, second):
    row, col = square_iotas(first.shape[0])
    mixed = jnp.where(row <= col, first, second)
    diag = jnp.sum(jnp.where(row == col, second, 0.0), axis=0, keepdims=True)
    return mixed, diag


def unfold(mixed, diag):
    row, col = square_iotas(mixed.shape[0])
    turned = mixed.T
    first = jnp.where(row <= col, mixed, turned)
    second = jnp.where(row > col, mixed, jnp.where(row < col, turned, diag))
    return first, second


def scale_code(peak):
    wanted = jnp.log(jnp.maximum(peak * SHRINK, 2.0**-120)) * STEPS
    return jnp.floor(wanted + 1.5).astype(jnp.int32)


def encode(x, code):
    inverse = jnp.exp(code.astype(jnp.float32) * (-1.0 / STEPS))
    return jnp.floor(x * SHRINK * inverse * TOP + 0.5).astype(jnp.int32)


def decode(q, code):
    scale = jnp.exp(code.astype(jnp.float32) * (1.0 / STEPS))
    return q.astype(jnp.float32) * (1.0 / TOP) * scale * (1.0 / SHRINK)


def pack(high, low):
    return lax.shift_left(high, 16) | (low & 0xFFFF)


def unpack(word):
    return lax.shift_right_arithmetic(word, 16), lax.shift_right_arithmetic(lax.shift_left(word, 16), 16)


def peak_of(x):
    return jnp.max(jnp.abs(x), axis=0, keepdims=True)


def fold_kernel(dens_ref, out_ref):
    mono_dev, basis, _ = dens_ref.shape
    half = basis // 2
    diags = []
    for m in range(mono_dev):
        out_ref[pl.ds(m * basis, half)] = dens_ref[m, :half, half:]
        mixed, diag = fold(
            dens_ref[m, :half, :half].astype(jnp.float32), dens_ref[m, half:, half:].astype(jnp.float32)
        )
        out_ref[pl.ds(m * basis + half, half)] = mixed.astype(out_ref.dtype)
        diags.append(diag)
    rows = out_ref.shape[0] - mono_dev * basis
    row = lax.broadcasted_iota(jnp.int32, (rows, half), 0)
    tail = jnp.zeros((rows, half), jnp.float32)
    for m in range(mono_dev):
        tail = jnp.where(row == m, diags[m], tail)
    out_ref[pl.ds(mono_dev * basis, rows)] = tail.astype(out_ref.dtype)


def gate_kernel(piece_ref, *refs):
    refs[-1][...] = piece_ref[...]


def stage_kernel(nbr_ref, esp_ref, piece_ref, *refs):
    nbr_out, esp_out, piece_out, sems = refs[-4:]
    copies = [
        pltpu.make_async_copy(esp_ref, esp_out, sems.at[0]),
        pltpu.make_async_copy(nbr_ref, nbr_out, sems.at[1]),
    ]
    for copy in copies:
        copy.start()
    piece_out[...] = piece_ref[...]
    for copy in copies:
        copy.wait()


def couple_kernel(groups, lanes, mono_dev, units, nbr_ref, esp_ref, *refs):
    outs = refs[len(refs) - len(units) :]
    if len(refs) > len(units) + 1:
        pieces, store = refs[: -1 - len(units)], refs[-1 - len(units)]
        for i, piece in enumerate(pieces):
            store[i] = piece[...]
    else:
        store = refs[0]
    my_group = lax.axis_index("gddi")
    my_lane = lax.axis_index("intra")
    _, slot_dev, basis, _ = esp_ref.shape
    mono_grp = mono_dev * lanes
    half = basis // 2
    tail_rows = store.shape[1] - mono_dev * basis

    def near_density(fragment):
        apart = (fragment // mono_grp) ^ my_group
        lane = ((fragment % mono_grp) // mono_dev) ^ my_lane
        place = ((apart & 1) * (groups // 2) + (apart >> 1)) * lanes + lane
        member = fragment % mono_dev
        start = pl.multiple_of(member * basis, basis)
        off = store[place, pl.ds(start, half)]
        mixed = store[place, pl.ds(start + half, half)].astype(jnp.float32)
        tail = store[place, pl.ds(mono_dev * basis, tail_rows)].astype(jnp.float32)
        row = lax.broadcasted_iota(jnp.int32, (tail_rows, half), 0)
        diag = jnp.sum(jnp.where(row == member, tail, 0.0), axis=0, keepdims=True)
        first, second = unfold(mixed, diag)
        top = jnp.concatenate([first.astype(off.dtype), off], axis=1)
        bottom = jnp.concatenate([off.T, second.astype(off.dtype)], axis=1)
        return jnp.concatenate([top, bottom], axis=0)

    def partial_of(fragment):
        high, low, blocks = [], [], []
        for s in range(slot_dev):
            name = nbr_ref[my_lane * slot_dev + s, my_group * mono_grp + fragment]
            block = esp_ref[fragment, s]
            half_term = jnp.dot(block, near_density(name), preferred_element_type=jnp.float32)
            high.append(half_term.astype(jnp.bfloat16))
            low.append((half_term - high[-1].astype(jnp.float32)).astype(jnp.bfloat16))
            blocks.append(block)
        both = jnp.concatenate([jnp.concatenate(high, axis=1), jnp.concatenate(low, axis=1)], axis=0)
        both = transposed_dot(both, jnp.concatenate(blocks, axis=1))
        total = both[:basis] + both[basis:]
        mixed, diag = fold(total[:half, :half], total[half:, half:])
        return total[:half, half:], mixed, diag

    for (k, coded), out in zip(units, outs):
        write = write_coded if coded else write_plain
        write(out, [partial_of((my_lane ^ k) * mono_dev + m) for m in range(mono_dev)])


def write_plain(out, parts):
    half = out.shape[2]
    for m, (off, mixed, diag) in enumerate(parts):
        out[m, :half] = off
        out[m, half : 2 * half] = mixed
        out[m, 2 * half :] = jnp.broadcast_to(diag, (8, half))


def read_plain(ref, m):
    half = ref.shape[2]
    return ref[m, :half], ref[m, half : 2 * half], ref[m, 2 * half : 2 * half + 1]


def write_coded(out, parts):
    half = out.shape[1]
    tail = []
    for m, (off, mixed, diag) in enumerate(parts):
        off_code = scale_code(peak_of(off))
        mixed_code = scale_code(jnp.maximum(peak_of(mixed), jnp.abs(diag)))
        out[pl.ds(m * half, half)] = pack(encode(off, off_code), encode(mixed, mixed_code))
        tail += [pack(off_code, mixed_code), encode(diag, mixed_code)]
    row = lax.broadcasted_iota(jnp.int32, (out.shape[0] - len(parts) * half, half), 0)
    last = jnp.zeros(row.shape, jnp.int32)
    for i, values in enumerate(tail):
        last = jnp.where(row == i, values, last)
    out[pl.ds(len(parts) * half, row.shape[0])] = last


def read_coded(ref, m, mono_dev):
    half = ref.shape[1]
    tail = mono_dev * half + 2 * m
    off_code, mixed_code = unpack(ref[tail : tail + 1])
    off_q, mixed_q = unpack(ref[m * half : (m + 1) * half])
    return decode(off_q, off_code), decode(mixed_q, mixed_code), decode(ref[tail + 1 : tail + 2], mixed_code)


def summed(plain_ref, coded_refs, m):
    total = read_plain(plain_ref, m)
    for ref in coded_refs:
        total = [a + b for a, b in zip(total, read_coded(ref, m, plain_ref.shape[0]))]
    return total


def add_kernel(plain_ref, *refs):
    write_plain(refs[-1], [summed(plain_ref, refs[:-1], m) for m in range(plain_ref.shape[0])])


def finish_kernel(core_ref, own_ref, *refs):
    parts, (out_ref, ready, sems) = refs[:-3], refs[-3:]
    mono_dev, basis, _ = ready.shape
    half = basis // 2
    copies = []
    for m in range(mono_dev):
        off, mixed, diag = summed(own_ref, parts, m)
        first, second = unfold(mixed, diag)
        core = core_ref[m].astype(jnp.float32)
        ready[m, :half, :half] = core[:half, :half] + first
        ready[m, :half, half:] = core[:half, half:] + off
        ready[m, half:, :half] = core[half:, :half] + off.T
        ready[m, half:, half:] = core[half:, half:] + second
        copies.append(pltpu.make_async_copy(ready.at[m], out_ref.at[m], sems.at[m]))
        copies[-1].start()
    for copy in copies:
        copy.wait()


def local(density, h_core, esp_block, nbr):
    groups = lax.axis_size("gddi")
    lanes = lax.axis_size("intra")
    mono_dev, basis = density.shape[0], density.shape[1]
    half = basis // 2
    hbm = pl.BlockSpec(memory_space=pl.ANY)
    small = pltpu.CompilerParams(vmem_limit_bytes=8 * 2**20)

    rows = mono_dev * basis + round_up(mono_dev, 16)
    shard = pl.pallas_call(
        fold_kernel,
        out_shape=pltpu.VMEM((rows, half), density.dtype),
        in_specs=[IN_VMEM],
        out_specs=IN_VMEM,
        compiler_params=small,
        name="fold",
    )(pltpu.with_memory_space_constraint(density, pltpu.HBM))
    def along_z(piece, bit):
        return lax.ppermute(piece, "intra", xor_pairs(lanes, bit))

    def along_y(piece, y):
        return lax.ppermute(piece, "gddi", xor_pairs(groups, 2 * y))

    rows_y = groups // 2
    top = lanes // 2
    near = {(0, 0): shard, (0, top): along_z(shard, top)}

    def double(start):
        bit = top // 2
        while bit:
            for k in range(start, start + top):
                if (0, k) in near and (0, k ^ bit) not in near:
                    near[0, k ^ bit] = along_z(near[0, k], bit)
            bit //= 2

    double(0)
    for y in range(1, rows_y):
        near[y, 0] = along_y(shard, y)

    def gate(piece, *after):
        return pl.pallas_call(
            gate_kernel,
            out_shape=pltpu.VMEM(piece.shape, piece.dtype),
            in_specs=[IN_VMEM] + [hbm] * len(after),
            out_specs=IN_VMEM,
            compiler_params=small,
            name="gate",
        )(piece, *after)

    others = [piece for key, piece in near.items() if key != (0, top)]
    near[0, top] = gate(gate(near[0, top]), *others)
    double(top)
    for y in range(1, rows_y):
        for k in range(1, top):
            near[y, k] = along_z(near[y, k & (k - 1)], k & -k)
        for k in range(top, lanes):
            near[y, k] = along_y(near[0, k], y)

    names, blocks, near[rows_y - 1, 0] = pl.pallas_call(
        stage_kernel,
        out_shape=[
            pltpu.SMEM((nbr.shape[1], nbr.shape[0]), nbr.dtype),
            pltpu.VMEM(esp_block.shape, esp_block.dtype),
            pltpu.VMEM(shard.shape, shard.dtype),
        ],
        in_specs=[hbm, hbm, IN_VMEM, hbm],
        out_specs=[IN_SMEM, IN_VMEM, IN_VMEM],
        scratch_shapes=[pltpu.SemaphoreType.DMA((2,))],
        compiler_params=small,
        name="stage",
    )(
        pltpu.with_memory_space_constraint(nbr.T, pltpu.HBM),
        pltpu.with_memory_space_constraint(esp_block, pltpu.HBM),
        near[rows_y - 1, 0],
        near[0, lanes - 1],
    )
    keys = [(y, k) for y in range(rows_y) for k in range(lanes)]
    mine = [near[key] for key in keys]
    pieces = mine + [lax.ppermute(piece, "gddi", xor_pairs(groups, 1)) for piece in mine]

    plain = pltpu.VMEM((mono_dev, basis + 8, half), jnp.float32)
    coded = pltpu.VMEM((mono_dev * half + round_up(2 * mono_dev, 8), half), jnp.int32)
    piece_bytes = groups * lanes * rows * half * 2

    keep = pltpu.VMEM if piece_bytes <= 4 * 2**20 else jax.ShapeDtypeStruct
    store = keep((groups * lanes, rows, half), density.dtype)

    def couple(units, name, pieces, fill=False):
        return pl.pallas_call(
            functools.partial(couple_kernel, groups, lanes, mono_dev, units),
            out_shape=[store] * fill + [coded if is_coded else plain for _, is_coded in units],
            in_specs=[IN_SMEM] + [IN_VMEM] * (1 + len(pieces)),
            out_specs=[IN_VMEM] * (fill + len(units)),
            compiler_params=pltpu.CompilerParams(
                vmem_limit_bytes=2 * (piece_bytes + esp_block.size * 2) + 8 * 2**20
            ),
            name=name,
        )(names, blocks, *pieces)

    filled, beyond = couple([(top, True)], "couple_first", pieces, fill=True)
    beyond = {top: along_z(beyond, top)}
    for _ in range(5):
        beyond[top] = gate(beyond[top])
    rest = [k for k in range(1, lanes) if k != top]
    units = couple([(k, True) for k in rest], "couple_rest", [filled])
    for k, unit in zip(rest, units):
        beyond[k] = along_z(unit, k)
    (own,) = couple([(0, False)], "couple_own", [filled])
    for k in [top] + [k for k in rest if k < top]:
        own = pl.pallas_call(
            add_kernel,
            out_shape=plain,
            in_specs=[IN_VMEM] * 2,
            out_specs=IN_VMEM,
            compiler_params=small,
            name="add",
        )(own, beyond[k])
    rest = [k for k in rest if k > top]
    return pl.pallas_call(
        finish_kernel,
        out_shape=jax.ShapeDtypeStruct((mono_dev, basis, basis), jnp.float32),
        in_specs=[IN_VMEM] * (2 + len(rest)),
        out_specs=hbm,
        scratch_shapes=[
            pltpu.VMEM((mono_dev, basis, basis), jnp.float32),
            pltpu.SemaphoreType.DMA((mono_dev,)),
        ],
        compiler_params=small,
        name="finish",
    )(h_core, own, *[beyond[k] for k in rest])


def solution(mesh):
    return jax.shard_map(
        local,
        mesh=mesh,
        in_specs=(
            P(("job", "gddi", "intra"), None, None),
            P(("job", "gddi", "intra"), None, None),
            P(("job", "gddi"), "intra", None, None),
            P("job", None),
        ),
        out_specs=P(("job", "gddi", "intra"), None, None),
        check_vma=False,
    )
```
